128 devices in a mesh: seq: 32 (over z, y, core), mp: 4 (over x).
Axes of the slice: x: 4, y: 4, z: 4, core: 2. Of those that a mesh axis runs over, the one named last changes fastest.
Arguments:
- tokens: bfloat16 [4096, 2048], P('seq'), may hold values from -6 to 6
- cotangent: bfloat16 [4096, 2048], P('seq'), may hold values from -6 to 6
- resets: int32 [4096], P('seq'), may hold values from 0 to 1, as said below
- norm1_gain: bfloat16 [2048], P('seq'), may hold values from 0.5 to 1.5
- in_weight: bfloat16 [2048, 3, 2048], P('seq', None, 'mp'), may hold values from -0.125 to 0.125
- conv_weight: float32 [3, 3, 2048], P(None, None, 'mp'), may hold values from -3 to 3
- pole_decay: float32 [16, 2048], P(None, 'mp'), may hold values from 7.3242187e-06 to 0.04
- pole_angle: float32 [16, 2048], P(None, 'mp'), may hold values from -3.140625 to 3.140625
- residue_re: float32 [16, 2048], P(None, 'mp'), may hold values from -2 to 2
- residue_im: float32 [16, 2048], P(None, 'mp'), may hold values from -2 to 2
- out_weight: bfloat16 [2048, 2048], P('seq', 'mp'), may hold values from -0.125 to 0.125
- norm2_gain: bfloat16 [2048], P('seq'), may hold values from 0.5 to 1.5
- gate_weight: bfloat16 [2048, 5632], P('seq', 'mp'), may hold values from -0.125 to 0.125
- up_weight: bfloat16 [2048, 5632], P('seq', 'mp'), may hold values from -0.125 to 0.125
- down_weight: bfloat16 [2048, 5632], P('seq', 'mp'), may hold values from -0.078125 to 0.078125
Outputs:
- block_out: bfloat16 [4096, 2048], P('seq')
- grad_tokens: bfloat16 [4096, 2048], P('seq')
- grad_norm1_gain: float32 [2048], P('seq')
- grad_in_weight: float32 [2048, 3, 2048], P('seq', None, 'mp')
- grad_conv_weight: float32 [3, 3, 2048], P(None, None, 'mp')
- grad_pole_decay: float32 [16, 2048], P(None, 'mp')
- grad_pole_angle: float32 [16, 2048], P(None, 'mp')
- grad_residue_re: float32 [16, 2048], P(None, 'mp')
- grad_residue_im: float32 [16, 2048], P(None, 'mp')
- grad_out_weight: float32 [2048, 2048], P('seq', 'mp')
- grad_norm2_gain: float32 [2048], P('seq')
- grad_gate_weight: float32 [2048, 5632], P('seq', 'mp')
- grad_up_weight: float32 [2048, 5632], P('seq', 'mp')
- grad_down_weight: float32 [2048, 5632], P('seq', 'mp')
The draws below stay inside these ranges and needn't reach their ends.
Inputs may be any that keep to these rules, and one draw needn't show every extreme that they name: resets[0] is 1. One document begins among the first 64 tokens and its successor begins among the last 64 tokens, with no reset in between; further resets fall only before or after that document.
All inputs are finite; a program needn't handle non-finite values.
Results may differ from the reference program's by a relative error of at most 0.025.
Values may be sent and summed in bfloat16 or wider, within the bound.
A program may use at most 192 MiB of HBM per device.

```python
import jax
import jax.numpy as jnp
from jax import lax

D = 2048
FF = 5632
POLES = 16
TOK_DEV = 128
TOKENS = 4096


def draw_resets(key, part):
    key = jax.random.fold_in(key, 7)
    first_key, last_key, extra_key = jax.random.split(key, 3)
    half = max(TOK_DEV // 2, 2)
    first = jax.random.randint(first_key, (), 1, half)
    last = jax.random.randint(last_key, (), TOKENS - half, TOKENS)
    places = jnp.arange(TOKENS)
    extra = jax.random.randint(extra_key, (TOKENS,), 0, 16) == 0
    outside = (places < first) | (places > last)
    flags = (places == 0) | (places == first) | (places == last) | extra & outside
    return flags.astype(jnp.int32)


def draw_pole_decay(key, part):
    key = jax.random.fold_in(key, 11)
    lowest = 0.03 / TOKENS
    highest = 0.04
    spread = jax.random.uniform(key, (POLES, D), jnp.float32)
    return lowest * jnp.exp(spread * jnp.log(highest / lowest))


def strengthened(array, key, source, target, blocks, factor):
    def block_of(axis_at):
        return (jnp.arange(array.shape[axis_at]) // (array.shape[axis_at] // blocks)).reshape((-1,) + (1,) * (array.ndim - 1 - axis_at))

    one_side = jax.random.permutation(key, blocks)[block_of(target)]
    second = (block_of(target) + blocks // 2) % blocks
    return jnp.where((block_of(source) == one_side) | (block_of(source) == second), factor * array, array)


def level_of(own_key, dims, shards, low, top_value):
    factor_of, own = 1.0, jax.random.fold_in(own_key, 6)
    for position, parts in shards:
        draws = jnp.exp(jax.random.uniform(jax.random.fold_in(own, position), (parts,), jnp.float32, low / len(shards), top_value / len(shards)))
        factor_of = factor_of * jnp.repeat(draws, dims[position] // parts).reshape([-1 if axis == position else 1 for axis in range(len(dims))])
    return factor_of


def gaussian(stream_key, extent, scale, bound, cuts=(), kind=jnp.bfloat16):
    values = jax.random.normal(stream_key, extent, jnp.float32) * scale
    if len(cuts) > 0:
        values = level_of(stream_key, extent, cuts, -0.22, 0.18) * values
    return jnp.clip(values, min=-bound, max=bound).astype(kind)


def bell_draw_with(stream_key, dims, width, bound, cuts, heavy, held_as=jnp.bfloat16):
    entries = width * jax.random.normal(stream_key, dims, jnp.float32)
    if cuts:
        entries = entries * level_of(stream_key, dims, cuts, -0.22, 0.18)
    return jnp.clip(strengthened(entries, jax.random.fold_in(stream_key, 3), *heavy), -bound, bound).astype(held_as)


def setup_inputs(seed: int = 0) -> dict:
    seeds = jax.random.split(jax.random.key(seed), 16)
    return {
        "tokens": gaussian(seeds[0], (TOKENS, D), 1.0, 6.0, ((0, 32),)),
        "cotangent": bell_draw_with(seeds[1], (TOKENS, D), 1.0, 6.0, ((0, 32),), (0, 1, 32, 2.75)),
        "resets": draw_resets(jax.random.fold_in(seeds[15], 71), 0),
        "norm1_gain": jnp.clip(1.0 + 0.1 * jax.random.normal(seeds[3], (D,), jnp.float32), 0.5, 1.5).astype(jnp.bfloat16),
        "in_weight": gaussian(seeds[4], (D, 3, D), D ** -0.5, 0.125, ((0, 32), (2, 4))),
        "conv_weight": gaussian(seeds[5], (3, 3, D), 0.6, 3.0, ((2, 4),), jnp.float32),
        "pole_decay": draw_pole_decay(jax.random.fold_in(seeds[15], 71), 0),
        "pole_angle": jnp.clip(jax.random.uniform(seeds[7], (POLES, D), jnp.float32, -3.140625, 3.140625), -3.140625, 3.140625),
        "residue_re": gaussian(seeds[8], (POLES, D), 0.35, 2.0, ((1, 4),), jnp.float32),
        "residue_im": gaussian(seeds[9], (POLES, D), 0.35, 2.0, ((1, 4),), jnp.float32),
        "out_weight": gaussian(seeds[10], (D, D), D ** -0.5, 0.125, ((0, 32), (1, 4))),
        "norm2_gain": jnp.clip(1.0 + 0.1 * jax.random.normal(seeds[11], (D,), jnp.float32), 0.5, 1.5).astype(jnp.bfloat16),
        "gate_weight": gaussian(seeds[12], (D, FF), D ** -0.5, 0.125, ((0, 32), (1, 4))),
        "up_weight": gaussian(seeds[13], (D, FF), D ** -0.5, 0.125, ((0, 32), (1, 4))),
        "down_weight": gaussian(seeds[14], (D, FF), FF ** -0.5, 0.078125, ((0, 32), (1, 4))),
    }


EPSILON = 1e-05
HIGH = lax.Precision.HIGHEST

@jax.custom_vjp
def low(v):
    return lax.optimization_barrier(v.astype(jnp.bfloat16)).astype(jnp.float32)

@jax.custom_vjp
def low_back(v):
    return v

def low_keep(v):
    return (low(v), None)

def low_pass(kept, grad):
    return (grad,)

def back_keep(v):
    return (v, None)

def back_low(kept, grad):
    return (low(grad),)
low.defvjp(low_keep, low_pass)
low_back.defvjp(back_keep, back_low)

def long_conv(signal, keep, decay, angle, res_real, res_imag):
    magnitude = jnp.exp(-decay)
    lam_real = magnitude * jnp.cos(angle)
    lam_imag = magnitude * jnp.sin(angle)
    gain_in = jnp.sqrt(-jnp.expm1(-2.0 * decay))

    def advance(state, pieces):
        value, kept = pieces
        old_real, old_imag = state
        new_real = kept * (lam_real * old_real - lam_imag * old_imag) + gain_in * value[None, :]
        new_imag = kept * (lam_real * old_imag + lam_imag * old_real)
        result = lax.optimization_barrier(jnp.sum(res_real * new_real - res_imag * new_imag, axis=0))
        return ((new_real, new_imag), result)

    def run_block(state, pieces):
        return lax.scan(advance, state, pieces)
    blocks = signal.shape[0] // 64
    zero = jnp.zeros(decay.shape, decay.dtype)
    _, outputs = lax.scan(jax.checkpoint(run_block), (zero, zero), (signal.reshape(blocks, 64, signal.shape[1]), keep.reshape(blocks, 64)))
    return outputs.reshape(signal.shape)

def reference(tokens, cotangent, resets, norm1_gain, in_weight, conv_weight, pole_decay, pole_angle, residue_re, residue_im, out_weight, norm2_gain, gate_weight, up_weight, down_weight):
    keep = 1.0 - resets.astype(jnp.float32)
    near = keep
    far = keep * jnp.concatenate([jnp.ones((1,), keep.dtype), keep[:-1]])

    def forward(stream, gain_one, weight_in, taps, decay, angle, res_real, res_imag, weight_out, gain_two, weight_gate, weight_up, weight_down):
        scale_one = lax.rsqrt(lax.optimization_barrier(jnp.mean(stream * stream, axis=-1, keepdims=True)) + EPSILON)
        normed_one = low(stream * scale_one * gain_one)
        projected = low(low_back(jnp.einsum('td,dbc->tbc', normed_one, weight_in, precision=HIGH)))
        padded = jnp.pad(projected, ((2, 0), (0, 0), (0, 0)))
        mixed = taps[0] * padded[2:] + near[:, None, None] * taps[1] * padded[1:-1] + far[:, None, None] * taps[2] * padded[:-2]
        signal = mixed[:, 1] * mixed[:, 2]
        long_out = long_conv(signal, keep, decay, angle, res_real, res_imag)
        gated = low(mixed[:, 0] * long_out)
        mixer = low_back(jnp.einsum('tc,dc->td', gated, weight_out, precision=HIGH))
        hidden_stream = stream + mixer
        scale_two = lax.rsqrt(lax.optimization_barrier(jnp.mean(hidden_stream * hidden_stream, axis=-1, keepdims=True)) + EPSILON)
        normed_two = low(hidden_stream * scale_two * gain_two)
        gate = low_back(jnp.dot(normed_two, weight_gate, precision=HIGH))
        upper = low_back(jnp.dot(normed_two, weight_up, precision=HIGH))
        activated = low(jax.nn.silu(gate) * upper)
        ffn = low_back(jnp.einsum('tf,df->td', activated, weight_down, precision=HIGH))
        return hidden_stream + ffn
    inputs = (tokens.astype(jnp.float32), norm1_gain.astype(jnp.float32), in_weight.astype(jnp.float32), conv_weight.astype(jnp.float32), pole_decay.astype(jnp.float32), pole_angle.astype(jnp.float32), residue_re.astype(jnp.float32), residue_im.astype(jnp.float32), out_weight.astype(jnp.float32), norm2_gain.astype(jnp.float32), gate_weight.astype(jnp.float32), up_weight.astype(jnp.float32), down_weight.astype(jnp.float32))
    result, pullback = jax.vjp(forward, *inputs)
    grads = pullback(cotangent.astype(jnp.float32))
    return (result.astype(jnp.bfloat16), grads[0].astype(jnp.bfloat16), grads[1], grads[2], grads[3], grads[4], grads[5], grads[6], grads[7], grads[8], grads[9], grads[10], grads[11], grads[12])
```

```python
import functools

import jax
import jax.numpy as jnp
from jax import lax
from jax.experimental import pallas as pl
from jax.experimental.pallas import tpu as pltpu
from jax.sharding import PartitionSpec as P

EPSILON = 1e-05
BF16, F32 = jnp.bfloat16, jnp.float32
MESH = pl.DeviceIdType.MESH
LANES_A, LANES_B = 1664, 1536
CHUNKS = (
    ((0, 384), (0, 384)),
    ((384, 128), (384, 128)),
    ((512, 768), (512, 640)),
    ((1280, 384), (1152, 384)),
)
IN, OUT, GU, DOWN = range(4)


def where():
    place = lax.axis_index("seq")
    chip = place // 2
    return chip // 4, lax.rem(chip, 4), lax.rem(place, 2), lax.axis_index("mp")


def device(z, y, c, x):
    return ((z * 4 + y) * 2 + c, x)


def rem4(a):
    return lax.rem(a + 4, 4)


def remote(src, dst, send, recv, to):
    return pltpu.make_async_remote_copy(
        src_ref=src, dst_ref=dst, send_sem=send, recv_sem=recv, device_id=to, device_id_type=MESH
    )


def nn(a, b):
    return jnp.dot(a, b, preferred_element_type=F32)


def nt(a, b):
    return lax.dot_general(a, b, (((1,), (1,)), ((), ())), preferred_element_type=F32)


def tn(a, b):
    return lax.dot_general(a, b, (((0,), (0,)), ((), ())), preferred_element_type=F32)


def loop(count, body):
    lax.fori_loop(0, count, lambda i, _: (body(i), 0)[1], 0)


def span(start, size):
    return pl.ds(pl.multiple_of(start, size), size)


class Rings:
    def __init__(self):
        self.z, self.y, self.c, self.x = where()
        self.chip = self.z * 4 + self.y
        self.sib = device(self.z, self.y, 1 - self.c, self.x)

    def near(self, axis, d):
        if axis == 0:
            return device(rem4(self.z + d), self.y, self.c, self.x)
        if axis == 1:
            return device(self.z, rem4(self.y + d), self.c, self.x)
        return device(self.z, self.y, self.c, rem4(self.x + d))

    def along(self, d):
        return (lax.rem(self.chip + d + 16, 16) * 2 + self.c, self.x)


class Gather:
    def __init__(self, r, ref, rows, cut, lanes, first, send, recv):
        self.r, self.ref, self.rows, self.cut, self.lanes = r, ref, rows, cut, lanes
        self.first, self.send, self.recv, self.sent = first, send, recv, []

    def copy(self, phase, d, part, to, i):
        r = self.r
        axis = self.first if phase == 0 else 1 - self.first
        z, y = (rem4(r.z + d), r.y) if axis == 0 else (r.z, rem4(r.y + d))
        if phase == 0:
            rows = (pl.ds(0, self.rows), pl.ds(0, self.cut), pl.ds(self.cut, self.rows - self.cut))[part]
            ref = self.ref.at[z, y, rows, self.lanes]
        else:
            many = (pl.ds(0, 4), pl.ds(0, 2), pl.ds(2, 2))[part]
            ref = self.ref.at[z, many, :, self.lanes] if axis == 0 else self.ref.at[many, y, :, self.lanes]
        j = phase * 4 + i
        return remote(ref, ref, self.send.at[j], self.recv.at[j], r.near(axis, to))

    def start(self, *a):
        copy = self.copy(*a)
        copy.start()
        self.sent.append(copy)

    def full(self, phase):
        self.start(phase, 0, 0, 1, 0)
        self.start(phase, 0, 0, -1, 1)

    def forward(self, phase):
        self.copy(phase, -1, 0, 1, 0).wait_recv()
        self.start(phase, -1, 1, 1, 2)
        self.copy(phase, 1, 0, -1, 1).wait_recv()
        self.start(phase, 1, 2, -1, 3)

    def finish(self, phase):
        self.copy(phase, -2, 1, 1, 2).wait_recv()
        self.copy(phase, 2, 2, -1, 3).wait_recv()

    def drain(self):
        for copy in self.sent:
            copy.wait_send()
        self.sent = []


class Both:
    def __init__(self, parts):
        self.parts = parts

    def step(self, i):
        for p in self.parts:
            if i == 1:
                p.full(0)
            elif i == 2:
                p.forward(0)
            elif i == 3:
                p.finish(0)
                p.full(1)
            elif i == 4:
                p.forward(1)
            elif i == 5:
                p.finish(1)

    def run(self):
        for i in range(1, 6):
            self.step(i)

    def drain(self):
        for p in self.parts:
            p.drain()


class Scatter:
    def __init__(self, r, ref, lanes, width, first, bufs, send, recv):
        self.r, self.ref, self.lanes, self.width = r, ref, lanes, width
        self.first, self.bufs, self.send, self.recv, self.sent = first, bufs, send, recv, []

    def unit(self, phase, d, part):
        r = self.r
        axis = self.first if phase == 0 else 1 - self.first
        z, y = (rem4(r.z + d), r.y) if axis == 0 else (r.z, rem4(r.y + d))
        if phase == 1:
            rows = pl.ds(64 * part, 64)
            return self.ref.at[z, y, rows, self.lanes]
        many = pl.ds(2 * part, 2)
        return self.ref.at[z, many, :, self.lanes] if axis == 0 else self.ref.at[many, y, :, self.lanes]

    def landing(self, phase, i):
        return self.bufs[phase].at[i, :, :, self.lanes] if phase == 0 else self.bufs[phase].at[i, :, self.lanes]

    def copy(self, phase, d, part, to, i):
        j = phase * 6 + i
        axis = self.first if phase == 0 else 1 - self.first
        return remote(
            self.unit(phase, d, part), self.landing(phase, i), self.send.at[j], self.recv.at[j],
            self.r.near(axis, to),
        )

    def start(self, *a):
        copy = self.copy(*a)
        copy.start()
        self.sent.append(copy)

    def arrived(self, phase, i):
        self.copy(phase, 0, 0, 1, i).wait_recv()

    def add(self, phase, d, part, many):
        unit = self.unit(phase, d, part)
        lands = [self.landing(phase, i) for i in many]
        if phase == 0:
            def body(i):
                k, rows = i // 4, span(lax.rem(i, 4) * 32, 32)
                total = unit[k, rows, :].astype(F32)
                for l in lands:
                    total = total + l[k, rows, :].astype(F32)
                unit[k, rows, :] = total.astype(BF16)
            loop(8, body)
        else:
            def body(i):
                rows = span(i * 32, 32)
                total = unit[rows, :].astype(F32)
                for l in lands:
                    total = total + l[rows, :].astype(F32)
                unit[rows, :] = total.astype(BF16)
            loop(2, body)

    def begin(self, phase):
        self.start(phase, 2, 0, 1, 0)
        self.start(phase, 2, 1, -1, 1)
        self.start(phase, 1, 1, 1, 3)
        self.start(phase, -1, 0, -1, 4)

    def forward(self, phase):
        self.arrived(phase, 0)
        self.add(phase, 1, 0, (0,))
        self.start(phase, 1, 0, 1, 2)
        self.arrived(phase, 1)
        self.add(phase, -1, 1, (1,))
        self.start(phase, -1, 1, -1, 5)

    def finish(self, phase):
        self.arrived(phase, 4)
        self.arrived(phase, 2)
        self.add(phase, 0, 0, (2, 4))
        self.arrived(phase, 3)
        self.arrived(phase, 5)
        self.add(phase, 0, 1, (3, 5))

    def drain(self):
        for copy in self.sent:
            copy.wait_send()
        self.sent = []


class CrossSum:
    def __init__(self, r, part, got, mid, one, two, send, recv):
        self.r, self.part, self.got, self.mid, self.one, self.two = r, part, got, mid, one, two
        self.send, self.recv, self.sent = send, recv, []

    def start(self, copy):
        copy.start()
        self.sent.append(copy)

    def rows(self, c, x):
        return span((c * 4 + x) * 32, 32)

    def pair(self, d):
        x = rem4(self.r.x + d)
        return remote(
            self.part.at[self.rows(1 - self.r.c, x)], self.got.at[x],
            self.send.at[d], self.recv.at[d], self.r.sib,
        )

    def begin(self):
        for d in (2, 1, 3, 0):
            self.start(self.pair(d))

    def pairsum(self, d):
        self.pair(d).wait_recv()
        x = rem4(self.r.x + d)
        rows = self.rows(self.r.c, x)
        self.mid[x] = (self.part[rows].astype(F32) + self.got[x].astype(F32)).astype(BF16)

    def far(self, side):
        x = rem4(self.r.x + 2)
        return remote(
            self.mid.at[x, pl.ds(16 * side, 16)], self.one.at[side],
            self.send.at[4 + side], self.recv.at[4 + side], self.r.near(2, 1 - 2 * side),
        )

    def late(self, side, summed):
        d = 1 - 2 * side
        x = rem4(self.r.x + d)
        half = side if summed else 1 - side
        j = 6 + side * 2 + summed
        return remote(
            self.mid.at[x, pl.ds(16 * half, 16)], self.two.at[side, pl.ds(16 * half, 16)],
            self.send.at[j], self.recv.at[j], self.r.near(2, d),
        )

    def middle(self):
        self.pairsum(2)
        self.start(self.far(0))
        self.start(self.far(1))
        self.pairsum(1)
        self.start(self.late(0, 0))
        self.pairsum(3)
        self.start(self.late(1, 0))
        for side in range(2):
            self.far(side).wait_recv()
            x = rem4(self.r.x + 1 - 2 * side)
            rows = pl.ds(16 * side, 16)
            self.mid[x, rows] = (self.mid[x, rows].astype(F32) + self.one[side].astype(F32)).astype(BF16)
            self.start(self.late(side, 1))

    def end(self):
        self.pair(0).wait_recv()
        for side in range(2):
            self.late(side, 0).wait_recv()
            self.late(side, 1).wait_recv()

    def result(self, rows):
        base = (self.r.c * 4 + self.r.x) * 32
        own = self.part[pl.ds(pl.multiple_of(base + rows.start, rows.size), rows.size)].astype(F32)
        own = own + self.got[self.r.x, rows].astype(F32)
        return own + self.two[0, rows].astype(F32) + self.two[1, rows].astype(F32)

    def drain(self):
        for copy in self.sent:
            copy.wait_send()
        self.sent = []


class CrossGather:
    def __init__(self, r, ref, both, send, recv):
        self.r, self.ref, self.both, self.send, self.recv, self.sent = r, ref, both, send, recv, []

    def start(self, copy):
        copy.start()
        self.sent.append(copy)

    def rows(self, d, part, sibling=False):
        c = 1 - self.r.c if sibling else self.r.c
        base = rem4(self.r.x + d) * 32
        if self.both:
            base = base + c * 128
        if part is None:
            return self.ref.at[pl.ds(pl.multiple_of(base, 32), 32)]
        return self.ref.at[pl.ds(pl.multiple_of(base + 16 * part, 16), 16)]

    def ring(self, d, part, to, i):
        ref = self.rows(d, part)
        return remote(ref, ref, self.send.at[i], self.recv.at[i], self.r.near(2, to))

    def pair(self, d):
        ref = self.rows(d, None)
        return remote(ref, ref, self.send.at[4 + d % 4], self.recv.at[4 + d % 4], self.r.sib)

    def begin(self):
        self.start(self.ring(0, None, 1, 0))
        self.start(self.ring(0, None, -1, 1))
        if self.both:
            self.start(self.pair(0))

    def middle(self):
        self.ring(-1, None, 1, 0).wait_recv()
        self.start(self.ring(-1, 0, 1, 2))
        self.ring(1, None, -1, 1).wait_recv()
        self.start(self.ring(1, 1, -1, 3))
        if self.both:
            self.start(self.pair(-1))
            self.start(self.pair(1))

    def end(self):
        self.ring(-2, 0, 1, 2).wait_recv()
        self.ring(2, 1, -1, 3).wait_recv()
        if self.both:
            self.start(self.pair(2))
            for d in (0, -1, 1, 2):
                ref = self.rows(d, None, True)
                remote(ref, ref, self.send.at[4 + d % 4], self.recv.at[4 + d % 4], self.r.sib).wait_recv()

    def drain(self):
        for copy in self.sent:
            copy.wait_send()
        self.sent = []


class Refs:
    pass


SCRATCH = {
    "ga": ((4, 4, 128, LANES_A), BF16),
    "gb": ((4, 4, 128, LANES_B), BF16),
    "s0a": ((6, 2, 128, LANES_A), BF16),
    "s0b": ((6, 2, 128, LANES_B), BF16),
    "s1a": ((6, 64, LANES_A), BF16),
    "s1b": ((6, 64, LANES_B), BF16),
    "sib_a": ((64, LANES_A), BF16),
    "sib_b": ((64, LANES_B), BF16),
    "gains_all": ((4, 4, 16, 128), F32),
    "gains": ((8, 2048), F32),
    "keep": ((256, 256), F32),
    "gy": ((256, 2048), BF16),
    "n1": ((256, 2048), BF16),
    "n2": ((256, 2048), BF16),
    "dh": ((256, 2048), BF16),
    "part": ((256, 2048), BF16),
    "mid": ((4, 32, 2048), BF16),
    "got": ((4, 4, 32, 2048), BF16),
    "one": ((4, 2, 16, 2048), BF16),
    "two": ((4, 2, 32, 2048), BF16),
    "bo": ((128, 2048), BF16),
    "gt": ((128, 2048), BF16),
    "h": ((32, 2048), F32),
    "dhf": ((32, 2048), F32),
    "p": ((264, 768), F32),
    "q0": ((256, 256), F32),
    "q1": ((256, 256), F32),
    "q2": ((256, 256), F32),
    "u": ((256, 256), F32),
    "v": ((256, 256), F32),
    "z": ((256, 256), BF16),
    "st_re": ((257, 16, 256), F32),
    "st_im": ((257, 16, 256), F32),
    "ends": ((4, 4, 32, 256), F32),
    "back_ends": ((4, 4, 32, 256), F32),
    "gu": ((256, 1408), F32),
    "act": ((256, 768), BF16),
    "dgu": ((256, 1408), BF16),
    "dv": ((256, 256), F32),
    "dq": ((264, 768), F32),
    "dp": ((256, 768), BF16),
    "small": ((4, 4, 80, 256), BF16),
    "small_sum": ((80, 256), F32),
    "small_sib": ((80, 256), F32),
    "ggain": ((8, 2048), F32),
    "ggain_all": ((8, 8, 2048), F32),
}
SEMS = {
    "w": (4, 2, 8), "w_sib": (4, 2), "gain": (8,), "gain_sib": (), "keep_s": (), "gy_s": (), "n1_s": (),
    "p_s": (), "dq_s": (), "ends_s": (2, 8), "back_s": (2, 8), "sum": (4, 10), "cg": (4, 8),
    "rs": (4, 2, 12), "rs_sib": (4, 2), "small_s": (2, 8), "small_x": (), "gg": (8,),
}


def kernel(*refs):
    names = ["mine", "other", "gain_in", "keep_in", "tok", "cot", "taps", "poles"]
    outs = ["block_out", "grad_tok", "grad_w", "grad_small", "grad_gain"]
    k = Refs()
    for name, ref in zip(names + outs + list(SCRATCH), refs):
        setattr(k, name, ref)
    rest = refs[len(names) + len(outs) + len(SCRATCH):]
    S, R = {}, {}
    for i, name in enumerate(SEMS):
        S[name], R[name] = rest[2 * i], rest[2 * i + 1]
    local = rest[2 * len(SEMS)]
    r = Rings()
    g = (k.ga, k.gb)
    z, y, c, x = r.z, r.y, r.c, r.x

    barrier = pltpu.get_barrier_semaphore()
    peers = [r.sib] + [r.near(a, d) for a in range(3) for d in (1, -1)] + [r.along(1), r.along(-1)]
    for peer in peers:
        pl.semaphore_signal(barrier, inc=1, device_id=peer, device_id_type=MESH)
    pl.semaphore_wait(barrier, len(peers))

    def lanes(n, h):
        o, w = CHUNKS[n][h]
        return pl.ds(o, w)

    def weight(n, h, i):
        o, w = CHUNKS[n][h]
        return g[h][i, :, :, o:o + w].reshape(512, w)

    pending = []

    my64 = span(c * 64, 64)
    my128 = span(c * 128, 128)
    gather = [
        Both([Gather(r, g[h], 128, 64, lanes(n, h), 1 - h, S["w"].at[n, h], R["w"].at[n, h]) for h in range(2)])
        for n in range(4)
    ]

    def weight_sib(n, h):
        o, w = CHUNKS[n][h]
        return remote(
            k.other.at[:, pl.ds(o + (LANES_A if h else 0), w)], g[h].at[z, y, my64, lanes(n, h)],
            S["w_sib"].at[n, h], R["w_sib"].at[n, h], r.sib,
        )

    for n in range(4):
        for h in range(2):
            weight_sib(n, h).start()
            o, w = CHUNKS[n][h]
            so = o + (LANES_A if h else 0)
            g[h][z, y, my64, o:o + w] = k.mine[:, so:so + w]
        if n == 0:
            eight = span(c * 8, 8)
            gain_sib = remote(k.gain_in, k.gains_all.at[z, y, eight], S["gain_sib"], R["gain_sib"], r.sib)
            gain_sib.start()
            k.gains_all[z, y, eight] = k.gain_in[...]
    keep_sib = remote(k.keep_in, k.keep.at[my128], S["keep_s"], R["keep_s"], r.sib)
    keep_sib.start()
    k.keep[my128] = k.keep_in[...]
    gy_sib = remote(k.cot, k.gy.at[my128], S["gy_s"], R["gy_s"], r.sib)
    gy_sib.start()
    k.gy[my128] = k.cot[...]

    def ag(n, i):
        if i == 1:
            for h in range(2):
                weight_sib(n, h).wait_recv()
        gather[n].step(i)

    gain_all = Both([Gather(r, k.gains_all, 16, 8, pl.ds(0, 128), 1, S["gain"], R["gain"])])
    gain_sib.wait_recv()
    gain_all.step(1)
    ag(IN, 1)
    gain_all.step(2)
    gain_all.step(3)
    ag(IN, 2)
    gain_all.step(4)
    gain_all.step(5)
    ag(OUT, 1)
    ag(IN, 3)
    for i in range(16):
        k.gains[:, i * 128:(i + 1) * 128] = k.gains_all[i // 4, i % 4, 0:8] + k.gains_all[i // 4, i % 4, 8:16]

    def norm_one(i):
        rows = span(i * 16, 16)
        a = k.tok[rows, :].astype(F32)
        s = lax.rsqrt(jnp.mean(a * a, axis=-1, keepdims=True) + EPSILON)
        k.n1[pl.ds(pl.multiple_of(c * 128 + i * 16, 16), 16), :] = (a * s * k.gains[0:1, :]).astype(BF16)
    loop(8, norm_one)
    n1_sib = remote(k.n1.at[my128], k.n1.at[my128], S["n1_s"], R["n1_s"], r.sib)
    n1_sib.start()
    ag(OUT, 2)
    ag(GU, 1)
    ag(IN, 4)
    ag(OUT, 3)
    ag(GU, 2)
    k_other = span((1 - c) * 128, 128)
    remote(k.n1.at[k_other], k.n1.at[k_other], S["n1_s"], R["n1_s"], r.sib).wait_recv()
    ag(IN, 5)
    ag(DOWN, 1)
    ag(OUT, 4)
    ag(GU, 3)

    k.p[8:264, :] = jnp.zeros((256, 768), F32)

    def project(i):
        a = k.n1[:, pl.ds(pl.multiple_of(i * 512, 512), 512)]
        for h in range(2):
            o = 384 * h
            k.p[8:264, o:o + 384] += nn(a, weight(IN, h, i))
    loop(4, project)

    def round_p(i):
        rows = span(8 + i * 8, 8)
        k.p[rows, :] = k.p[rows, :].astype(BF16).astype(F32)
    loop(32, round_p)
    p_next = remote(k.p.at[256:264], k.p.at[0:8], S["p_s"], R["p_s"], r.along(1))
    p_next.start()
    ag(DOWN, 2)
    p_next.wait()
    remote(k.keep.at[k_other], k.keep.at[k_other], S["keep_s"], R["keep_s"], r.sib).wait_recv()

    def masks(i):
        rows = span(i * 16, 16)
        near = k.keep[rows, :]
        before = k.keep[span(jnp.maximum(i * 16 - 8, 0), 8), :]
        first = jnp.where(i == 0, 1.0, before[7:8, :])
        shifted = jnp.concatenate([first, near[0:15, :]], 0)
        return near, near * shifted

    def short(i):
        near, far = masks(i)
        ext = k.p[pl.ds(pl.multiple_of(i * 16, 16), 24), :]
        q = []
        for b in range(3):
            l = slice(b * 256, b * 256 + 256)
            e = ext[:, l]
            q.append(
                k.taps[0:1, l] * e[8:24] + near * k.taps[1:2, l] * e[7:23] + far * k.taps[2:3, l] * e[6:22]
            )
        rows = span(i * 16, 16)
        k.q0[rows, :] = q[0]
        k.q1[rows, :] = q[1]
        k.q2[rows, :] = q[2]
        k.u[rows, :] = q[1] * q[2]
    loop(16, short)

    zero = jnp.zeros((16, 256), F32)
    lr, li, cr, ci, pr, pi = (k.poles[i] for i in range(6))

    def advance(re, im, u, keep):
        kr, ki = keep * re, keep * im
        return lr * kr - li * ki + u, lr * ki + li * kr

    def end_state(i, state):
        rows = span(i * 8, 8)
        u, keep = k.u[rows, :], k.keep[rows, :]
        for j in range(8):
            state = advance(*state, u[j:j + 1, :], keep[j:j + 1, :])
        return state

    def exchange(re, im, ref, send, recv):
        ref[z, y, 0:16] = re
        ref[z, y, 16:32] = im
        return Both([
            Gather(r, ref, 32, 16, pl.ds(128 * h, 128), 1 - h, send.at[h], recv.at[h]) for h in range(2)
        ])

    end = lax.fori_loop(0, 32, end_state, (zero, zero))
    ends = exchange(*end, k.ends, S["ends_s"], R["ends_s"])
    ends.step(1)
    ag(OUT, 5)
    ends.step(2)
    ends.step(3)
    ag(GU, 4)
    ag(DOWN, 3)
    ends.step(4)
    ends.step(5)
    enter = (zero, zero)
    for i in range(15):
        er, ei = enter
        nr = pr * er - pi * ei + k.ends[i // 4, i % 4, 0:16]
        ni = pr * ei + pi * er + k.ends[i // 4, i % 4, 16:32]
        enter = (jnp.where(i < r.chip, nr, er), jnp.where(i < r.chip, ni, ei))
    k.st_re[0] = enter[0]
    k.st_im[0] = enter[1]

    def scan(i, state):
        rows = span(i * 8, 8)
        u, keep = k.u[rows, :], k.keep[rows, :]
        for j in range(8):
            state = advance(*state, u[j:j + 1, :], keep[j:j + 1, :])
            k.st_re[i * 8 + j + 1] = state[0]
            k.st_im[i * 8 + j + 1] = state[1]
            k.v[pl.ds(i * 8 + j, 1), :] = jnp.sum(cr * state[0] - ci * state[1], axis=0, keepdims=True)
        return state
    lax.fori_loop(0, 32, scan, enter)

    def gated(i):
        rows = span(i * 32, 32)
        k.z[rows, :] = (k.q0[rows, :] * k.v[rows, :]).astype(BF16)
    loop(8, gated)

    def out_weight(i):
        return jnp.concatenate([weight(OUT, 0, i), weight(OUT, 1, i)], 1)

    def mix(i):
        k.part[:, span(i * 512, 512)] = nt(k.z[...], out_weight(i)).astype(BF16)
    loop(4, mix)

    def cross(i):
        return CrossSum(r, k.part, k.got.at[i], k.mid, k.one.at[i], k.two.at[i], S["sum"].at[i], R["sum"].at[i])

    s_mix = cross(0)
    s_mix.begin()
    s_mix.middle()
    s_mix.end()

    own = (c * 4 + x) * 32

    def norm_two(i):
        rows = pl.ds(pl.multiple_of(i * 16, 16), 16)
        a = k.tok[pl.ds(pl.multiple_of(x * 32 + i * 16, 16), 16), :].astype(F32) + s_mix.result(rows)
        k.h[rows, :] = a
        s = lax.rsqrt(jnp.mean(a * a, axis=-1, keepdims=True) + EPSILON)
        k.n2[pl.ds(pl.multiple_of(own + i * 16, 16), 16), :] = (a * s * k.gains[1:2, :]).astype(BF16)
    loop(2, norm_two)
    g_n2 = CrossGather(r, k.n2, True, S["cg"].at[0], R["cg"].at[0])
    g_n2.begin()
    g_n2.middle()
    ag(GU, 5)
    ag(DOWN, 4)
    g_n2.end()
    s_mix.drain()

    def gate_up(i):
        a = k.n2[:, pl.ds(pl.multiple_of(i * 512, 512), 512)]
        for h in range(2):
            o, w = (0, 768) if h == 0 else (768, 640)
            t = nn(a, weight(GU, h, i))

            @pl.when(i == 0)
            def _():
                k.gu[:, o:o + w] = t

            @pl.when(i > 0)
            def _():
                k.gu[:, o:o + w] += t
    loop(4, gate_up)
    k.act[:, 640:768] = jnp.zeros((256, 128), BF16)

    def activate(i):
        rows = span(i * 16, 16)
        gu = k.gu[rows, :]
        gate, up = gu[:, 0:704], gu[:, 704:1408]
        k.act[rows, 0:704] = (gate * jax.nn.sigmoid(gate) * up).astype(BF16)
    loop(16, activate)
    ag(DOWN, 5)

    def down_weight(i):
        return jnp.concatenate([weight(DOWN, 0, i), weight(DOWN, 1, i)], 1)

    def ffn(i):
        k.part[:, span(i * 512, 512)] = nt(k.act[...], down_weight(i)).astype(BF16)
    loop(4, ffn)
    s_ffn = cross(1)
    s_ffn.begin()
    s_ffn.middle()
    s_ffn.end()

    def top(i):
        rows = pl.ds(pl.multiple_of(i * 16, 16), 16)
        k.bo[pl.ds(pl.multiple_of(x * 32 + i * 16, 16), 16), :] = (k.h[rows, :] + s_ffn.result(rows)).astype(BF16)
    loop(2, top)
    s_ffn.drain()
    g_bo = CrossGather(r, k.bo, False, S["cg"].at[1], R["cg"].at[1])
    g_bo.begin()
    g_bo.middle()

    remote(k.gy.at[k_other], k.gy.at[k_other], S["gy_s"], R["gy_s"], r.sib).wait_recv()
    for n in range(4):
        gather[n].drain()

    def d_act(i):
        t = nn(k.gy[:, pl.ds(pl.multiple_of(i * 512, 512), 512)], down_weight(i))

        @pl.when(i == 0)
        def _():
            k.dq[0:256, :] = t

        @pl.when(i > 0)
        def _():
            k.dq[0:256, :] += t
    loop(4, d_act)

    def d_gates(i):
        rows = span(i * 16, 16)
        gu = k.gu[rows, :]
        gate, up = gu[:, 0:704], gu[:, 704:1408]
        da = k.dq[rows, :][:, 0:704]
        sg = jax.nn.sigmoid(gate)
        dgate = da * up * sg * (1.0 + gate * (1.0 - sg))
        dup = da * (gate * sg)
        k.dgu[rows, :] = jnp.concatenate([dgate, dup], 1).astype(BF16)
    loop(16, d_gates)

    def d_n2(i):
        w = jnp.concatenate([weight(GU, 0, i), weight(GU, 1, i)], 1)
        k.part[:, span(i * 512, 512)] = nt(k.dgu[...], w).astype(BF16)
    loop(4, d_n2)
    s_dn2 = cross(2)
    s_dn2.begin()

    scatter = [
        [Scatter(r, g[h], lanes(n, h), CHUNKS[n][h][1], h, ((k.s0a, k.s1a), (k.s0b, k.s1b))[h],
                 S["rs"].at[n, h], R["rs"].at[n, h]) for h in range(2)]
        for n in range(4)
    ]
    sib_bufs = (k.sib_a, k.sib_b)

    def rs_sib(n, h):
        return remote(
            g[h].at[z, y, span((1 - c) * 64, 64), lanes(n, h)], sib_bufs[h].at[:, lanes(n, h)],
            S["rs_sib"].at[n, h], R["rs_sib"].at[n, h], r.sib,
        )

    def rs(n, i):
        for h in range(2):
            s = scatter[n][h]
            if i == 0:
                s.begin(0)
            elif i == 1:
                s.forward(0)
            elif i == 2:
                s.finish(0)
                s.begin(1)
            elif i == 3:
                s.forward(1)
            elif i == 4:
                s.finish(1)
                rs_sib(n, h).start()

    def weight_grad(n, a, b):
        wa, wb = CHUNKS[n][0][1], CHUNKS[n][1][1]

        def body(i):
            t = tn(a[:, pl.ds(pl.multiple_of(i * 512, 512), 512)], b[...]).astype(BF16)
            oa, ob = CHUNKS[n][0][0], CHUNKS[n][1][0]
            g[0][i, :, :, oa:oa + wa] = t[:, 0:wa].reshape(4, 128, wa)
            g[1][i, :, :, ob:ob + wb] = t[:, wa:wa + wb].reshape(4, 128, wb)
        loop(4, body)

    weight_grad(DOWN, k.gy, k.act)
    rs(DOWN, 0)
    s_dn2.middle()
    weight_grad(GU, k.n2, k.dgu)
    rs(GU, 0)
    g_bo.end()
    out_bo = pltpu.make_async_copy(k.bo, k.block_out, local.at[0])
    out_bo.start()
    s_dn2.end()

    def d_norm_two(i):
        rows = pl.ds(pl.multiple_of(i * 16, 16), 16)
        a = k.h[rows, :]
        s = lax.rsqrt(jnp.mean(a * a, axis=-1, keepdims=True) + EPSILON)
        hat = a * s
        dn = s_dn2.result(rows)
        dng = dn * k.gains[1:2, :]
        gy = k.gy[pl.ds(pl.multiple_of(own + i * 16, 16), 16), :].astype(F32)
        dh = gy + s * (dng - hat * jnp.mean(dng * hat, axis=-1, keepdims=True))
        k.dhf[rows, :] = dh
        k.dh[pl.ds(pl.multiple_of(own + i * 16, 16), 16), :] = dh.astype(BF16)
        t = jnp.sum(dn * hat, axis=0, keepdims=True)

        @pl.when(i == 0)
        def _():
            k.ggain[1:2, :] = t

        @pl.when(i > 0)
        def _():
            k.ggain[1:2, :] += t
    loop(2, d_norm_two)
    s_dn2.drain()
    g_dh = CrossGather(r, k.dh, True, S["cg"].at[2], R["cg"].at[2])
    g_dh.begin()
    rs(DOWN, 1)
    g_dh.middle()
    rs(DOWN, 2)
    rs(GU, 1)
    g_dh.end()

    def d_z(i):
        t = nn(k.dh[:, pl.ds(pl.multiple_of(i * 512, 512), 512)], out_weight(i))

        @pl.when(i == 0)
        def _():
            k.dv[...] = t

        @pl.when(i > 0)
        def _():
            k.dv[...] += t
    loop(4, d_z)

    def d_gated(i):
        rows = span(i * 32, 32)
        dz = k.dv[rows, :]
        k.dq[rows, 0:256] = dz * k.v[rows, :]
        k.dv[rows, :] = dz * k.q0[rows, :]
    loop(8, d_gated)

    def retreat(a, b, keep):
        ka, kb = keep * a, keep * b
        return ka, kb, lr * ka + li * kb, lr * kb - li * ka

    def start_state(i, state):
        rows = span((31 - i) * 8, 8)
        dv, keep = k.dv[rows, :], k.keep[rows, :]
        for j in reversed(range(8)):
            a = cr * dv[j:j + 1, :] + state[0]
            b = state[1] - ci * dv[j:j + 1, :]
            _, _, pa, pb = retreat(a, b, keep[j:j + 1, :])
            state = (pa, pb)
        return state

    begin = lax.fori_loop(0, 32, start_state, (zero, zero))
    backs = exchange(*begin, k.back_ends, S["back_s"], R["back_s"])
    backs.step(1)
    weight_grad(OUT, k.dh, k.z)
    rs(OUT, 0)
    backs.step(2)
    backs.step(3)
    rs(DOWN, 3)
    backs.step(4)
    rs(GU, 2)
    backs.step(5)
    arrive = (zero, zero)
    for i in reversed(range(1, 16)):
        er, ei = arrive
        nr = pr * er + pi * ei + k.back_ends[i // 4, i % 4, 0:16]
        ni = pr * ei - pi * er + k.back_ends[i // 4, i % 4, 16:32]
        arrive = (jnp.where(i > r.chip, nr, er), jnp.where(i > r.chip, ni, ei))

    def adjoint(i, carry):
        pa, pb, dcr, dci, dlr, dli = carry
        rows = span((31 - i) * 8, 8)
        dv, keep = k.dv[rows, :], k.keep[rows, :]
        for j in reversed(range(8)):
            t = (31 - i) * 8 + j
            d = dv[j:j + 1, :]
            a = cr * d + pa
            b = pb - ci * d
            k.u[pl.ds(t, 1), :] = jnp.sum(a, axis=0, keepdims=True)
            dcr = dcr + d * k.st_re[t + 1]
            dci = dci - d * k.st_im[t + 1]
            ka, kb, pa, pb = retreat(a, b, keep[j:j + 1, :])
            sr, si = k.st_re[t], k.st_im[t]
            dlr = dlr + ka * sr + kb * si
            dli = dli + kb * sr - ka * si
        return pa, pb, dcr, dci, dlr, dli

    _, _, dcr, dci, dlr, dli = lax.fori_loop(0, 32, adjoint, (*arrive, zero, zero, zero, zero))

    def d_branches(i):
        rows = span(i * 32, 32)
        du = k.u[rows, :]
        k.dq[rows, 256:512] = du * k.q2[rows, :]
        k.dq[rows, 512:768] = du * k.q1[rows, :]
    loop(8, d_branches)
    dq_next = remote(k.dq.at[0:8], k.dq.at[256:264], S["dq_s"], R["dq_s"], r.along(-1))
    dq_next.start()
    rs(OUT, 1)
    dq_next.wait()

    last = jnp.where(r.chip < 15, 1.0, 0.0)

    def d_short(i, taps):
        d = k.dq[pl.ds(pl.multiple_of(i * 16, 16), 24), :]
        near, far = masks(i)
        j = jnp.minimum(i * 16 + 16, 248)
        after = k.keep[span(j, 8), :]
        inside = i < 15
        tail_near = jnp.where(inside, after, last)
        tail_far = jnp.where(
            inside, after * jnp.concatenate([near[15:16, :], after[0:7, :]], 0), last
        )
        near = jnp.concatenate([near, tail_near], 0)
        far = jnp.concatenate([far, tail_far], 0)
        ext = k.p[pl.ds(pl.multiple_of(i * 16, 16), 24), :]
        rows = span(i * 16, 16)
        new = []
        for b in range(3):
            l = slice(b * 256, b * 256 + 256)
            e, db = ext[:, l], d[:, l]
            dn, df = near * db, far * db
            k.dp[rows, l] = (
                k.taps[0:1, l] * db[0:16] + k.taps[1:2, l] * dn[1:17] + k.taps[2:3, l] * df[2:18]
            ).astype(BF16)
            new.append(taps[3 * 0 + b] + jnp.sum(e[8:24] * db[0:16], axis=0, keepdims=True))
            new.append(taps[3 * 1 + b] + jnp.sum(e[7:23] * dn[0:16], axis=0, keepdims=True))
            new.append(taps[3 * 2 + b] + jnp.sum(e[6:22] * df[0:16], axis=0, keepdims=True))
        return tuple(new[3 * b + t] for t in range(3) for b in range(3))

    line = jnp.zeros((1, 256), F32)
    dtaps = lax.fori_loop(0, 16, d_short, (line,) * 9)

    def d_n1(i):
        w = jnp.concatenate([weight(IN, 0, i), weight(IN, 1, i)], 1)
        k.part[:, span(i * 512, 512)] = nt(k.dp[...], w).astype(BF16)
    loop(4, d_n1)
    s_dn1 = cross(3)
    s_dn1.begin()
    weight_grad(IN, k.n1, k.dp)
    rs(IN, 0)

    mine_small = [dcr, dci, dlr, dli]
    for i in range(4):
        k.small[z, y, 16 * i:16 * i + 16] = mine_small[i].astype(BF16)
    k.small[z, y, 64:80] = jnp.concatenate(list(dtaps) + [jnp.zeros((7, 256), F32)], 0).astype(BF16)
    smalls = Both([
        Gather(r, k.small, 80, 48, pl.ds(128 * h, 128), 1 - h, S["small_s"].at[h], R["small_s"].at[h])
        for h in range(2)
    ])
    s_dn1.middle()
    smalls.step(1)
    rs(GU, 3)
    rs(DOWN, 4)
    s_dn1.end()

    def d_norm_one(i):
        rows = pl.ds(pl.multiple_of(i * 16, 16), 16)
        here = pl.ds(pl.multiple_of(x * 32 + i * 16, 16), 16)
        a = k.tok[here, :].astype(F32)
        s = lax.rsqrt(jnp.mean(a * a, axis=-1, keepdims=True) + EPSILON)
        hat = a * s
        dn = s_dn1.result(rows)
        dng = dn * k.gains[0:1, :]
        k.gt[here, :] = (
            k.dhf[rows, :] + s * (dng - hat * jnp.mean(dng * hat, axis=-1, keepdims=True))
        ).astype(BF16)
        t = jnp.sum(dn * hat, axis=0, keepdims=True)

        @pl.when(i == 0)
        def _():
            k.ggain[0:1, :] = t

        @pl.when(i > 0)
        def _():
            k.ggain[0:1, :] += t
    loop(2, d_norm_one)
    s_dn1.drain()
    g_gt = CrossGather(r, k.gt, False, S["cg"].at[3], R["cg"].at[3])
    g_gt.begin()
    rs(IN, 1)
    smalls.step(2)
    g_gt.middle()
    smalls.step(3)
    rs(OUT, 2)
    rs(GU, 4)
    smalls.step(4)
    rs(IN, 2)
    g_gt.end()
    out_gt = pltpu.make_async_copy(k.gt, k.grad_tok, local.at[1])
    out_gt.start()
    smalls.step(5)

    def small_total(i):
        rows = span(i * 16, 16)
        t = jnp.zeros((16, 256), F32)
        for j in range(16):
            t = t + k.small[j // 4, j % 4, rows, :].astype(F32)
        k.small_sum[rows, :] = t
    loop(5, small_total)
    small_x = remote(k.small_sum, k.small_sib, S["small_x"], R["small_x"], r.sib)
    small_x.start()
    rs(OUT, 3)
    rs(IN, 3)
    rs(OUT, 4)
    rs(IN, 4)
    small_x.wait()

    copies = [out_bo, out_gt]
    for j, src in enumerate((k.small_sum, k.small_sib)):
        copies.append(pltpu.make_async_copy(src, k.grad_small.at[j], local.at[2 + j]))
    copies.append(pltpu.make_async_copy(k.ggain, k.grad_gain, local.at[4]))
    for n in range(4):
        for h in range(2):
            rs_sib(n, h).wait()
    for h in range(2):
        wide = pl.ds(LANES_A if h else 0, LANES_B if h else LANES_A)
        copies.append(pltpu.make_async_copy(g[h].at[z, y, my64], k.grad_w.at[0, :, wide], local.at[5 + 2 * h]))
        copies.append(pltpu.make_async_copy(sib_bufs[h], k.grad_w.at[1, :, wide], local.at[6 + 2 * h]))
    for copy in copies[2:]:
        copy.start()
    for copy in copies:
        copy.wait()
    for n in range(4):
        for h in range(2):
            weight_sib(n, h).wait_send()
            scatter[n][h].drain()
    for copy in (gain_sib, keep_sib, gy_sib, n1_sib):
        copy.wait_send()
    for group in (gain_all, ends, backs, smalls, g_n2, g_bo, g_dh, g_gt):
        group.drain()


def block(*arrays):
    sems = []
    for shape in SEMS.values():
        sems += [pltpu.SemaphoreType.DMA(shape)] * 2
    vmem = pl.BlockSpec(memory_space=pltpu.VMEM)
    return pl.pallas_call(
        kernel,
        out_shape=(
            jax.ShapeDtypeStruct((128, 2048), BF16),
            jax.ShapeDtypeStruct((128, 2048), BF16),
            jax.ShapeDtypeStruct((2, 64, LANES_A + LANES_B), BF16),
            jax.ShapeDtypeStruct((2, 80, 256), F32),
            jax.ShapeDtypeStruct((8, 2048), F32),
        ),
        in_specs=[vmem] * len(arrays),
        out_specs=[pl.BlockSpec(memory_space=pl.ANY)] * 5,
        scratch_shapes=[pltpu.VMEM(s, t) for s, t in SCRATCH.values()] + sems + [pltpu.SemaphoreType.DMA((9,))],
        compiler_params=pltpu.CompilerParams(
            collective_id=0, has_side_effects=True, vmem_limit_bytes=63 * 2**20
        ),
        name="block",
    )(*arrays)


def on_device(
    tokens, cotangent, resets, norm1_gain, in_weight, conv_weight, pole_decay, pole_angle, residue_re, residue_im,
    out_weight, norm2_gain, gate_weight, up_weight, down_weight,
):
    c = lax.rem(lax.axis_index("seq"), 2)

    def columns(c):
        def half(w, n):
            return lax.dynamic_slice_in_dim(w, c * n, n, axis=w.ndim - 1)

        i, o = half(in_weight, 256).reshape(64, 768), half(out_weight, 256)
        gu = jnp.concatenate([half(gate_weight, 704), half(up_weight, 704)], 1)
        d = jnp.pad(half(down_weight, 704), ((0, 0), (0, 64)))
        return jnp.concatenate(
            [i[:, :384], o[:, :128], gu[:, :768], d[:, :384], i[:, 384:], o[:, 128:], gu[:, 768:], d[:, 384:]], 1
        )

    def half(a):
        return lax.dynamic_slice_in_dim(a, c * 256, 256, axis=a.ndim - 1)

    gains = jnp.stack([norm1_gain, norm2_gain]).astype(F32)
    gains = lax.dynamic_update_slice(jnp.zeros((8, 128), F32), gains, (0, c * 64))
    keep = jnp.broadcast_to((1.0 - resets.astype(F32))[:, None], (128, 256))
    taps = jnp.pad(half(conv_weight).reshape(3, 768), ((0, 5), (0, 0)))
    decay, angle, res_re, res_im = (half(a) for a in (pole_decay, pole_angle, residue_re, residue_im))
    size, wide = jnp.exp(-decay), jnp.exp(-256.0 * decay)
    gin = jnp.sqrt(-jnp.expm1(-2.0 * decay))
    lr, li = size * jnp.cos(angle), size * jnp.sin(angle)
    poles = jnp.stack(
        [lr, li, gin * res_re, gin * res_im, wide * jnp.cos(256.0 * angle), wide * jnp.sin(256.0 * angle)]
    )
    block_out, grad_tok, grad_w, grad_small, ggain = block(
        columns(c), columns(1 - c), gains, keep, tokens, cotangent, taps, poles
    )

    def order(a, b):
        return jnp.where(c == 0, a, b), jnp.where(c == 0, b, a)

    first, second = order(grad_w[0], grad_w[1])
    s_first, s_second = order(grad_small[0], grad_small[1])

    def join(f):
        return jnp.concatenate([f(first), f(second)], -1).astype(F32)

    def cut(a, n):
        return [a[:, o:o + w] for o, w in ((CHUNKS[n][0][0], CHUNKS[n][0][1]), (LANES_A + CHUNKS[n][1][0], CHUNKS[n][1][1]))]

    def whole(a, n):
        return jnp.concatenate(cut(a, n), 1)

    grad_in = join(lambda a: whole(a, IN).reshape(64, 3, 256))
    grad_out = join(lambda a: whole(a, OUT))
    grad_gate = join(lambda a: whole(a, GU)[:, :704])
    grad_up = join(lambda a: whole(a, GU)[:, 704:])
    grad_down = join(lambda a: whole(a, DOWN)[:, :704])
    small = jnp.concatenate([s_first, s_second], 1)
    dcr, dci, dlr, dli = (small[16 * i:16 * i + 16] for i in range(4))
    grad_taps = small[64:73].reshape(3, 3, 512)
    size = jnp.exp(-pole_decay)
    gin = jnp.sqrt(-jnp.expm1(-2.0 * pole_decay))
    lr, li = size * jnp.cos(pole_angle), size * jnp.sin(pole_angle)
    dgin = residue_re * dcr + residue_im * dci
    grad_decay = dgin * size * size / gin - (lr * dlr + li * dli)
    grad_angle = lr * dli - li * dlr
    gain_sum = lax.psum_scatter(
        lax.psum(ggain[0:2], "mp"), "seq", scatter_dimension=1, tiled=True
    )
    return (
        block_out, grad_tok, gain_sum[0], grad_in, grad_taps, grad_decay, grad_angle, gin * dcr, gin * dci, grad_out,
        gain_sum[1], grad_gate, grad_up, grad_down,
    )


def solution(mesh):
    row, cols = P("seq", "mp"), P(None, "mp")
    return jax.shard_map(
        on_device,
        mesh=mesh,
        in_specs=(
            P("seq", None), P("seq", None), P("seq"), P("seq"), P("seq", None, "mp"), P(None, None, "mp"),
            cols, cols, cols, cols, row, P("seq"), row, row, row,
        ),
        out_specs=(
            P("seq", None), P("seq", None), P("seq"), P("seq", None, "mp"), P(None, None, "mp"),
            cols, cols, cols, cols, row, P("seq"), row, row, row,
        ),
        check_vma=False,
    )
```

```python
import functools

import jax
import jax.numpy as jnp
from jax import lax
from jax.experimental import pallas as pl
from jax.experimental.pallas import tpu as pltpu
from jax.sharding import PartitionSpec as P

EPSILON = 1e-05
BF16, F32 = jnp.bfloat16, jnp.float32
MESH = pl.DeviceIdType.MESH
LANES_A, LANES_B = 1664, 1536
CHUNKS = (
    ((0, 384), (0, 384)),
    ((384, 128), (384, 128)),
    ((512, 384), (512, 384)),
    ((896, 384), (896, 256)),
    ((1280, 384), (1152, 384)),
)
IN, OUT, GU, GU_2, DOWN = range(5)
WHOLE = {IN: CHUNKS[IN], OUT: CHUNKS[OUT], GU: ((512, 768), (512, 640)), DOWN: CHUNKS[DOWN]}


def where():
    place = lax.axis_index("seq")
    chip = place // 2
    return chip // 4, lax.rem(chip, 4), lax.rem(place, 2), lax.axis_index("mp")


def device(z, y, c, x):
    return ((z * 4 + y) * 2 + c, x)


def rem4(a):
    return lax.rem(a + 4, 4)


def remote(src, dst, send, recv, to):
    return pltpu.make_async_remote_copy(
        src_ref=src, dst_ref=dst, send_sem=send, recv_sem=recv, device_id=to, device_id_type=MESH
    )


def nn(a, b):
    return jnp.dot(a, b, preferred_element_type=F32)


def nt(a, b):
    return lax.dot_general(a, b, (((1,), (1,)), ((), ())), preferred_element_type=F32)


def tn(a, b):
    return lax.dot_general(a, b, (((0,), (0,)), ((), ())), preferred_element_type=F32)


def expm1(x):
    series = x / 8.0 + 1.0
    for n in range(7, 1, -1):
        series = series * (x / n) + 1.0
    return jnp.where(jnp.abs(x) < 0.25, x * series, jnp.exp(x) - 1.0)


def fold(count, body, state):
    return lax.fori_loop(0, count, body, state)


def loop(count, body):
    lax.fori_loop(0, count, lambda i, _: (body(i), 0)[1], 0)


def span(start, size):
    return pl.ds(pl.multiple_of(start, size), size)


PLAN = {
    "start": (("ag", IN, 1),),
    "gain_y": (("ag", DOWN, 1), ("ag", IN, 2), ("ag", GU, 1), ("ag", OUT, 1),),
    "gain_z": (("ag", DOWN, 2), ("ag", IN, 3),),
    "n1": (("ag", IN, 4),),
    "edge": (("ag", IN, 5), ("ag", GU_2, 1),),
    "project": (("ag", OUT, 2), ("ag", GU, 2), ("ag", DOWN, 3), ("ag", IN, 6),),
    "short": (("ag", GU_2, 2),),
    "ends_y": (("ag", OUT, 3), ("ag", GU, 3),),
    "ends_z": (("ag", OUT, 4), ("ag", OUT, 5), ("ag", GU_2, 3), ("ag", GU, 4), ("ag", GU_2, 4),),
    "mix": (("ag", OUT, 6),),
    "mix_1": (("ag", GU, 5),),
    "n2_0": (("ag", GU_2, 5), ("ag", DOWN, 4), ("ag", DOWN, 5),),
    "n2_1": (("ag", GU, 6),),
    "ff": (("ag", GU_2, 6),),
    "act": (("wg", DOWN), ("rs", DOWN, 0), ("rs", DOWN, 1), ("ag", DOWN, 6),),
    "dn2_1": (("wg", GU),),
    "dn2_2": (("rs", GU, 0), ("rs", DOWN, 2), ("rs", GU_2, 0), ("rs", GU, 1),),
    "dh_0": (("ffn_0",),),
    "dh_1": (("ffn_1",), ("rs", DOWN, 3),),
    "backs_y": (("wg", OUT), ("rs", OUT, 0), ("ffn_2",),),
    "backs_z": (("rs", DOWN, 4), ("rs", GU, 2), ("rs", OUT, 1), ("ffn_3",),),
    "dq": (("rs", OUT, 2), ("rs", GU_2, 1), ("rs", GU_2, 2),),
    "dn1_0": (("wg", IN), ("rs", IN, 0), ("rs", IN, 1),),
    "dn1_1": (("small", 0), ("rs", IN, 2), ("rs", OUT, 3),),
    "dn1_2": (("rs", GU_2, 3), ("small", 1), ("rs", DOWN, 5),),
    "gt_0": (("ffn_4",), ("rs", IN, 3), ("rs", GU, 3),),
    "gt_1": (("rs", OUT, 4),),
    "gt_2": (("rs", IN, 4), ("rs", GU_2, 4), ("rs", GU, 4), ("small", 2),),
    "gt_3": (("rs", OUT, 5),),
    "gt_4": (("rs", IN, 5), ("rs", GU_2, 5), ("rs", GU, 5), ("ffn_5",),),
}


class Rings:
    def __init__(self):
        self.z, self.y, self.c, self.x = where()
        self.chip = self.z * 4 + self.y
        self.sib = device(self.z, self.y, 1 - self.c, self.x)

    def near(self, axis, d):
        if axis == 0:
            return device(rem4(self.z + d), self.y, self.c, self.x)
        if axis == 1:
            return device(self.z, rem4(self.y + d), self.c, self.x)
        return device(self.z, self.y, self.c, rem4(self.x + d))

    def along(self, d):
        return (lax.rem(self.chip + d + 16, 16) * 2 + self.c, self.x)


class Gather:
    def __init__(self, r, ref, rows, cut, lanes, first, send, recv):
        self.r, self.ref, self.rows, self.cut, self.lanes = r, ref, rows, cut, lanes
        self.first, self.send, self.recv, self.sent = first, send, recv, []

    def copy(self, phase, d, part, to, i):
        r = self.r
        axis = self.first if phase == 0 else 1 - self.first
        z, y = (rem4(r.z + d), r.y) if axis == 0 else (r.z, rem4(r.y + d))
        if phase == 0:
            rows = (pl.ds(0, self.rows), pl.ds(0, self.cut), pl.ds(self.cut, self.rows - self.cut))[part]
            ref = self.ref.at[z, y, rows, self.lanes]
        else:
            many = (pl.ds(0, 4), pl.ds(0, 2), pl.ds(2, 2))[part]
            ref = self.ref.at[z, many, :, self.lanes] if axis == 0 else self.ref.at[many, y, :, self.lanes]
        j = phase * 6 + i
        return remote(ref, ref, self.send.at[j], self.recv.at[j], r.near(axis, to))

    def start(self, *a):
        copy = self.copy(*a)
        copy.start()
        self.sent.append(copy)

    def first_halves(self, phase):
        self.start(phase, 0, 1, 1, 0)
        self.start(phase, 0, 2, -1, 1)

    def second_halves(self, phase):
        self.start(phase, 0, 2, 1, 2)
        self.start(phase, 0, 1, -1, 3)

    def forward(self, phase):
        self.copy(phase, -1, 1, 1, 0).wait_recv()
        self.start(phase, -1, 1, 1, 4)
        self.copy(phase, 1, 2, -1, 1).wait_recv()
        self.start(phase, 1, 2, -1, 5)

    def finish(self, phase):
        self.copy(phase, -1, 2, 1, 2).wait_recv()
        self.copy(phase, 1, 1, -1, 3).wait_recv()
        self.copy(phase, -2, 1, 1, 4).wait_recv()
        self.copy(phase, 2, 2, -1, 5).wait_recv()

    def drain(self):
        for copy in self.sent:
            copy.wait_send()
        self.sent = []


class Both:
    def __init__(self, parts):
        self.parts = parts

    def step(self, i):
        for p in self.parts:
            if i == 1:
                p.first_halves(0)
                p.second_halves(0)
            elif i == 2:
                p.forward(0)
            elif i == 3:
                p.finish(0)
                p.first_halves(1)
            elif i == 4:
                p.second_halves(1)
            elif i == 5:
                p.forward(1)
            elif i == 6:
                p.finish(1)

    def drain(self):
        for p in self.parts:
            p.drain()


class Trade:
    def __init__(self, r, axis, src, land, send, recv):
        self.r, self.axis, self.src, self.land, self.send, self.recv = r, axis, src, land, send, recv
        self.me = (r.z, r.y, r.x)[axis]

    def copy(self, d):
        return remote(
            self.src(rem4(self.me + d)), self.land.at[self.me], self.send.at[d - 1], self.recv.at[d - 1],
            self.r.near(self.axis, d),
        )

    def begin(self):
        for d in (2, 1, 3):
            self.copy(d).start()

    def end(self):
        for d in (1, 3, 2):
            landed = self.land.at[rem4(self.me - d)]
            remote(landed, landed, self.send.at[d - 1], self.recv.at[d - 1], self.r.near(self.axis, d)).wait_recv()

    def drain(self):
        for d in (1, 2, 3):
            self.copy(d).wait_send()


class Scatter:
    def __init__(self, r, ref, lanes, at, first, bufs, send, recv):
        self.r, self.ref, self.lanes, self.at = r, ref, lanes, at
        self.first, self.bufs, self.send, self.recv, self.sent = first, bufs, send, recv, []

    def unit(self, phase, d, part):
        r = self.r
        axis = self.first if phase == 0 else 1 - self.first
        z, y = (rem4(r.z + d), r.y) if axis == 0 else (r.z, rem4(r.y + d))
        if phase == 1:
            rows = pl.ds(64 * part, 64)
            return self.ref.at[z, y, rows, self.lanes]
        many = pl.ds(2 * part, 2)
        return self.ref.at[z, many, :, self.lanes] if axis == 0 else self.ref.at[many, y, :, self.lanes]

    def landing(self, phase, i):
        return self.bufs[phase].at[i, :, :, self.at] if phase == 0 else self.bufs[phase].at[i, :, self.at]

    def copy(self, phase, d, part, to, i):
        j = phase * 6 + i
        axis = self.first if phase == 0 else 1 - self.first
        return remote(
            self.unit(phase, d, part), self.landing(phase, i), self.send.at[j], self.recv.at[j],
            self.r.near(axis, to),
        )

    def start(self, *a):
        copy = self.copy(*a)
        copy.start()
        self.sent.append(copy)

    def arrived(self, phase, i):
        self.copy(phase, 0, 0, 1, i).wait_recv()

    def add(self, phase, d, part, many):
        unit = self.unit(phase, d, part)
        lands = [self.landing(phase, i) for i in many]
        if phase == 0:
            def body(i):
                k, rows = i // 4, span(lax.rem(i, 4) * 32, 32)
                total = unit[k, rows, :].astype(F32)
                for l in lands:
                    total = total + l[k, rows, :].astype(F32)
                unit[k, rows, :] = total.astype(BF16)
            loop(8, body)
        else:
            def body(i):
                rows = span(i * 32, 32)
                total = unit[rows, :].astype(F32)
                for l in lands:
                    total = total + l[rows, :].astype(F32)
                unit[rows, :] = total.astype(BF16)
            loop(2, body)

    def far(self, phase):
        self.start(phase, 2, 0, 1, 0)
        self.start(phase, 2, 1, -1, 1)

    def early(self, phase):
        self.start(phase, 1, 1, 1, 3)
        self.start(phase, -1, 0, -1, 4)

    def forward(self, phase):
        self.arrived(phase, 0)
        self.add(phase, 1, 0, (0,))
        self.start(phase, 1, 0, 1, 2)
        self.arrived(phase, 1)
        self.add(phase, -1, 1, (1,))
        self.start(phase, -1, 1, -1, 5)

    def finish(self, phase):
        self.arrived(phase, 4)
        self.arrived(phase, 2)
        self.add(phase, 0, 0, (2, 4))
        self.arrived(phase, 3)
        self.arrived(phase, 5)
        self.add(phase, 0, 1, (3, 5))

    def drain(self):
        for copy in self.sent:
            copy.wait_send()
        self.sent = []


class CrossSum:
    def __init__(self, r, part, got, mid, one, two, send, recv):
        self.r, self.part, self.got, self.mid, self.one, self.two = r, part, got, mid, one, two
        self.send, self.recv, self.sent = send, recv, []

    def start(self, copy):
        copy.start()
        self.sent.append(copy)

    def rows(self, c, x):
        return span((c * 4 + x) * 32, 32)

    def pair(self, d):
        x = rem4(self.r.x + d)
        return remote(
            self.part.at[self.rows(1 - self.r.c, x)], self.got.at[x],
            self.send.at[d], self.recv.at[d], self.r.sib,
        )

    def begin(self):
        for d in (2, 1, 3, 0):
            self.start(self.pair(d))

    def pairsum(self, d):
        self.pair(d).wait_recv()
        x = rem4(self.r.x + d)
        rows = self.rows(self.r.c, x)
        self.mid[x] = (self.part[rows].astype(F32) + self.got[x].astype(F32)).astype(BF16)

    def far(self, side):
        x = rem4(self.r.x + 2)
        return remote(
            self.mid.at[x, pl.ds(16 * side, 16)], self.one.at[side],
            self.send.at[4 + side], self.recv.at[4 + side], self.r.near(2, 1 - 2 * side),
        )

    def late(self, side, summed):
        d = 1 - 2 * side
        x = rem4(self.r.x + d)
        half = side if summed else 1 - side
        j = 6 + side * 2 + summed
        return remote(
            self.mid.at[x, pl.ds(16 * half, 16)], self.two.at[side, pl.ds(16 * half, 16)],
            self.send.at[j], self.recv.at[j], self.r.near(2, d),
        )

    def middle(self):
        self.near_half()
        self.far_half()

    def near_half(self):
        self.pairsum(2)
        self.start(self.far(0))
        self.start(self.far(1))
        self.pairsum(1)
        self.start(self.late(0, 0))
        self.pairsum(3)
        self.start(self.late(1, 0))

    def far_half(self):
        for side in range(2):
            self.far(side).wait_recv()
            x = rem4(self.r.x + 1 - 2 * side)
            rows = pl.ds(16 * side, 16)
            self.mid[x, rows] = (self.mid[x, rows].astype(F32) + self.one[side].astype(F32)).astype(BF16)
            self.start(self.late(side, 1))

    def end(self):
        self.pair(0).wait_recv()
        for side in range(2):
            self.late(side, 0).wait_recv()
            self.late(side, 1).wait_recv()

    def result(self, rows):
        base = (self.r.c * 4 + self.r.x) * 32
        own = self.part[pl.ds(pl.multiple_of(base + rows.start, rows.size), rows.size)].astype(F32)
        own = own + self.got[self.r.x, rows].astype(F32)
        return own + self.two[0, rows].astype(F32) + self.two[1, rows].astype(F32)

    def drain(self):
        for copy in self.sent:
            copy.wait_send()
        self.sent = []


class CrossGather:
    def __init__(self, r, ref, both, send, recv):
        self.r, self.ref, self.both, self.send, self.recv, self.sent = r, ref, both, send, recv, []

    def start(self, copy):
        copy.start()
        self.sent.append(copy)

    def rows(self, d, part, sibling=False):
        c = 1 - self.r.c if sibling else self.r.c
        base = rem4(self.r.x + d) * 32
        if self.both:
            base = base + c * 128
        if part is None:
            return self.ref.at[pl.ds(pl.multiple_of(base, 32), 32)]
        return self.ref.at[pl.ds(pl.multiple_of(base + 16 * part, 16), 16)]

    def ring(self, d, part, to, i):
        ref = self.rows(d, part)
        return remote(ref, ref, self.send.at[i], self.recv.at[i], self.r.near(2, to))

    def pair(self, d, sibling=False):
        ref = self.rows(d, None, sibling)
        return remote(ref, ref, self.send.at[6 + d % 4], self.recv.at[6 + d % 4], self.r.sib)

    def begin(self):
        self.start(self.ring(0, 0, 1, 0))
        self.start(self.ring(0, 1, -1, 1))
        self.start(self.ring(0, 1, 1, 2))
        self.start(self.ring(0, 0, -1, 3))
        if self.both:
            self.start(self.pair(0))

    def middle(self):
        self.ring(-1, 0, 1, 0).wait_recv()
        self.start(self.ring(-1, 0, 1, 4))
        self.ring(1, 1, -1, 1).wait_recv()
        self.start(self.ring(1, 1, -1, 5))
        self.ring(-1, 1, 1, 2).wait_recv()
        self.ring(1, 0, -1, 3).wait_recv()
        if self.both:
            self.start(self.pair(-1))
            self.start(self.pair(1))

    def end(self):
        self.ring(-2, 0, 1, 4).wait_recv()
        self.ring(2, 1, -1, 5).wait_recv()
        if self.both:
            self.start(self.pair(2))
            for d in (0, -1, 1, 2):
                self.pair(d, True).wait_recv()

    def drain(self):
        for copy in self.sent:
            copy.wait_send()
        self.sent = []


class Refs:
    pass


SCRATCH = {
    "other": ((64, LANES_A + LANES_B), BF16),
    "tab": ((8, 16, 256), F32),
    "ga": ((4, 4, 128, LANES_A), BF16),
    "gb": ((4, 4, 128, LANES_B), BF16),
    "s0a": ((6, 2, 128, LANES_A), BF16),
    "s0b": ((6, 2, 128, LANES_B), BF16),
    "s1a": ((6, 64, LANES_A), BF16),
    "s1b": ((6, 64, LANES_B), BF16),
    "da": ((4, 4, 128, 384), BF16),
    "db": ((4, 4, 128, 384), BF16),
    "sib_a": ((64, LANES_A), BF16),
    "sib_b": ((64, LANES_B), BF16),
    "gains_y": ((4, 16, 128), F32),
    "gains_all": ((4, 4, 16, 128), F32),
    "gains": ((8, 2048), F32),
    "gain_in": ((8, 128), F32),
    "taps": ((8, 768), F32),
    "keep": ((256, 256), F32),
    "gy": ((256, 2048), BF16),
    "n1": ((272, 2048), BF16),
    "n2": ((256, 2048), BF16),
    "dh": ((256, 2048), BF16),
    "part": ((256, 2048), BF16),
    "mid": ((4, 32, 2048), BF16),
    "part_f": ((256, 2048), BF16),
    "mid_f": ((4, 32, 2048), BF16),
    "got": ((4, 4, 32, 2048), BF16),
    "one": ((4, 2, 16, 2048), BF16),
    "two": ((4, 2, 32, 2048), BF16),
    "bo": ((128, 2048), BF16),
    "gt": ((128, 2048), BF16),
    "h": ((32, 2048), F32),
    "dhf": ((32, 2048), F32),
    "p": ((272, 768), F32),
    "q0": ((256, 256), F32),
    "q1": ((256, 256), F32),
    "q2": ((256, 256), F32),
    "u": ((256, 256), F32),
    "v": ((256, 256), F32),
    "z": ((256, 256), BF16),
    "st_re": ((257, 16, 256), F32),
    "st_im": ((257, 16, 256), F32),
    "ends_y": ((4, 32, 256), F32),
    "ends_z": ((4, 32, 256), F32),
    "backs_y": ((4, 32, 256), F32),
    "backs_z": ((4, 32, 256), F32),
    "gu": ((256, 1408), F32),
    "act": ((256, 768), BF16),
    "dgu": ((256, 1408), BF16),
    "dv": ((256, 256), F32),
    "dq": ((264, 768), F32),
    "dp": ((256, 768), BF16),
    "small_y": ((4, 80, 256), BF16),
    "small_z": ((4, 80, 256), BF16),
    "small_sum": ((80, 256), F32),
    "small_sib": ((80, 256), F32),
    "ggain": ((8, 2048), F32),
    "gg_z": ((4, 8, 512), F32),
    "gg_1": ((8, 512), F32),
    "gg_y": ((4, 8, 128), F32),
    "gg_2": ((8, 128), F32),
    "gg_s": ((8, 128), F32),
    "gg_x": ((4, 8, 128), F32),
    "gg_out": ((8, 128), F32),
}
SEMS = {
    "w": (5, 2, 12), "w_sib": (5, 2), "gain_sib": (), "keep_s": (), "gy_s": (), "n1_s": (),
    "edge": (), "dq_s": (), "trade": (11, 3), "sum": (4, 10), "cg": (4, 10),
    "rs": (5, 2, 12), "rs_sib": (5, 2), "small_x": (), "gg_s": (),
}


def kernel(*refs):
    names = [
        "in_w", "out_w", "gate_w", "up_w", "down_w", "gain_1", "gain_2", "resets", "tok", "cot", "conv_w",
        "decay", "angle", "res_re", "res_im",
    ]
    outs = ["block_out", "grad_tok", "grad_w", "grad_small", "grad_gain"]
    k = Refs()
    for name, ref in zip(names + outs + list(SCRATCH), refs):
        setattr(k, name, ref)
    rest = refs[len(names) + len(outs) + len(SCRATCH):]
    S, R = {}, {}
    for i, name in enumerate(SEMS):
        S[name], R[name] = rest[2 * i], rest[2 * i + 1]
    local = rest[2 * len(SEMS)]
    r = Rings()
    g = (k.ga, k.gb)
    z, y, c, x = r.z, r.y, r.c, r.x

    barrier = pltpu.get_barrier_semaphore()
    peers = [r.sib] + [r.near(a, d) for a in range(3) for d in (1, 2, 3)] + [r.along(1), r.along(-1)]
    for peer in peers:
        pl.semaphore_signal(barrier, inc=1, device_id=peer, device_id_type=MESH)
    pl.semaphore_wait(barrier, len(peers))

    def lanes(n, h):
        o, w = CHUNKS[n][h]
        return pl.ds(o, w)

    def columns(n, start, stop):
        (oa, wa), (ob, _) = WHOLE[n]
        parts = []
        if start < wa:
            parts.append(g[0][:, :, :, oa + start:oa + min(stop, wa)])
        if stop > wa:
            parts.append(g[1][:, :, :, ob + max(start - wa, 0):ob + stop - wa])
        return jnp.concatenate([p.reshape(2048, p.shape[-1]) for p in parts], 1)

    def weight(n, h, i):
        o, w = WHOLE[n][h]
        return g[h][i, :, :, o:o + w].reshape(512, w)

    trades = []

    def trade(axis, src, land):
        i = len(trades)
        trades.append(Trade(r, axis, src if callable(src) else lambda _: src, land, S["trade"].at[i], R["trade"].at[i]))
        return trades[-1]

    my64 = span(c * 64, 64)
    my128 = span(c * 128, 128)
    gather = [
        Both([Gather(r, g[h], 128, 64, lanes(n, h), 1 - h, S["w"].at[n, h], R["w"].at[n, h]) for h in range(2)])
        for n in range(5)
    ]

    def put(cc, n, sink):
        wa = WHOLE[n][0][1]

        def store(start, value):
            stop = start + value.shape[1]
            if start < wa:
                sink(0, WHOLE[n][0][0] + start, value[:, :min(stop, wa) - start])
            if stop > wa:
                sink(1, WHOLE[n][1][0] + max(start - wa, 0), value[:, max(wa - start, 0):])

        def main(ref):
            return ref[:, pl.ds(pl.multiple_of(cc * 640, 128), 640)]

        def tail(ref):
            a = ref[:, 1280:1408].astype(F32)
            return jnp.where(cc == 0, a[:, 0:64], a[:, 64:128])

        channels = pl.ds(pl.multiple_of(cc * 256, 256), 256)
        if n == IN:
            for b in range(3):
                store(b * 256, k.in_w[b, :, channels])
        elif n == OUT:
            store(0, k.out_w[:, channels])
        elif n == GU:
            store(0, main(k.gate_w))
            store(640, main(k.up_w))
            store(1280, jnp.concatenate([tail(k.gate_w), tail(k.up_w)], 1).astype(BF16))
        else:
            store(0, main(k.down_w))
            store(640, jnp.concatenate([tail(k.down_w), jnp.zeros((64, 64), F32)], 1).astype(BF16))

    def to_other(h, at, value):
        at = at + (LANES_A if h else 0)
        k.other[:, at:at + value.shape[1]] = value

    def to_own(h, at, value):
        g[h][z, y, my64, at:at + value.shape[1]] = value

    def weight_sib(n, h):
        o, w = CHUNKS[n][h]
        return remote(
            k.other.at[:, pl.ds(o + (LANES_A if h else 0), w)], g[h].at[z, y, my64, lanes(n, h)],
            S["w_sib"].at[n, h], R["w_sib"].at[n, h], r.sib,
        )

    eight = span(c * 8, 8)
    side = lax.broadcasted_iota(jnp.int32, (1, 128), 1) // 64 == c
    for i, ref in enumerate((k.gain_1, k.gain_2)):
        a = ref[...].astype(F32)
        k.gain_in[i:i + 1, :] = jnp.where(side, jnp.concatenate([a, a], 1), 0.0)
    k.gain_in[2:8, :] = jnp.zeros((6, 128), F32)
    gain_sib = remote(k.gain_in, k.gains_y.at[y, eight], S["gain_sib"], R["gain_sib"], r.sib)
    gain_sib.start()
    k.gains_y[y, eight] = k.gain_in[...]
    for n in (IN, OUT, GU, DOWN):
        put(1 - c, n, to_other)
        for m in (GU, GU_2) if n == GU else (n,):
            for h in range(2):
                weight_sib(m, h).start()
        put(c, n, to_own)
    keep = 1.0 - k.resets[...].astype(F32)
    keep = jnp.broadcast_to(keep, (128, 128)).T
    k.keep[my128] = jnp.concatenate([keep, keep], 1)
    keep_sib = remote(k.keep.at[my128], k.keep.at[my128], S["keep_s"], R["keep_s"], r.sib)
    keep_sib.start()
    gy_sib = remote(k.cot, k.gy.at[my128], S["gy_s"], R["gy_s"], r.sib)
    k.gy[my128] = k.cot[...]

    channels = pl.ds(pl.multiple_of(c * 256, 256), 256)
    decay, angle = k.decay[:, channels], k.angle[:, channels]
    size = jnp.exp(-decay)
    gin = jnp.sqrt(-expm1(-2.0 * decay))
    power = (size * jnp.cos(angle), size * jnp.sin(angle))
    k.tab[0], k.tab[1] = power
    k.tab[2] = gin * k.res_re[:, channels]
    k.tab[3] = gin * k.res_im[:, channels]
    for _ in range(8):
        power = (power[0] * power[0] - power[1] * power[1], 2.0 * power[0] * power[1])
    k.tab[4], k.tab[5] = power
    k.tab[6] = gin
    k.tab[7] = size * size / gin
    for i in range(3):
        for b in range(3):
            k.taps[i:i + 1, b * 256:b * 256 + 256] = k.conv_w[i, b:b + 1, channels]

    def ag(n, i):
        if i == 1:
            for h in range(2):
                weight_sib(n, h).wait_recv()
        gather[n].step(i)

    tasks = {}

    def task(f):
        tasks[f.__name__] = f
        return f

    def at(point):
        for name, *rest in PLAN.get(point, ()):
            tasks[name](*rest)

    task(ag)
    at("start")
    gain_y = trade(1, k.gains_y.at[y], k.gains_y)
    gain_z = trade(0, k.gains_y, k.gains_all)
    gain_sib.wait_recv()
    gain_y.begin()
    at("gain_y")
    gain_y.end()
    gain_z.begin()
    k.gains_all[z] = k.gains_y[...]
    at("gain_z")
    gain_z.end()
    for i in range(16):
        k.gains[:, i * 128:(i + 1) * 128] = k.gains_all[i // 4, i % 4, 0:8] + k.gains_all[i // 4, i % 4, 8:16]

    def norm_one(i):
        rows = span(i * 16, 16)
        a = k.tok[rows, :].astype(F32)
        s = lax.rsqrt(jnp.mean(a * a, axis=-1, keepdims=True) + EPSILON)
        k.n1[pl.ds(pl.multiple_of(16 + c * 128 + i * 16, 16), 16), :] = (a * s * k.gains[0:1, :]).astype(BF16)
    loop(8, norm_one)

    def n1_rows(c):
        return k.n1.at[pl.ds(pl.multiple_of(16 + c * 128, 16), 128)]

    n1_sib = remote(n1_rows(c), n1_rows(c), S["n1_s"], R["n1_s"], r.sib)
    n1_sib.start()
    at("n1")
    k_other = span((1 - c) * 128, 128)
    remote(n1_rows(1 - c), n1_rows(1 - c), S["n1_s"], R["n1_s"], r.sib).wait_recv()
    edge = remote(k.n1.at[256:272], k.n1.at[0:16], S["edge"], R["edge"], r.along(1))
    edge.start()
    gy_sib.start()
    at("edge")

    edge.wait_recv()
    at("project")

    def project(_):
        for o in range(0, 768, 256):
            k.p[:, o:o + 256] = nn(k.n1[...], columns(IN, o, o + 256))
    loop(1, project)

    def round_p(i):
        rows = span(i * 16, 16)
        k.p[rows, :] = k.p[rows, :].astype(BF16).astype(F32)
    loop(17, round_p)
    remote(k.keep.at[k_other], k.keep.at[k_other], S["keep_s"], R["keep_s"], r.sib).wait_recv()
    at("short")

    def masks(i):
        rows = span(i * 16, 16)
        near = k.keep[rows, :]
        before = k.keep[span(jnp.maximum(i * 16 - 8, 0), 8), :]
        first = jnp.where(i == 0, 1.0, before[7:8, :])
        shifted = jnp.concatenate([first, near[0:15, :]], 0)
        return near, near * shifted

    def short(i):
        near, far = masks(i)
        ext = k.p[pl.ds(pl.multiple_of(i * 16 + 8, 8), 24), :]
        q = []
        for b in range(3):
            l = slice(b * 256, b * 256 + 256)
            e = ext[:, l]
            q.append(
                k.taps[0:1, l] * e[8:24] + near * k.taps[1:2, l] * e[7:23] + far * k.taps[2:3, l] * e[6:22]
            )
        rows = span(i * 16, 16)
        k.q0[rows, :] = q[0]
        k.q1[rows, :] = q[1]
        k.q2[rows, :] = q[2]
        k.u[rows, :] = q[1] * q[2]
    loop(16, short)

    zero = jnp.zeros((16, 256), F32)
    lr, li, cr, ci, pr, pi = (k.tab[i] for i in range(6))

    def advance(re, im, u, keep):
        kr, ki = keep * re, keep * im
        return lr * kr - li * ki + u, lr * ki + li * kr

    def end_state(i, state):
        rows = span(i * 8, 8)
        u, keep = k.u[rows, :], k.keep[rows, :]
        for j in range(8):
            state = advance(*state, u[j:j + 1, :], keep[j:j + 1, :])
        return state

    def times(a, b, g, h):
        return a * g - b * h, a * h + b * g

    def chain(own, ref_y, ref_z, sign, between):
        order = range(4) if sign > 0 else range(3, -1, -1)
        qr, qi = pr, sign * pi

        def put(ref, at, state):
            ref[at, 0:16] = state[0]
            ref[at, 16:32] = state[1]

        def horner(ref, wr, wi, state, here, every):
            for i in order:
                nr, ni = times(wr, wi, *state)
                nr, ni = nr + ref[i, 0:16], ni + ref[i, 16:32]
                use = (i < here) if sign > 0 else (i > here)
                state = (nr, ni) if every else (jnp.where(use, nr, state[0]), jnp.where(use, ni, state[1]))
            return state

        put(ref_y, y, own)
        t = trade(1, ref_y.at[y], ref_y)
        t.begin()
        at(between[0])
        t.end()
        put(ref_z, z, horner(ref_y, qr, qi, (zero, zero), y, True))
        t = trade(0, ref_z.at[z], ref_z)
        t.begin()
        at(between[1])
        t.end()
        w = times(*times(qr, qi, qr, qi), *times(qr, qi, qr, qi))
        return horner(ref_y, qr, qi, horner(ref_z, *w, (zero, zero), z, False), y, False)

    end = fold(32, end_state, (zero, zero))
    enter = chain(end, k.ends_y, k.ends_z, 1, ("ends_y", "ends_z"))
    k.st_re[0] = enter[0]
    k.st_im[0] = enter[1]
    at("scan")

    def scan(i, state):
        rows = span(i * 8, 8)
        u, keep = k.u[rows, :], k.keep[rows, :]
        for j in range(8):
            state = advance(*state, u[j:j + 1, :], keep[j:j + 1, :])
            k.st_re[i * 8 + j + 1] = state[0]
            k.st_im[i * 8 + j + 1] = state[1]
            k.v[pl.ds(i * 8 + j, 1), :] = jnp.sum(cr * state[0] - ci * state[1], axis=0, keepdims=True)
        return state
    fold(32, scan, enter)

    def gated(i):
        rows = span(i * 32, 32)
        k.z[rows, :] = (k.q0[rows, :] * k.v[rows, :]).astype(BF16)
    loop(8, gated)

    at("mix")
    def out_weight(i):
        return jnp.concatenate([weight(OUT, 0, i), weight(OUT, 1, i)], 1)

    def mix(i):
        k.part[:, span(i * 512, 512)] = nt(k.z[...], out_weight(i)).astype(BF16)
    loop(4, mix)

    def cross(i):
        part, mid = (k.part_f, k.mid_f) if i == 1 else (k.part, k.mid)
        return CrossSum(r, part, k.got.at[i], mid, k.one.at[i], k.two.at[i], S["sum"].at[i], R["sum"].at[i])

    s_mix = cross(0)
    s_mix.begin()
    at("mix_0")
    s_mix.near_half()
    at("mix_1")
    s_mix.far_half()
    at("mix_2")
    s_mix.end()

    own = (c * 4 + x) * 32

    def norm_two(i):
        rows = pl.ds(pl.multiple_of(i * 16, 16), 16)
        a = k.tok[pl.ds(pl.multiple_of(x * 32 + i * 16, 16), 16), :].astype(F32) + s_mix.result(rows)
        k.h[rows, :] = a
        s = lax.rsqrt(jnp.mean(a * a, axis=-1, keepdims=True) + EPSILON)
        k.n2[pl.ds(pl.multiple_of(own + i * 16, 16), 16), :] = (a * s * k.gains[1:2, :]).astype(BF16)
    loop(2, norm_two)
    g_n2 = CrossGather(r, k.n2, True, S["cg"].at[0], R["cg"].at[0])
    g_n2.begin()
    at("n2_0")
    g_n2.middle()
    at("n2_1")
    g_n2.end()
    s_mix.drain()
    at("ff")

    def gate_up(_):
        for o in range(0, 1408, 256):
            e = min(o + 256, 1408)
            k.gu[:, o:e] = nn(k.n2[...], columns(GU, o, e))
    loop(1, gate_up)
    def halves(t):
        last = t[:, 1280:1408]
        turned = jnp.concatenate([last[:, 64:128], last[:, 0:64]], 1)
        return jnp.concatenate([t[:, 0:640], last], 1), jnp.concatenate([t[:, 640:1280], turned], 1)

    used = lax.broadcasted_iota(jnp.int32, (1, 768), 1) < 704

    def activate(i):
        rows = span(i * 16, 16)
        gate, up = halves(k.gu[rows, :])
        k.act[rows, :] = jnp.where(used, gate * jax.nn.sigmoid(gate) * up, 0.0).astype(BF16)
    loop(16, activate)

    def down_weight(i):
        return jnp.concatenate([weight(DOWN, 0, i), weight(DOWN, 1, i)], 1)

    s_ffn = cross(1)
    g_bo = CrossGather(r, k.bo, False, S["cg"].at[1], R["cg"].at[1])
    out_bo = pltpu.make_async_copy(k.bo, k.block_out, local.at[0])

    @task
    def ffn_0():
        def ffn(i):
            k.part_f[:, span(i * 512, 512)] = nt(k.act[...], down_weight(i)).astype(BF16)
        loop(4, ffn)
        s_ffn.begin()

    @task
    def ffn_1():
        s_ffn.near_half()

    @task
    def ffn_2():
        s_ffn.far_half()

    @task
    def ffn_3():
        s_ffn.end()

        def top(i):
            rows = pl.ds(pl.multiple_of(i * 16, 16), 16)
            here = pl.ds(pl.multiple_of(x * 32 + i * 16, 16), 16)
            k.bo[here, :] = (k.h[rows, :] + s_ffn.result(rows)).astype(BF16)
        loop(2, top)
        s_ffn.drain()
        g_bo.begin()

    @task
    def ffn_4():
        g_bo.middle()

    @task
    def ffn_5():
        g_bo.end()
        out_bo.start()

    d_refs = (k.da, k.db)
    scatter = []
    for n in range(5):
        scatter.append([])
        for h in range(2):
            ref, here = (d_refs[h], pl.ds(0, 384)) if n == DOWN else (g[h], lanes(n, h))
            bufs = ((k.s0a, k.s1a), (k.s0b, k.s1b))[h]
            scatter[n].append(Scatter(r, ref, here, lanes(n, h), h, bufs, S["rs"].at[n, h], R["rs"].at[n, h]))
    sib_bufs = (k.sib_a, k.sib_b)

    def rs_sib(n, h):
        s = scatter[n][h]
        return remote(
            s.ref.at[z, y, span((1 - c) * 64, 64), s.lanes], sib_bufs[h].at[:, s.at],
            S["rs_sib"].at[n, h], R["rs_sib"].at[n, h], r.sib,
        )

    @task
    def rs(n, i):
        for h in range(2):
            s = scatter[n][h]
            if i == 0:
                s.far(0)
            elif i == 1:
                s.early(0)
            elif i == 2:
                s.forward(0)
            elif i == 3:
                s.finish(0)
                s.far(1)
                s.early(1)
            elif i == 4:
                s.forward(1)
            elif i == 5:
                s.finish(1)
                rs_sib(n, h).start()

    @task
    def wg(n):
        a, b, first = {
            IN: (k.n1, k.dp, 16), OUT: (k.dh, k.z, 0), GU: (k.n2, k.dgu, 0), DOWN: (k.gy, k.act, 0)
        }[n]
        if n == GU:
            gather[GU_2].drain()
        if n != DOWN:
            gather[n].drain()
        (oa, wa), (ob, wb) = ((0, 384), (0, 384)) if n == DOWN else WHOLE[n]
        into = d_refs if n == DOWN else g

        def weight_grad(i):
            t = tn(a[pl.ds(first, 256), pl.ds(pl.multiple_of(i * 512, 512), 512)], b[...]).astype(BF16)
            into[0][i, :, :, oa:oa + wa] = t[:, 0:wa].reshape(4, 128, wa)
            into[1][i, :, :, ob:ob + wb] = t[:, wa:wa + wb].reshape(4, 128, wb)
        weight_grad.width = wa + wb
        loop(4, weight_grad)

    remote(k.gy.at[k_other], k.gy.at[k_other], S["gy_s"], R["gy_s"], r.sib).wait_recv()
    at("act")

    def d_act(_):
        for o in range(0, 768, 256):
            k.dq[0:256, o:o + 256] = nn(k.gy[...], columns(DOWN, o, o + 256))
    loop(1, d_act)
    at("da")

    def d_gates(i):
        rows = span(i * 16, 16)
        gate, up = halves(k.gu[rows, :])
        da = k.dq[rows, :]
        sg = jax.nn.sigmoid(gate)
        dgate = da * up * sg * (1.0 + gate * (1.0 - sg))
        dup = da * (gate * sg)
        last = jnp.concatenate([dgate[:, 640:704], dup[:, 640:704]], 1)
        k.dgu[rows, :] = jnp.concatenate([dgate[:, 0:640], dup[:, 0:640], last], 1).astype(BF16)
    loop(16, d_gates)

    def d_n2(i):
        w = jnp.concatenate([weight(GU, 0, i), weight(GU, 1, i)], 1)
        k.part[:, span(i * 512, 512)] = nt(k.dgu[...], w).astype(BF16)
    loop(4, d_n2)
    s_dn2 = cross(2)
    s_dn2.begin()
    at("dn2_0")
    s_dn2.near_half()
    at("dn2_1")
    s_dn2.far_half()
    at("dn2_2")
    s_dn2.end()

    def d_norm_two(i):
        rows = pl.ds(pl.multiple_of(i * 16, 16), 16)
        a = k.h[rows, :]
        s = lax.rsqrt(jnp.mean(a * a, axis=-1, keepdims=True) + EPSILON)
        hat = a * s
        dn = s_dn2.result(rows)
        dng = dn * k.gains[1:2, :]
        gy = k.gy[pl.ds(pl.multiple_of(own + i * 16, 16), 16), :].astype(F32)
        dh = gy + s * (dng - hat * jnp.mean(dng * hat, axis=-1, keepdims=True))
        k.dhf[rows, :] = dh
        k.dh[pl.ds(pl.multiple_of(own + i * 16, 16), 16), :] = dh.astype(BF16)
        t = jnp.sum(dn * hat, axis=0, keepdims=True)

        @pl.when(i == 0)
        def _():
            k.ggain[...] = jnp.zeros((8, 2048), F32)
            k.ggain[1:2, :] = t

        @pl.when(i > 0)
        def _():
            k.ggain[1:2, :] += t
    loop(2, d_norm_two)
    s_dn2.drain()
    g_dh = CrossGather(r, k.dh, True, S["cg"].at[2], R["cg"].at[2])
    g_dh.begin()
    at("dh_0")
    g_dh.middle()
    at("dh_1")
    g_dh.end()
    at("dz")

    def d_z(_):
        k.dv[...] = nn(k.dh[...], columns(OUT, 0, 256))
    loop(1, d_z)

    def d_gated(i):
        rows = span(i * 32, 32)
        dz = k.dv[rows, :]
        k.dq[rows, 0:256] = dz * k.v[rows, :]
        k.dv[rows, :] = dz * k.q0[rows, :]
    loop(8, d_gated)

    def retreat(a, b, keep):
        ka, kb = keep * a, keep * b
        return ka, kb, lr * ka + li * kb, lr * kb - li * ka

    def start_state(i, state):
        rows = span((31 - i) * 8, 8)
        dv, keep = k.dv[rows, :], k.keep[rows, :]
        for j in reversed(range(8)):
            a = cr * dv[j:j + 1, :] + state[0]
            b = state[1] - ci * dv[j:j + 1, :]
            _, _, pa, pb = retreat(a, b, keep[j:j + 1, :])
            state = (pa, pb)
        return state

    begin = fold(32, start_state, (zero, zero))
    arrive = chain(begin, k.backs_y, k.backs_z, -1, ("backs_y", "backs_z"))
    at("adjoint")

    def adjoint(i, carry):
        rows = span((31 - i) * 8, 8)
        dv, keep = k.dv[rows, :], k.keep[rows, :]
        for j in reversed(range(8)):
            t = (31 - i) * 8 + j
            d = dv[j:j + 1, :]
            a = cr * d + carry[0]
            b = carry[1] - ci * d
            k.u[pl.ds(t, 1), :] = jnp.sum(a, axis=0, keepdims=True)
            _, _, pa, pb = retreat(a, b, keep[j:j + 1, :])
            carry = (pa, pb)
        return carry

    fold(32, adjoint, arrive)

    def d_poles(i, carry):
        pa, pb, dcr, dci, dlr, dli = carry
        rows = span((31 - i) * 8, 8)
        dv, keep = k.dv[rows, :], k.keep[rows, :]
        for j in reversed(range(8)):
            t = (31 - i) * 8 + j
            d = dv[j:j + 1, :]
            a = cr * d + pa
            b = pb - ci * d
            dcr = dcr + d * k.st_re[t + 1]
            dci = dci - d * k.st_im[t + 1]
            ka, kb, pa, pb = retreat(a, b, keep[j:j + 1, :])
            sr, si = k.st_re[t], k.st_im[t]
            dlr = dlr + ka * sr + kb * si
            dli = dli + kb * sr - ka * si
        return pa, pb, dcr, dci, dlr, dli

    def d_branches(i):
        rows = span(i * 32, 32)
        du = k.u[rows, :]
        k.dq[rows, 256:512] = du * k.q2[rows, :]
        k.dq[rows, 512:768] = du * k.q1[rows, :]
    loop(8, d_branches)
    dq_next = remote(k.dq.at[0:8], k.dq.at[256:264], S["dq_s"], R["dq_s"], r.along(-1))
    dq_next.start()
    at("dq")
    dq_next.wait()

    last = jnp.where(r.chip < 15, 1.0, 0.0)

    def d_short(i, taps):
        d = k.dq[pl.ds(pl.multiple_of(i * 16, 16), 24), :]
        near, far = masks(i)
        j = jnp.minimum(i * 16 + 16, 248)
        after = k.keep[span(j, 8), :]
        inside = i < 15
        tail_near = jnp.where(inside, after, last)
        tail_far = jnp.where(
            inside, after * jnp.concatenate([near[15:16, :], after[0:7, :]], 0), last
        )
        near = jnp.concatenate([near, tail_near], 0)
        far = jnp.concatenate([far, tail_far], 0)
        ext = k.p[pl.ds(pl.multiple_of(i * 16 + 8, 8), 24), :]
        rows = span(i * 16, 16)
        new = []
        for b in range(3):
            l = slice(b * 256, b * 256 + 256)
            e, db = ext[:, l], d[:, l]
            dn, df = near * db, far * db
            k.dp[rows, l] = (
                k.taps[0:1, l] * db[0:16] + k.taps[1:2, l] * dn[1:17] + k.taps[2:3, l] * df[2:18]
            ).astype(BF16)
            new.append(taps[3 * 0 + b] + jnp.sum(e[8:24] * db[0:16], axis=0, keepdims=True))
            new.append(taps[3 * 1 + b] + jnp.sum(e[7:23] * dn[0:16], axis=0, keepdims=True))
            new.append(taps[3 * 2 + b] + jnp.sum(e[6:22] * df[0:16], axis=0, keepdims=True))
        return tuple(new[3 * b + t] for t in range(3) for b in range(3))

    line = jnp.zeros((1, 256), F32)
    dtaps = fold(16, d_short, (line,) * 9)

    def d_n1(i):
        w = jnp.concatenate([weight(IN, 0, i), weight(IN, 1, i)], 1)
        k.part[:, span(i * 512, 512)] = nt(k.dp[...], w).astype(BF16)
    loop(4, d_n1)
    s_dn1 = cross(3)
    s_dn1.begin()
    at("dn1_0")

    small_1 = trade(1, k.small_y.at[y], k.small_y)
    small_2 = trade(0, k.small_z.at[z], k.small_z)

    def small_total(ref):
        return sum(ref[j].astype(F32) for j in range(4))

    small_x = remote(k.small_sum, k.small_sib, S["small_x"], R["small_x"], r.sib)

    @task
    def small(i):
        if i == 0:
            _, _, *dpoles = fold(32, d_poles, (*arrive, zero, zero, zero, zero))
            for j in range(4):
                k.small_y[y, 16 * j:16 * j + 16] = dpoles[j].astype(BF16)
            k.small_y[y, 64:80] = jnp.concatenate(list(dtaps) + [jnp.zeros((7, 256), F32)], 0).astype(BF16)
            small_1.begin()
        elif i == 1:
            small_1.end()
            k.small_z[z] = small_total(k.small_y).astype(BF16)
            small_2.begin()
        else:
            small_2.end()
            k.small_sum[...] = small_total(k.small_z)
            dcr, dci, dlr, dli = (k.small_sum[16 * j:16 * j + 16, :] for j in range(4))
            dgin = k.res_re[:, channels] * dcr + k.res_im[:, channels] * dci
            k.small_sum[0:16, :] = dgin * k.tab[7] - (lr * dlr + li * dli)
            k.small_sum[16:32, :] = lr * dli - li * dlr
            k.small_sum[32:48, :] = k.tab[6] * dcr
            k.small_sum[48:64, :] = k.tab[6] * dci
            small_x.start()

    at("dn1_x")
    s_dn1.near_half()
    at("dn1_1")
    s_dn1.far_half()
    at("dn1_2")
    s_dn1.end()

    def d_norm_one(i):
        rows = pl.ds(pl.multiple_of(i * 16, 16), 16)
        here = pl.ds(pl.multiple_of(x * 32 + i * 16, 16), 16)
        a = k.tok[here, :].astype(F32)
        s = lax.rsqrt(jnp.mean(a * a, axis=-1, keepdims=True) + EPSILON)
        hat = a * s
        dn = s_dn1.result(rows)
        dng = dn * k.gains[0:1, :]
        k.gt[here, :] = (
            k.dhf[rows, :] + s * (dng - hat * jnp.mean(dng * hat, axis=-1, keepdims=True))
        ).astype(BF16)
        t = jnp.sum(dn * hat, axis=0, keepdims=True)

        @pl.when(i == 0)
        def _():
            k.ggain[0:1, :] = t

        @pl.when(i > 0)
        def _():
            k.ggain[0:1, :] += t
    loop(2, d_norm_one)
    g_gt = CrossGather(r, k.gt, False, S["cg"].at[3], R["cg"].at[3])
    g_gt.begin()

    def piece(ref, width):
        return lambda i: ref.at[:, pl.ds(pl.multiple_of(i * width, width), width)]

    gg_1 = trade(0, piece(k.ggain, 512), k.gg_z)
    gg_2 = trade(1, piece(k.gg_1, 128), k.gg_y)
    gg_3 = trade(2, k.gg_s, k.gg_x)
    gg_sib = remote(k.gg_2, k.gg_s, S["gg_s"], R["gg_s"], r.sib)
    gg_1.begin()
    k.gg_z[z] = k.ggain[:, span(z * 512, 512)]
    at("gt_0")
    gg_1.end()
    k.gg_1[...] = sum(k.gg_z[j] for j in range(4))
    gg_2.begin()
    k.gg_y[y] = k.gg_1[:, span(y * 128, 128)]
    at("gt_1")
    g_gt.middle()
    at("gt_2")
    gg_2.end()
    k.gg_2[...] = sum(k.gg_y[j] for j in range(4))
    gg_sib.start()
    at("gt_3")
    gg_sib.wait()
    k.gg_s[...] = k.gg_s[...] + k.gg_2[...]
    gg_3.begin()
    k.gg_x[x] = k.gg_s[...]
    g_gt.end()
    out_gt = pltpu.make_async_copy(k.gt, k.grad_tok, local.at[1])
    out_gt.start()
    at("gt_4")
    small_x.wait()
    gg_3.end()
    k.gg_out[...] = sum(k.gg_x[j] for j in range(4))

    copies = [out_bo, out_gt]
    for j, src in enumerate((k.small_sum, k.small_sib)):
        copies.append(pltpu.make_async_copy(src, k.grad_small.at[j], local.at[2 + j]))
    copies.append(pltpu.make_async_copy(k.gg_out, k.grad_gain, local.at[4]))
    for n in range(5):
        for h in range(2):
            rs_sib(n, h).wait()
    for h in range(2):
        o, w = (0, 1280) if h == 0 else (LANES_A, 1152)
        end = o + w
        down, wide = pl.ds(end, 384), pl.ds(o, w)
        copies.append(pltpu.make_async_copy(g[h].at[z, y, my64, pl.ds(0, w)], k.grad_w.at[0, :, wide], local.at[5 + 3 * h]))
        copies.append(pltpu.make_async_copy(d_refs[h].at[z, y, my64], k.grad_w.at[0, :, down], local.at[6 + 3 * h]))
        copies.append(pltpu.make_async_copy(sib_bufs[h], k.grad_w.at[1, :, pl.ds(o, w + 384)], local.at[7 + 3 * h]))
    for copy in copies[2:]:
        copy.start()
    for copy in copies:
        copy.wait()
    for n in range(5):
        gather[n].drain()
        for h in range(2):
            weight_sib(n, h).wait_send()
            scatter[n][h].drain()
    for copy in (gain_sib, keep_sib, gy_sib, n1_sib, edge):
        copy.wait_send()
    for group in trades + [s_dn1, g_n2, g_bo, g_dh, g_gt]:
        group.drain()


def block(*arrays):
    sems = []
    for shape in SEMS.values():
        sems += [pltpu.SemaphoreType.DMA(shape)] * 2
    vmem = pl.BlockSpec(memory_space=pltpu.VMEM)
    return pl.pallas_call(
        kernel,
        out_shape=(
            jax.ShapeDtypeStruct((128, 2048), BF16),
            jax.ShapeDtypeStruct((128, 2048), BF16),
            jax.ShapeDtypeStruct((2, 64, LANES_A + LANES_B), BF16),
            jax.ShapeDtypeStruct((2, 80, 256), F32),
            jax.ShapeDtypeStruct((8, 128), F32),
        ),
        in_specs=[vmem] * len(arrays),
        out_specs=[pl.BlockSpec(memory_space=pl.ANY)] * 5,
        scratch_shapes=[pltpu.VMEM(s, t) for s, t in SCRATCH.values()] + sems + [pltpu.SemaphoreType.DMA((11,))],
        compiler_params=pltpu.CompilerParams(
            collective_id=0, has_side_effects=True, vmem_limit_bytes=63 * 2**20
        ),
        name="block",
    )(*arrays)


def results(*refs):
    sources, refs = refs[:5], refs[5:]
    (bo, gt, g_gain_1, g_in, g_taps, g_decay, g_angle, g_re, g_im, g_out, g_gain_2, g_gate, g_up, g_down) = refs[:14]
    grad_w, small, gain, sems = refs[14:]
    c = lax.rem(lax.axis_index("seq"), 2)
    copies = [
        pltpu.make_async_copy(source, ref, sems.at[i])
        for i, (source, ref) in enumerate(zip(sources, (bo, gt, grad_w, small, gain)))
    ]
    for copy in copies:
        copy.start()
    for copy in copies[::-1]:
        copy.wait()

    def cols(core, n, start, stop):
        wa = WHOLE[n][0][1]
        parts = []
        if start < wa:
            parts.append(grad_w[core, :, WHOLE[n][0][0] + start:WHOLE[n][0][0] + min(stop, wa)])
        if stop > wa:
            o = LANES_A + WHOLE[n][1][0]
            parts.append(grad_w[core, :, o + max(start - wa, 0):o + stop - wa])
        return jnp.concatenate(parts, 1).astype(F32)

    for at, core in ((0, c), (1, 1 - c)):
        for b in range(3):
            g_in[b, :, at * 256:at * 256 + 256] = cols(core, IN, b * 256, b * 256 + 256)
        g_out[:, at * 256:at * 256 + 256] = cols(core, OUT, 0, 256)
        g_gate[:, at * 640:at * 640 + 640] = cols(core, GU, 0, 640)
        g_up[:, at * 640:at * 640 + 640] = cols(core, GU, 640, 1280)
        g_down[:, at * 640:at * 640 + 640] = cols(core, DOWN, 0, 640)
        here = slice(at * 256, at * 256 + 256)
        for i, ref in enumerate((g_decay, g_angle, g_re, g_im)):
            ref[:, here] = small[core, 16 * i:16 * i + 16, :]
        for i in range(3):
            g_taps[i, :, here] = small[core, 64 + 3 * i:67 + 3 * i, :]
    first, second = cols(c, GU, 1280, 1408), cols(1 - c, GU, 1280, 1408)
    g_gate[:, 1280:1408] = jnp.concatenate([first[:, 0:64], second[:, 0:64]], 1)
    g_up[:, 1280:1408] = jnp.concatenate([first[:, 64:128], second[:, 64:128]], 1)
    first, second = cols(c, DOWN, 640, 768), cols(1 - c, DOWN, 640, 768)
    g_down[:, 1280:1408] = jnp.concatenate([first[:, 0:64], second[:, 0:64]], 1)
    for i, ref in enumerate((g_gain_1, g_gain_2)):
        a = gain[i:i + 1, :]
        ref[...] = jnp.where(c == 0, a[:, 0:64], a[:, 64:128])


def on_device(
    tokens, cotangent, resets, norm1_gain, in_weight, conv_weight, pole_decay, pole_angle, residue_re, residue_im,
    out_weight, norm2_gain, gate_weight, up_weight, down_weight,
):
    raw = block(
        in_weight.transpose(1, 0, 2), out_weight, gate_weight, up_weight, down_weight, norm1_gain.reshape(1, 64),
        norm2_gain.reshape(1, 64), resets.reshape(1, 128), tokens, cotangent, conv_weight, pole_decay, pole_angle,
        residue_re, residue_im,
    )
    vmem = pl.BlockSpec(memory_space=pltpu.VMEM)
    shapes = [
        ((128, 2048), BF16), ((128, 2048), BF16), ((1, 64), F32), ((3, 64, 512), F32), ((3, 3, 512), F32),
        ((16, 512), F32), ((16, 512), F32), ((16, 512), F32), ((16, 512), F32), ((64, 512), F32), ((1, 64), F32),
        ((64, 1408), F32), ((64, 1408), F32), ((64, 1408), F32),
    ]
    outs = list(pl.pallas_call(
        results,
        out_shape=[jax.ShapeDtypeStruct(s, t) for s, t in shapes],
        in_specs=[pl.BlockSpec(memory_space=pl.ANY)] * len(raw),
        out_specs=[vmem] * len(shapes),
        scratch_shapes=[pltpu.VMEM(a.shape, a.dtype) for a in raw[2:]] + [pltpu.SemaphoreType.DMA((5,))],
        compiler_params=pltpu.CompilerParams(vmem_limit_bytes=60 * 2**20),
        name="results",
    )(*raw))
    outs[2], outs[10] = outs[2].reshape(64), outs[10].reshape(64)
    outs[3] = outs[3].transpose(1, 0, 2)
    return tuple(outs)


def solution(mesh):
    row, cols = P("seq", "mp"), P(None, "mp")
    return jax.shard_map(
        on_device,
        mesh=mesh,
        in_specs=(
            P("seq", None), P("seq", None), P("seq"), P("seq"), P("seq", None, "mp"), P(None, None, "mp"),
            cols, cols, cols, cols, row, P("seq"), row, row, row,
        ),
        out_specs=(
            P("seq", None), P("seq", None), P("seq"), P("seq", None, "mp"), P(None, None, "mp"),
            cols, cols, cols, cols, row, P("seq"), row, row, row,
        ),
        check_vma=False,
    )
```

```python
import functools

import jax
import jax.numpy as jnp
from jax import lax
from jax.experimental import pallas as pl
from jax.experimental.pallas import tpu as pltpu
from jax.sharding import PartitionSpec as P

EPSILON = 1e-05
BF16, F32 = jnp.bfloat16, jnp.float32
MESH = pl.DeviceIdType.MESH
LANES_A, LANES_B = 1664, 1536
CHUNKS = (
    ((0, 128), (0, 128)),
    ((128, 256), (128, 256)),
    ((384, 128), (384, 128)),
    ((512, 384), (512, 384)),
    ((896, 384), (896, 256)),
    ((1280, 384), (1152, 384)),
)
IN, IN_2, OUT, GU, GU_2, DOWN = range(6)
def pieces(a, b, last=False):
    both = [(0, 0, *a, 0, 128), (1, 1, *b, 0, 128)]
    return both + [(0, 0, 1536, 128, 0, 64), (1, 0, 1536, 128, 64, 64)] * last


GATHERS = (
    (0, False, pieces((0, 384), (0, 384))),
    (0, False, pieces((384, 1152), (384, 1152), True)),
    (1, True, pieces((0, 384), (0, 384))),
    (1, False, pieces((384, 128), (384, 128))),
    (1, True, pieces((512, 384), (512, 384))),
    (1, True, pieces((896, 384), (896, 256))),
    (1, True, pieces((1280, 256), (1152, 384), True)),
)
A_IN, A_REST, B_IN, B_OUT, B_GU, B_GU_2, B_DOWN = range(7)
SECOND = (CHUNKS[0], CHUNKS[1], CHUNKS[2], ((512, 768), (512, 640)), CHUNKS[5])
SCATTERS = [pieces(*parts) for parts in CHUNKS[:5] + SECOND[:4]]
SCATTERS = SCATTERS[:5] + [pieces((1280, 256), (1152, 384), True)] + SCATTERS[5:] + [pieces((1280, 256), (1152, 384), True)]
S_IN, S_IN_2, S_OUT, S_GU, S_DOWN = range(6, 11)
WHOLE = {n: CHUNKS[n] for n in (IN, IN_2, OUT, DOWN)} | {GU: ((512, 768), (512, 640))}


def where():
    place = lax.axis_index("seq")
    chip = place // 2
    return chip // 4, lax.rem(chip, 4), lax.rem(place, 2), lax.axis_index("mp")


def device(z, y, c, x):
    return ((z * 4 + y) * 2 + c, x)


def rem4(a):
    return lax.rem(a + 4, 4)


def remote(src, dst, send, recv, to):
    return pltpu.make_async_remote_copy(
        src_ref=src, dst_ref=dst, send_sem=send, recv_sem=recv, device_id=to, device_id_type=MESH
    )


def waiting(ref, sem):
    return remote(ref, ref, sem, sem, device(0, 0, 0, 0))


def nn(a, b):
    return jnp.dot(a, b, preferred_element_type=F32)


def nt(a, b):
    return lax.dot_general(a, b, (((1,), (1,)), ((), ())), preferred_element_type=F32)


def tn(a, b):
    return lax.dot_general(a, b, (((0,), (0,)), ((), ())), preferred_element_type=F32)


def expm1(x):
    series = x / 8.0 + 1.0
    for n in range(7, 1, -1):
        series = series * (x / n) + 1.0
    return jnp.where(jnp.abs(x) < 0.25, x * series, jnp.exp(x) - 1.0)


def fold(count, body, state):
    return lax.fori_loop(0, count, body, state)


def loop(count, body):
    lax.fori_loop(0, count, lambda i, _: (body(i), 0)[1], 0)


def span(start, size):
    return pl.ds(pl.multiple_of(start, size), size)


(
    START, GAIN_Y, GAIN_Z, NORM_1, EDGE, PROJECT, SHORT, ENDS_Y,
    ENDS_Z, SCAN, MIX, MIX_0, MIX_1, MIX_2, N2_0, N2_1,
    FF, ACT, DA, DN2_0, DN2_1, DN2_2, DH_0, DH_1,
    DZ, BACKS_Y, BACKS_Z, ADJOINT, DQ, DN1_0, DN1_X, DN1_1,
    DN1_2, GT_0, GT_1, GT_2, GT_3, GT_4,
) = range(38)
AG, RS, WG, FFN, SMALL, SHORT_1 = range(6)
PLAN = {
    START: ((AG, A_IN, 1),),
    GAIN_Y: ((AG, A_REST, 1),),
    GAIN_Z: ((AG, A_IN, 3), (AG, A_REST, 3), (AG, A_IN, 4), (AG, B_IN, 1), (AG, B_IN, 2), (AG, A_REST, 4),),
    NORM_1: ((AG, B_IN, 3),),
    EDGE: ((AG, B_GU_2, 1), (AG, B_IN, 4), (AG, B_OUT, 1),),
    ENDS_Y: ((AG, B_GU_2, 2), (AG, B_OUT, 3),),
    ENDS_Z: ((AG, B_GU, 1), (AG, B_DOWN, 1), (AG, B_GU, 2), (AG, B_OUT, 4),),
    MIX_1: ((AG, B_GU, 3),),
    MIX_2: ((AG, B_GU_2, 3),),
    N2_0: ((AG, B_DOWN, 2),),
    N2_1: ((AG, B_DOWN, 3), (AG, B_GU, 4), (AG, B_GU_2, 4),),
    ACT: ((WG, DOWN), (RS, DOWN, 0), (AG, B_DOWN, 4),),
    DA: ((RS, DOWN, 1),),
    DN2_1: ((RS, DOWN, 2), (WG, GU), (RS, GU, 0), (RS, GU_2, 0),),
    DH_0: ((RS, GU, 1), (RS, GU_2, 1),),
    BACKS_Y: ((RS, GU, 2), (RS, DOWN, 3), (WG, OUT), (RS, OUT, 0),),
    BACKS_Z: ((RS, OUT, 1), (FFN, 0), (RS, GU_2, 2), (FFN, 1), (SHORT_1,), (WG, IN), (RS, S_DOWN, 0),
        (RS, GU, 3),),
    DQ: ((RS, IN, 0), (RS, OUT, 2), (RS, GU_2, 3), (FFN, 2), (RS, S_GU, 0), (RS, IN, 1),),
    DN1_X: ((WG, IN_2), (RS, IN_2, 0), (RS, IN, 2), (RS, IN_2, 1),),
    DN1_1: ((SMALL, 0),),
    DN1_2: ((RS, IN_2, 2),),
    GT_0: ((RS, IN, 3), (RS, S_IN, 0), (RS, OUT, 3), (RS, S_OUT, 0), (RS, S_DOWN, 1), (SMALL, 1),),
    GT_1: ((FFN, 3), (RS, IN_2, 3), (RS, S_IN_2, 0),),
    GT_2: ((RS, S_IN, 1), (RS, S_GU, 1), (RS, S_OUT, 1), (RS, S_DOWN, 2), (FFN, 4), (SMALL, 2),),
    GT_3: ((RS, S_IN_2, 1),),
    GT_4: ((RS, S_GU, 2), (FFN, 5), (RS, S_IN, 2), (RS, S_OUT, 2), (RS, S_IN_2, 2),),
}


class Rings:
    def __init__(self):
        self.z, self.y, self.c, self.x = where()
        self.chip = self.z * 4 + self.y
        self.sib = device(self.z, self.y, 1 - self.c, self.x)

    def near(self, axis, d):
        if axis == 0:
            return device(rem4(self.z + d), self.y, self.c, self.x)
        if axis == 1:
            return device(self.z, rem4(self.y + d), self.c, self.x)
        return device(self.z, self.y, self.c, rem4(self.x + d))

    def along(self, d):
        return (lax.rem(self.chip + d + 16, 16) * 2 + self.c, self.x)


class Gather:
    def __init__(self, r, ref, lanes, rows, phase, axis, split, send, recv):
        self.r, self.ref, self.lanes, self.rows = r, ref, lanes, rows
        self.phase, self.axis, self.split = phase, axis, split
        self.send, self.recv, self.sent = send, recv, []

    def copy(self, d, part, to, i):
        r, axis = self.r, self.axis
        z, y = (rem4(r.z + d), r.y) if axis == 0 else (r.z, rem4(r.y + d))
        if self.phase == 0:
            o, n = self.rows
            rows = (pl.ds(o, n), pl.ds(o, n // 2), pl.ds(o + n // 2, n // 2))[part]
            ref = self.ref.at[z, y, rows, self.lanes]
        else:
            many, rows = (pl.ds(0, 4), pl.ds(0, 2), pl.ds(2, 2))[part], pl.ds(*self.rows)
            ref = self.ref.at[z, many, rows, self.lanes] if axis == 0 else self.ref.at[many, y, rows, self.lanes]
        return remote(ref, ref, self.send, self.recv.at[i], r.near(axis, to))

    def start(self, *a):
        copy = self.copy(*a)
        copy.start()
        self.sent.append(copy)

    def step(self, i):
        if i == 1 and not self.split:
            self.start(0, 0, 1, 0)
            self.start(0, 0, -1, 1)
        elif i == 1:
            self.start(0, 1, 1, 0)
            self.start(0, 2, -1, 1)
        elif i == 2 and not self.split:
            pass
        elif i == 2:
            self.start(0, 2, 1, 2)
            self.start(0, 1, -1, 2)
        elif i == 3:
            self.copy(-1, 1 if self.split else 0, 1, 0).wait_recv()
            self.start(-1, 1, 1, 2)
            self.copy(1, 2 if self.split else 0, -1, 1).wait_recv()
            self.start(1, 2, -1, 2)
        else:
            waiting(self.units(2 if self.split else 1), self.recv.at[2]).wait_recv()

    def units(self, count):
        rows = pl.ds(*self.rows)
        if self.phase == 0:
            return self.ref.at[0, pl.ds(0, count), rows, self.lanes]
        return self.ref.at[pl.ds(0, count), :, rows, self.lanes]

    def drain(self):
        if self.sent:
            waiting(self.units(3), self.send).wait_send()
        self.sent = []


class Trade:
    def __init__(self, r, axis, src, land, send, recv):
        self.r, self.axis, self.src, self.land, self.send, self.recv = r, axis, src, land, send, recv
        self.me, self.sent = (r.z, r.y, r.x)[axis], []

    def copy(self, d):
        return remote(
            self.src(rem4(self.me + d)), self.land.at[self.me], self.send, self.recv,
            self.r.near(self.axis, d),
        )

    def begin(self):
        for d in (2, 1, 3):
            copy = self.copy(d)
            copy.start()
            self.sent.append(copy)

    def end(self):
        waiting(self.land.at[0:3], self.recv).wait_recv()

    def drain(self):
        if self.sent:
            waiting(self.land.at[0:3], self.send).wait_send()


class Scatter:
    def __init__(self, r, ref, lanes, rows, at, phase, axis, buf, send, recv):
        self.r, self.ref, self.lanes, self.rows, self.at = r, ref, lanes, rows, at
        self.phase, self.axis, self.buf, self.send, self.recv, self.sent = phase, axis, buf, send, recv, []

    def unit(self, d, part):
        r, axis = self.r, self.axis
        z, y = (rem4(r.z + d), r.y) if axis == 0 else (r.z, rem4(r.y + d))
        if self.phase == 1:
            o, n = self.rows
            return self.ref.at[z, y, pl.ds(o + n // 2 * part, n // 2), self.lanes]
        many, rows = pl.ds(2 * part, 2), pl.ds(*self.rows)
        return self.ref.at[z, many, rows, self.lanes] if axis == 0 else self.ref.at[many, y, rows, self.lanes]

    def landing(self, i):
        o, n = self.rows
        if self.phase == 0:
            return self.buf.at[i, :, pl.ds(o, n), self.at]
        return self.buf.at[i, pl.ds(o // 2, n // 2), self.at]

    def copy(self, d, part, to, i):
        return remote(
            self.unit(d, part), self.landing(i), self.send, self.recv.at[min(i, 2)],
            self.r.near(self.axis, to),
        )

    def start(self, *a):
        copy = self.copy(*a)
        copy.start()
        self.sent.append(copy)

    def arrived(self, i):
        self.copy(0, 0, 1, i).wait_recv()

    def add(self, d, part, many):
        unit = self.unit(d, part)
        lands, many = [self.landing(i) for i in many], self.rows[1] // 32
        if self.phase == 0:
            def body(i):
                k, rows = i // many, span(lax.rem(i, many) * 32, 32)
                total = unit[k, rows, :].astype(F32)
                for l in lands:
                    total = total + l[k, rows, :].astype(F32)
                unit[k, rows, :] = total.astype(BF16)
            loop(2 * many, body)
        else:
            def body(i):
                rows = span(i * 32, 32)
                total = unit[rows, :].astype(F32)
                for l in lands:
                    total = total + l[rows, :].astype(F32)
                unit[rows, :] = total.astype(BF16)
            loop(many // 2, body)

    def far(self):
        self.start(2, 0, 1, 0)
        self.start(2, 1, -1, 1)

    def early(self):
        self.start(1, 1, 1, 3)
        self.start(-1, 0, -1, 4)

    def forward(self):
        self.arrived(0)
        self.add(1, 0, (0,))
        self.start(1, 0, 1, 2)
        self.arrived(1)
        self.add(-1, 1, (1,))
        self.start(-1, 1, -1, 5)

    def units(self, count):
        o, n = self.rows
        if self.phase == 0:
            return self.buf.at[pl.ds(0, 2 * count), :, pl.ds(o, n), self.at]
        return self.buf.at[pl.ds(0, 2 * count), pl.ds(o // 2, n // 2), self.at]

    def finish(self):
        waiting(self.units(2), self.recv.at[2]).wait_recv()
        self.add(0, 0, (2, 4))
        self.add(0, 1, (3, 5))

    def drain(self):
        if self.sent:
            waiting(self.units(3), self.send).wait_send()
        self.sent = []


class CrossSum:
    def __init__(self, r, part, got, mid, one, two, send, recv):
        self.r, self.part, self.got, self.mid, self.one, self.two = r, part, got, mid, one, two
        self.send, self.recv, self.sent = send, recv, []

    def start(self, copy):
        copy.start()
        self.sent.append(copy)

    def rows(self, c, x):
        return span((c * 4 + x) * 32, 32)

    def pair(self, d):
        x = rem4(self.r.x + d)
        return remote(
            self.part.at[self.rows(1 - self.r.c, x)], self.got.at[x],
            self.send, self.recv.at[(4, 1, 0, 1)[d]], self.r.sib,
        )

    def begin(self):
        for d in (2, 1, 3, 0):
            self.start(self.pair(d))

    def pairsum(self, d):
        x = rem4(self.r.x + d)
        rows = self.rows(self.r.c, x)
        self.mid[x] = (self.part[rows].astype(F32) + self.got[x].astype(F32)).astype(BF16)

    def far(self, side):
        x = rem4(self.r.x + 2)
        return remote(
            self.mid.at[x, pl.ds(16 * side, 16)], self.one.at[side],
            self.send, self.recv.at[2 + side], self.r.near(2, 1 - 2 * side),
        )

    def late(self, side, summed):
        d = 1 - 2 * side
        x = rem4(self.r.x + d)
        half = side if summed else 1 - side
        return remote(
            self.mid.at[x, pl.ds(16 * half, 16)], self.two.at[side, pl.ds(16 * half, 16)],
            self.send, self.recv.at[4], self.r.near(2, d),
        )

    def middle(self):
        self.near_half()
        self.far_half()

    def near_half(self):
        self.pair(2).wait_recv()
        self.pairsum(2)
        self.start(self.far(0))
        self.start(self.far(1))
        waiting(self.part.at[0:64], self.recv.at[1]).wait_recv()
        self.pairsum(1)
        self.start(self.late(0, 0))
        self.pairsum(3)
        self.start(self.late(1, 0))

    def far_half(self):
        for side in range(2):
            self.far(side).wait_recv()
            x = rem4(self.r.x + 1 - 2 * side)
            rows = pl.ds(16 * side, 16)
            self.mid[x, rows] = (self.mid[x, rows].astype(F32) + self.one[side].astype(F32)).astype(BF16)
            self.start(self.late(side, 1))

    def end(self):
        waiting(self.part.at[0:96], self.recv.at[4]).wait_recv()

    def result(self, rows):
        base = (self.r.c * 4 + self.r.x) * 32
        own = self.part[pl.ds(pl.multiple_of(base + rows.start, rows.size), rows.size)].astype(F32)
        own = own + self.got[self.r.x, rows].astype(F32)
        return own + self.two[0, rows].astype(F32) + self.two[1, rows].astype(F32)

    def drain(self):
        if self.sent:
            waiting(self.part.at[0:224], self.send).wait_send()
        self.sent = []


class CrossGather:
    def __init__(self, r, ref, both, send, recv):
        self.r, self.ref, self.both, self.send, self.recv, self.sent = r, ref, both, send, recv, []

    def start(self, copy):
        copy.start()
        self.sent.append(copy)

    def rows(self, d, part):
        base = rem4(self.r.x + d) * 32
        if self.both:
            base = base + self.r.c * 128
        if part is None:
            return self.ref.at[pl.ds(pl.multiple_of(base, 32), 32)]
        return self.ref.at[pl.ds(pl.multiple_of(base + 16 * part, 16), 16)]

    def ring(self, d, part, to, i):
        ref = self.rows(d, part)
        return remote(ref, ref, self.send, self.recv.at[i], self.r.near(2, to))

    def pair(self, d):
        ref = self.rows(d, None)
        return remote(ref, ref, self.send, self.recv.at[4], self.r.sib)

    def begin(self):
        self.start(self.ring(0, 0, 1, 0))
        self.start(self.ring(0, 1, -1, 1))
        self.start(self.ring(0, 1, 1, 2))
        self.start(self.ring(0, 0, -1, 2))
        if self.both:
            self.start(self.pair(0))

    def middle(self):
        self.ring(-1, 0, 1, 0).wait_recv()
        self.start(self.ring(-1, 0, 1, 3))
        self.ring(1, 1, -1, 1).wait_recv()
        self.start(self.ring(1, 1, -1, 3))
        waiting(self.ref.at[0:32], self.recv.at[2]).wait_recv()
        if self.both:
            self.start(self.pair(-1))
            self.start(self.pair(1))

    def end(self):
        waiting(self.ref.at[0:32], self.recv.at[3]).wait_recv()
        if self.both:
            self.start(self.pair(2))
            waiting(self.ref.at[0:128], self.recv.at[4]).wait_recv()

    def drain(self):
        waiting(self.ref.at[0:224 if self.both else 96], self.send).wait_send()


class Refs:
    pass


class Inputs:
    in_w = out_w = gate_w = up_w = down_w = gain_1 = gain_2 = resets = tok = cot = conv_w = 0
    decay = angle = res_re = res_im = 0


class Outputs:
    block_out = grad_tok = grad_w = grad_small = grad_gain = 0


class Scratch:
    other = ((64, LANES_A + LANES_B), BF16)
    tab = ((8, 16, 256), F32)
    ga = ((4, 4, 128, LANES_A), BF16)
    gb = ((4, 4, 128, LANES_B), BF16)
    s0a = ((6, 2, 128, LANES_A), BF16)
    s0b = ((6, 2, 128, LANES_B), BF16)
    s1a = ((6, 64, LANES_A), BF16)
    s1b = ((6, 64, LANES_B), BF16)
    da = ((4, 4, 128, 384), BF16)
    ia = ((4, 4, 128, 128), BF16)
    ib = ((4, 4, 128, 128), BF16)
    db = ((4, 4, 128, 384), BF16)
    sib_a = ((64, LANES_A), BF16)
    sib_b = ((64, LANES_B), BF16)
    gains_y = ((4, 16, 128), F32)
    gains_all = ((4, 4, 16, 128), F32)
    gains = ((8, 2048), F32)
    gain_in = ((8, 128), F32)
    taps = ((8, 768), F32)
    keep = ((256, 256), F32)
    gy = ((256, 2048), BF16)
    n1 = ((272, 2048), BF16)
    n2 = ((256, 2048), BF16)
    dh = ((256, 2048), BF16)
    part = ((256, 2048), BF16)
    mid = ((4, 32, 2048), BF16)
    part_f = ((256, 2048), BF16)
    mid_f = ((4, 32, 2048), BF16)
    got = ((4, 4, 32, 2048), BF16)
    one = ((4, 2, 16, 2048), BF16)
    two = ((4, 2, 32, 2048), BF16)
    bo = ((128, 2048), BF16)
    gt = ((128, 2048), BF16)
    h = ((32, 2048), F32)
    dhf = ((32, 2048), F32)
    p = ((272, 768), F32)
    q0 = ((256, 256), F32)
    q1 = ((256, 256), F32)
    q2 = ((256, 256), F32)
    u = ((256, 256), F32)
    v = ((256, 256), F32)
    z = ((256, 256), BF16)
    st_re = ((257, 16, 256), F32)
    st_im = ((257, 16, 256), F32)
    ends_y = ((4, 32, 256), F32)
    ends_z = ((4, 32, 256), F32)
    backs_y = ((4, 32, 256), F32)
    backs_z = ((4, 32, 256), F32)
    gu = ((256, 1408), F32)
    act = ((256, 768), BF16)
    dgu = ((256, 1408), BF16)
    dv = ((256, 256), F32)
    dq = ((264, 768), F32)
    dp = ((256, 768), BF16)
    small_y = ((4, 80, 256), BF16)
    small_z = ((4, 80, 256), BF16)
    small_sum = ((80, 256), F32)
    small_sib = ((80, 256), F32)
    ggain = ((8, 2048), F32)
    gg_z = ((4, 8, 512), F32)
    gg_1 = ((8, 512), F32)
    gg_y = ((4, 8, 128), F32)
    gg_2 = ((8, 128), F32)
    gg_s = ((8, 128), F32)
    gg_x = ((4, 8, 128), F32)
    gg_out = ((8, 128), F32)


def fields(group):
    return [(name, value) for name, value in vars(group).items() if name[0] != "_"]


class Sems:
    w = (7, 4), (7, 4, 3)
    w_sib = (2,), (2,)
    gain_sib = keep_s = gy_s = n1_s = edge = dq_s = dq_1 = small_x = gg_s = (), ()
    trade = (11,), (11,)
    sum = (4,), (4, 5)
    cg = (4,), (4, 5)
    rs = (11, 4), (11, 4, 3)
    rs_sib = (5,), (5,)


def kernel(*refs):
    names = [name for group in (Inputs, Outputs, Scratch) for name, _ in fields(group)]
    k, S, R = Refs(), Refs(), Refs()
    for name, ref in zip(names, refs):
        setattr(k, name, ref)
    rest = refs[len(names):]
    for i, (name, _) in enumerate(fields(Sems)):
        setattr(S, name, rest[2 * i])
        setattr(R, name, rest[2 * i + 1])
    local = rest[-1]
    r = Rings()
    g = (k.ga, k.gb)
    z, y, c, x = r.z, r.y, r.c, r.x

    barrier = pltpu.get_barrier_semaphore()
    peers = [r.sib] + [r.near(a, d) for a in range(3) for d in (1, 2, 3)] + [r.along(1), r.along(-1)]
    for peer in peers:
        pl.semaphore_signal(barrier, inc=1, device_id=peer, device_id_type=MESH)

    def lanes(n, h):
        o, w = CHUNKS[n][h]
        return pl.ds(o, w)

    def columns(n, start, stop):
        (oa, wa), (ob, _) = WHOLE[n]
        parts = []
        if start < wa:
            parts.append(g[0][:, :, :, oa + start:oa + min(stop, wa)])
        if stop > wa:
            parts.append(g[1][:, :, :, ob + max(start - wa, 0):ob + stop - wa])
        return jnp.concatenate([p.reshape(2048, p.shape[-1]) for p in parts], 1)

    def weight(n, h, i):
        o, w = WHOLE[n][h]
        return g[h][i, :, :, o:o + w].reshape(512, w)

    trades = []

    def trade(axis, src, land):
        i = len(trades)
        trades.append(Trade(r, axis, src if callable(src) else lambda _: src, land, S.trade.at[i], R.trade.at[i]))
        return trades[-1]

    my64 = span(c * 64, 64)
    my128 = span(c * 128, 128)
    gather = []
    for n, (phase, split, parts) in enumerate(GATHERS):
        gather.append([
            Gather(r, g[b], pl.ds(o, w), rows, phase, 1 - way if phase == 0 else way, split and rows[1] == 128,
                   S.w.at[n, i], R.w.at[n, i])
            for i, (way, b, o, w, *rows) in enumerate(parts)
        ])

    def put(cc, n, sink):
        wa = WHOLE[n][0][1]

        def store(start, value):
            stop = start + value.shape[1]
            if start < wa:
                sink(0, WHOLE[n][0][0] + start, value[:, :min(stop, wa) - start])
            if stop > wa:
                sink(1, WHOLE[n][1][0] + max(start - wa, 0), value[:, max(wa - start, 0):])

        def main(ref):
            return ref[:, pl.ds(pl.multiple_of(cc * 640, 128), 640)]

        def tail(ref):
            a = ref[:, 1280:1408].astype(F32)
            return jnp.where(cc == 0, a[:, 0:64], a[:, 64:128])

        channels = pl.ds(pl.multiple_of(cc * 256, 256), 256)
        if n == IN:
            store(0, k.in_w[0, :, channels])
        elif n == IN_2:
            store(0, k.in_w[1, :, channels])
            store(256, k.in_w[2, :, channels])
        elif n == OUT:
            store(0, k.out_w[:, channels])
        elif n == GU:
            store(0, main(k.gate_w))
            store(640, main(k.up_w))
            store(1280, jnp.concatenate([tail(k.gate_w), tail(k.up_w)], 1).astype(BF16))
        else:
            store(0, main(k.down_w))
            store(640, jnp.concatenate([tail(k.down_w), jnp.zeros((64, 64), F32)], 1).astype(BF16))

    def to_other(h, at, value):
        at = at + (LANES_A if h else 0)
        k.other[:, at:at + value.shape[1]] = value

    def to_own(h, at, value):
        g[h][z, y, my64, at:at + value.shape[1]] = value

    def weight_sib(n, h):
        o, w = ((0, 384), (384, (1280, 1152)[h]))[n]
        return remote(
            k.other.at[:, pl.ds(o + (LANES_A if h else 0), w)], g[h].at[z, y, my64, pl.ds(o, w)],
            S.w_sib.at[n], R.w_sib.at[n], r.sib,
        )

    eight = span(c * 8, 8)
    side = lax.broadcasted_iota(jnp.int32, (1, 128), 1) // 64 == c
    for i, ref in enumerate((k.gain_1, k.gain_2)):
        a = ref[...].astype(F32)
        k.gain_in[i:i + 1, :] = jnp.where(side, jnp.concatenate([a, a], 1), 0.0)
    k.gain_in[2:8, :] = jnp.zeros((6, 128), F32)
    k.gains_y[y, eight] = k.gain_in[...]
    for n in (IN, IN_2):
        put(1 - c, n, to_other)
        put(c, n, to_own)
    keep = 1.0 - k.resets[...].astype(F32)
    keep = jnp.broadcast_to(keep, (128, 128)).T
    k.keep[my128] = jnp.concatenate([keep, keep], 1)
    pl.semaphore_wait(barrier, len(peers))

    gain_sib = remote(k.gain_in, k.gains_y.at[y, eight], S.gain_sib, R.gain_sib, r.sib)
    keep_sib = remote(k.keep.at[my128], k.keep.at[my128], S.keep_s, R.keep_s, r.sib)
    gy_sib = remote(k.cot, k.gy.at[my128], S.gy_s, R.gy_s, r.sib)
    def share(n):
        for h in range(2):
            weight_sib(n, h).start()

    share(A_IN)
    gain_sib.start()

    def ag(n, i):
        if i == 1 and n in (A_IN, A_REST):
            waiting(k.other.at[:, 0:(768, 2432)[n]], R.w_sib.at[n]).wait_recv()
        for piece in gather[n]:
            piece.step(i)

    tasks = {}

    def at(point):
        for name, *rest in PLAN.get(point, ()):
            tasks[name](*rest)

    tasks[AG] = ag
    at(START)
    gain_y = trade(1, k.gains_y.at[y], k.gains_y)
    gain_z = trade(0, k.gains_y, k.gains_all)
    gain_sib.wait_recv()
    gain_y.begin()

    for n in (OUT, GU, DOWN):
        put(1 - c, n, to_other)
        put(c, n, to_own)
    share(A_REST)
    keep_sib.start()
    at(GAIN_Y)
    gain_y.end()
    gain_z.begin()
    k.gains_all[z] = k.gains_y[...]
    at(GAIN_Z)
    k.gy[my128] = k.cot[...]

    channels = pl.ds(pl.multiple_of(c * 256, 256), 256)
    decay, angle = k.decay[:, channels], k.angle[:, channels]
    size = jnp.exp(-decay)
    gin = jnp.sqrt(-expm1(-2.0 * decay))
    power = (size * jnp.cos(angle), size * jnp.sin(angle))
    k.tab[0], k.tab[1] = power
    k.tab[2] = gin * k.res_re[:, channels]
    k.tab[3] = gin * k.res_im[:, channels]
    for _ in range(8):
        power = (power[0] * power[0] - power[1] * power[1], 2.0 * power[0] * power[1])
    k.tab[4], k.tab[5] = power
    k.tab[6] = gin
    k.tab[7] = size * size / gin
    for i in range(3):
        for b in range(3):
            k.taps[i:i + 1, b * 256:b * 256 + 256] = k.conv_w[i, b:b + 1, channels]

    gain_z.end()
    for i in range(16):
        k.gains[:, i * 128:(i + 1) * 128] = k.gains_all[i // 4, i % 4, 0:8] + k.gains_all[i // 4, i % 4, 8:16]

    def norm_one(i):
        rows = span(i * 16, 16)
        a = k.tok[rows, :].astype(F32)
        s = lax.rsqrt(jnp.mean(a * a, axis=-1, keepdims=True) + EPSILON)
        k.n1[pl.ds(pl.multiple_of(16 + c * 128 + i * 16, 16), 16), :] = (a * s * k.gains[0:1, :]).astype(BF16)
    loop(8, norm_one)

    def n1_rows(c):
        return k.n1.at[pl.ds(pl.multiple_of(16 + c * 128, 16), 128)]

    n1_sib = remote(n1_rows(c), n1_rows(c), S.n1_s, R.n1_s, r.sib)
    n1_sib.start()
    at(NORM_1)
    k_other = span((1 - c) * 128, 128)
    remote(n1_rows(1 - c), n1_rows(1 - c), S.n1_s, R.n1_s, r.sib).wait_recv()
    edge = remote(k.n1.at[256:272], k.n1.at[0:16], S.edge, R.edge, r.along(1))
    edge.start()
    gy_sib.start()
    at(EDGE)

    edge.wait_recv()
    at(PROJECT)

    def project(_):
        for o in range(0, 512, 256):
            k.p[:, 256 + o:512 + o] = nn(k.n1[...], columns(IN_2, o, o + 256))
        k.p[:, 0:256] = nn(k.n1[...], columns(IN, 0, 256))
    loop(1, project)

    def round_p(i):
        rows = span(i * 16, 16)
        k.p[rows, :] = k.p[rows, :].astype(BF16).astype(F32)
    loop(17, round_p)
    remote(k.keep.at[k_other], k.keep.at[k_other], S.keep_s, R.keep_s, r.sib).wait_recv()
    at(SHORT)

    def masks(i):
        rows = span(i * 16, 16)
        near = k.keep[rows, :]
        before = k.keep[span(jnp.maximum(i * 16 - 8, 0), 8), :]
        first = jnp.where(i == 0, 1.0, before[7:8, :])
        shifted = jnp.concatenate([first, near[0:15, :]], 0)
        return near, near * shifted

    def short(i):
        near, far = masks(i)
        ext = k.p[pl.ds(pl.multiple_of(i * 16 + 8, 8), 24), :]
        q = []
        for b in range(3):
            l = slice(b * 256, b * 256 + 256)
            e = ext[:, l]
            q.append(
                k.taps[0:1, l] * e[8:24] + near * k.taps[1:2, l] * e[7:23] + far * k.taps[2:3, l] * e[6:22]
            )
        rows = span(i * 16, 16)
        k.q0[rows, :] = q[0]
        k.q1[rows, :] = q[1]
        k.q2[rows, :] = q[2]
        k.u[rows, :] = q[1] * q[2]
    loop(16, short)

    zero = jnp.zeros((16, 256), F32)
    lr, li, cr, ci, pr, pi = (k.tab[i] for i in range(6))

    def advance(re, im, u, keep):
        kr, ki = keep * re, keep * im
        return lr * kr - li * ki + u, lr * ki + li * kr

    def end_state(i, state):
        rows = span(i * 8, 8)
        u, keep = k.u[rows, :], k.keep[rows, :]
        for j in range(8):
            state = advance(*state, u[j:j + 1, :], keep[j:j + 1, :])
        return state

    def times(a, b, g, h):
        return a * g - b * h, a * h + b * g

    def chain(own, ref_y, ref_z, sign, between):
        order = range(4) if sign > 0 else range(3, -1, -1)
        qr, qi = pr, sign * pi

        def put(ref, at, state):
            ref[at, 0:16] = state[0]
            ref[at, 16:32] = state[1]

        def horner(ref, wr, wi, state, here, every):
            for i in order:
                nr, ni = times(wr, wi, *state)
                nr, ni = nr + ref[i, 0:16], ni + ref[i, 16:32]
                use = (i < here) if sign > 0 else (i > here)
                state = (nr, ni) if every else (jnp.where(use, nr, state[0]), jnp.where(use, ni, state[1]))
            return state

        put(ref_y, y, own)
        t = trade(1, ref_y.at[y], ref_y)
        t.begin()
        at(between[0])
        t.end()
        put(ref_z, z, horner(ref_y, qr, qi, (zero, zero), y, True))
        t = trade(0, ref_z.at[z], ref_z)
        t.begin()
        at(between[1])
        t.end()
        w = times(*times(qr, qi, qr, qi), *times(qr, qi, qr, qi))
        return horner(ref_y, qr, qi, horner(ref_z, *w, (zero, zero), z, False), y, False)

    end = fold(32, end_state, (zero, zero))
    enter = chain(end, k.ends_y, k.ends_z, 1, (ENDS_Y, ENDS_Z))
    k.st_re[0] = enter[0]
    k.st_im[0] = enter[1]
    at(SCAN)

    def scan(i, state):
        rows = span(i * 8, 8)
        u, keep = k.u[rows, :], k.keep[rows, :]
        for j in range(8):
            state = advance(*state, u[j:j + 1, :], keep[j:j + 1, :])
            k.st_re[i * 8 + j + 1] = state[0]
            k.st_im[i * 8 + j + 1] = state[1]
            k.v[pl.ds(i * 8 + j, 1), :] = jnp.sum(cr * state[0] - ci * state[1], axis=0, keepdims=True)
        return state
    fold(32, scan, enter)

    def gated(i):
        rows = span(i * 32, 32)
        k.z[rows, :] = (k.q0[rows, :] * k.v[rows, :]).astype(BF16)
    loop(8, gated)

    at(MIX)
    def out_weight(i):
        return jnp.concatenate([weight(OUT, 0, i), weight(OUT, 1, i)], 1)

    def mix(i):
        k.part[:, span(i * 512, 512)] = nt(k.z[...], out_weight(i)).astype(BF16)
    loop(4, mix)

    def cross(i):
        part, mid = (k.part_f, k.mid_f) if i == 1 else (k.part, k.mid)
        return CrossSum(r, part, k.got.at[i], mid, k.one.at[i], k.two.at[i], S.sum.at[i], R.sum.at[i])

    s_mix = cross(0)
    s_mix.begin()
    at(MIX_0)
    s_mix.near_half()
    at(MIX_1)
    s_mix.far_half()
    at(MIX_2)
    s_mix.end()

    own = (c * 4 + x) * 32

    def norm_two(i):
        rows = pl.ds(pl.multiple_of(i * 16, 16), 16)
        a = k.tok[pl.ds(pl.multiple_of(x * 32 + i * 16, 16), 16), :].astype(F32) + s_mix.result(rows)
        k.h[rows, :] = a
        s = lax.rsqrt(jnp.mean(a * a, axis=-1, keepdims=True) + EPSILON)
        k.n2[pl.ds(pl.multiple_of(own + i * 16, 16), 16), :] = (a * s * k.gains[1:2, :]).astype(BF16)
    loop(2, norm_two)
    g_n2 = CrossGather(r, k.n2, True, S.cg.at[0], R.cg.at[0])
    g_n2.begin()
    at(N2_0)
    g_n2.middle()
    at(N2_1)
    g_n2.end()
    s_mix.drain()
    at(FF)

    def gate_up(_):
        for o in range(0, 1408, 256):
            e = min(o + 256, 1408)
            k.gu[:, o:e] = nn(k.n2[...], columns(GU, o, e))
    loop(1, gate_up)
    def halves(t):
        last = t[:, 1280:1408]
        turned = jnp.concatenate([last[:, 64:128], last[:, 0:64]], 1)
        return jnp.concatenate([t[:, 0:640], last], 1), jnp.concatenate([t[:, 640:1280], turned], 1)

    used = lax.broadcasted_iota(jnp.int32, (1, 768), 1) < 704

    def activate(i):
        rows = span(i * 16, 16)
        gate, up = halves(k.gu[rows, :])
        k.act[rows, :] = jnp.where(used, gate * jax.nn.sigmoid(gate) * up, 0.0).astype(BF16)
    loop(16, activate)

    def down_weight(i):
        return jnp.concatenate([weight(DOWN, 0, i), weight(DOWN, 1, i)], 1)

    s_ffn = cross(1)
    g_bo = CrossGather(r, k.bo, False, S.cg.at[1], R.cg.at[1])
    out_bo = pltpu.make_async_copy(k.bo, k.block_out, local.at[0])

    def ffn_step(i):
        if i == 0:
            def ffn(i):
                k.part_f[:, span(i * 512, 512)] = nt(k.act[...], down_weight(i)).astype(BF16)
            loop(4, ffn)
            s_ffn.begin()
        elif i == 1:
            s_ffn.near_half()
        elif i == 2:
            s_ffn.far_half()
        elif i == 3:
            s_ffn.end()

            def top(i):
                rows = pl.ds(pl.multiple_of(i * 16, 16), 16)
                here = pl.ds(pl.multiple_of(x * 32 + i * 16, 16), 16)
                k.bo[here, :] = (k.h[rows, :] + s_ffn.result(rows)).astype(BF16)
            loop(2, top)
            s_ffn.drain()
            g_bo.begin()
        elif i == 4:
            g_bo.middle()
        else:
            g_bo.end()
            out_bo.start()

    tasks[FFN] = ffn_step

    apart = {DOWN: (k.da, k.db), IN: (k.ia, k.ib)}
    scatter = []
    for n, parts in enumerate(SCATTERS):
        phase = 0 if n < S_IN else 1
        m = {S_IN: IN, S_DOWN: DOWN}.get(n, n if phase == 0 else None)
        scatter.append([])
        for i, (way, b, o, w, *rows) in enumerate(parts):
            ref, here = g[b], pl.ds(o, w)
            if m in apart:
                ref, here = apart[m][b], pl.ds(o - CHUNKS[m][b][0], w)
            buf = ((k.s0a, k.s0b), (k.s1a, k.s1b))[phase][b]
            axis = 1 - way if phase == 0 else way
            scatter[n].append(
                Scatter(r, ref, here, rows, pl.ds(o, w), phase, axis, buf, S.rs.at[n, i], R.rs.at[n, i])
            )

    def finished(n, h):
        o, w = SECOND[n - S_IN][h]
        m = {S_IN: IN, S_DOWN: DOWN}.get(n)
        return (apart[m][h], pl.ds(0, w), pl.ds(o, w)) if m in apart else (g[h], pl.ds(o, w), pl.ds(o, w))

    sib_bufs = (k.sib_a, k.sib_b)

    def rs_sib(n, h):
        ref, here, at = finished(n, h)
        return remote(
            ref.at[z, y, span((1 - c) * 64, 64), here], sib_bufs[h].at[:, at],
            S.rs_sib.at[n - S_IN], R.rs_sib.at[n - S_IN], r.sib,
        )

    def rs(n, i):
        for s in scatter[n]:
            if n < S_IN:
                (s.far, s.early, s.forward, s.finish)[i]()
            elif i == 0:
                s.far()
                s.early()
            elif i == 1:
                s.forward()
            else:
                s.finish()
        if n >= S_IN and i == 2:
            for h in range(2):
                rs_sib(n, h).start()

    tasks[RS] = rs

    def wg(n):
        a, b, first = {
            IN: (k.n1, k.dp.at[:, 0:256], 16), IN_2: (k.n1, k.dp.at[:, 256:768], 16), OUT: (k.dh, k.z, 0),
            GU: (k.n2, k.dgu, 0), DOWN: (k.gy, k.act, 0),
        }[n]
        for m in {GU: (B_GU, B_GU_2), OUT: (B_OUT,), IN_2: (B_IN,)}.get(n, ()) + ((A_IN, A_REST) if n == GU else ()):
            for piece in gather[m]:
                piece.drain()
        (oa, wa), (ob, wb) = [(0, CHUNKS[n][h][1]) for h in range(2)] if n in apart else WHOLE[n]
        into = apart.get(n, g)

        def weight_grad(i):
            t = tn(a[pl.ds(first, 256), pl.ds(pl.multiple_of(i * 512, 512), 512)], b[...]).astype(BF16)
            into[0][i, :, :, oa:oa + wa] = t[:, 0:wa].reshape(4, 128, wa)
            into[1][i, :, :, ob:ob + wb] = t[:, wa:wa + wb].reshape(4, 128, wb)
        weight_grad.width = wa + wb
        loop(4, weight_grad)

    tasks[WG] = wg

    remote(k.gy.at[k_other], k.gy.at[k_other], S.gy_s, R.gy_s, r.sib).wait_recv()
    at(ACT)

    def d_act(_):
        for o in range(0, 768, 256):
            k.dq[0:256, o:o + 256] = nn(k.gy[...], columns(DOWN, o, o + 256))
    loop(1, d_act)
    at(DA)

    def d_gates(i):
        rows = span(i * 16, 16)
        gate, up = halves(k.gu[rows, :])
        da = k.dq[rows, :]
        sg = jax.nn.sigmoid(gate)
        dgate = da * up * sg * (1.0 + gate * (1.0 - sg))
        dup = da * (gate * sg)
        last = jnp.concatenate([dgate[:, 640:704], dup[:, 640:704]], 1)
        k.dgu[rows, :] = jnp.concatenate([dgate[:, 0:640], dup[:, 0:640], last], 1).astype(BF16)
    loop(16, d_gates)

    def d_n2(i):
        w = jnp.concatenate([weight(GU, 0, i), weight(GU, 1, i)], 1)
        k.part[:, span(i * 512, 512)] = nt(k.dgu[...], w).astype(BF16)
    loop(4, d_n2)
    s_dn2 = cross(2)
    s_dn2.begin()
    at(DN2_0)
    s_dn2.near_half()
    at(DN2_1)
    s_dn2.far_half()
    at(DN2_2)
    s_dn2.end()

    def d_norm_two(i):
        rows = pl.ds(pl.multiple_of(i * 16, 16), 16)
        a = k.h[rows, :]
        s = lax.rsqrt(jnp.mean(a * a, axis=-1, keepdims=True) + EPSILON)
        hat = a * s
        dn = s_dn2.result(rows)
        dng = dn * k.gains[1:2, :]
        gy = k.gy[pl.ds(pl.multiple_of(own + i * 16, 16), 16), :].astype(F32)
        dh = gy + s * (dng - hat * jnp.mean(dng * hat, axis=-1, keepdims=True))
        k.dhf[rows, :] = dh
        k.dh[pl.ds(pl.multiple_of(own + i * 16, 16), 16), :] = dh.astype(BF16)
        t = jnp.sum(dn * hat, axis=0, keepdims=True)

        @pl.when(i == 0)
        def _():
            k.ggain[...] = jnp.zeros((8, 2048), F32)
            k.ggain[1:2, :] = t

        @pl.when(i > 0)
        def _():
            k.ggain[1:2, :] += t
    loop(2, d_norm_two)
    s_dn2.drain()
    g_dh = CrossGather(r, k.dh, True, S.cg.at[2], R.cg.at[2])
    g_dh.begin()
    at(DH_0)
    g_dh.middle()
    at(DH_1)
    g_dh.end()
    at(DZ)

    def d_z(_):
        k.dv[...] = nn(k.dh[...], columns(OUT, 0, 256))
    loop(1, d_z)

    def d_gated(i):
        rows = span(i * 32, 32)
        dz = k.dv[rows, :]
        k.dq[rows, 0:256] = dz * k.v[rows, :]
        k.dv[rows, :] = dz * k.q0[rows, :]
    loop(8, d_gated)

    first = slice(0, 256)
    others = slice(256, 768)

    def dq_edge(at, send, recv):
        return remote(k.dq.at[0:8, at], k.dq.at[256:264, at], send, recv, r.along(-1))

    dq_first = dq_edge(first, S.dq_1, R.dq_1)
    dq_first.start()

    last = jnp.where(r.chip < 15, 1.0, 0.0)

    def d_short(i, taps, branches):
        near, far = masks(i)
        j = jnp.minimum(i * 16 + 16, 248)
        after = k.keep[span(j, 8), :]
        inside = i < 15
        tail_near = jnp.where(inside, after, last)
        tail_far = jnp.where(
            inside, after * jnp.concatenate([near[15:16, :], after[0:7, :]], 0), last
        )
        near = jnp.concatenate([near, tail_near], 0)
        far = jnp.concatenate([far, tail_far], 0)
        ext = k.p[pl.ds(pl.multiple_of(i * 16 + 8, 8), 24), :]
        rows = span(i * 16, 16)
        new = []
        for n, b in enumerate(branches):
            l = slice(b * 256, b * 256 + 256)
            e, db = ext[:, l], k.dq[pl.ds(pl.multiple_of(i * 16, 16), 24), l]
            dn, df = near * db, far * db
            k.dp[rows, l] = (
                k.taps[0:1, l] * db[0:16] + k.taps[1:2, l] * dn[1:17] + k.taps[2:3, l] * df[2:18]
            ).astype(BF16)
            new.append(taps[3 * n + 0] + jnp.sum(e[8:24] * db[0:16], axis=0, keepdims=True))
            new.append(taps[3 * n + 1] + jnp.sum(e[7:23] * dn[0:16], axis=0, keepdims=True))
            new.append(taps[3 * n + 2] + jnp.sum(e[6:22] * df[0:16], axis=0, keepdims=True))
        return tuple(new)

    line = jnp.zeros((1, 256), F32)
    def d_short_1(i, taps):
        return d_short(i, taps, (0,))

    def d_short_2(i, taps):
        return d_short(i, taps, (1, 2))

    d_taps = []

    def short_1():
        dq_first.wait()
        d_taps.extend(fold(16, d_short_1, (line,) * 3))

    tasks[SHORT_1] = short_1

    def retreat(a, b, keep):
        ka, kb = keep * a, keep * b
        return ka, kb, lr * ka + li * kb, lr * kb - li * ka

    def start_state(i, state):
        rows = span((31 - i) * 8, 8)
        dv, keep = k.dv[rows, :], k.keep[rows, :]
        for j in reversed(range(8)):
            a = cr * dv[j:j + 1, :] + state[0]
            b = state[1] - ci * dv[j:j + 1, :]
            _, _, pa, pb = retreat(a, b, keep[j:j + 1, :])
            state = (pa, pb)
        return state

    begin = fold(32, start_state, (zero, zero))
    arrive = chain(begin, k.backs_y, k.backs_z, -1, (BACKS_Y, BACKS_Z))
    at(ADJOINT)

    def adjoint(i, carry):
        rows = span((31 - i) * 8, 8)
        dv, keep = k.dv[rows, :], k.keep[rows, :]
        for j in reversed(range(8)):
            t = (31 - i) * 8 + j
            d = dv[j:j + 1, :]
            a = cr * d + carry[0]
            b = carry[1] - ci * d
            k.u[pl.ds(t, 1), :] = jnp.sum(a, axis=0, keepdims=True)
            _, _, pa, pb = retreat(a, b, keep[j:j + 1, :])
            carry = (pa, pb)
        return carry

    fold(32, adjoint, arrive)

    def d_poles(i, carry):
        pa, pb, dcr, dci, dlr, dli = carry
        rows = span((31 - i) * 8, 8)
        dv, keep = k.dv[rows, :], k.keep[rows, :]
        for j in reversed(range(8)):
            t = (31 - i) * 8 + j
            d = dv[j:j + 1, :]
            a = cr * d + pa
            b = pb - ci * d
            dcr = dcr + d * k.st_re[t + 1]
            dci = dci - d * k.st_im[t + 1]
            ka, kb, pa, pb = retreat(a, b, keep[j:j + 1, :])
            sr, si = k.st_re[t], k.st_im[t]
            dlr = dlr + ka * sr + kb * si
            dli = dli + kb * sr - ka * si
        return pa, pb, dcr, dci, dlr, dli

    def d_branches(i):
        rows = span(i * 32, 32)
        du = k.u[rows, :]
        k.dq[rows, 256:512] = du * k.q2[rows, :]
        k.dq[rows, 512:768] = du * k.q1[rows, :]
    loop(8, d_branches)
    dq_next = dq_edge(others, S.dq_s, R.dq_s)
    dq_next.start()
    at(DQ)
    dq_next.wait()
    d_taps.extend(fold(16, d_short_2, (line,) * 6))

    def d_n1(i):
        w = jnp.concatenate([weight(n, h, i) for n in (IN, IN_2) for h in range(2)], 1)
        k.part[:, span(i * 512, 512)] = nt(k.dp[...], w).astype(BF16)
    loop(4, d_n1)
    s_dn1 = cross(3)
    s_dn1.begin()
    at(DN1_0)

    small_1 = trade(1, k.small_y.at[y], k.small_y)
    small_2 = trade(0, k.small_z.at[z], k.small_z)

    def small_total(ref):
        return sum(ref[j].astype(F32) for j in range(4))

    small_x = remote(k.small_sum, k.small_sib, S.small_x, R.small_x, r.sib)

    def small(i):
        if i == 0:
            _, _, *dpoles = fold(32, d_poles, (*arrive, zero, zero, zero, zero))
            for j in range(4):
                k.small_y[y, 16 * j:16 * j + 16] = dpoles[j].astype(BF16)
            k.small_y[y, 64:80] = jnp.concatenate([d_taps[3 * b + t] for t in range(3) for b in range(3)] + [jnp.zeros((7, 256), F32)], 0).astype(BF16)
            small_1.begin()
        elif i == 1:
            small_1.end()
            k.small_z[z] = small_total(k.small_y).astype(BF16)
            small_2.begin()
        else:
            small_2.end()
            k.small_sum[...] = small_total(k.small_z)
            dcr, dci, dlr, dli = (k.small_sum[16 * j:16 * j + 16, :] for j in range(4))
            dgin = k.res_re[:, channels] * dcr + k.res_im[:, channels] * dci
            k.small_sum[0:16, :] = dgin * k.tab[7] - (lr * dlr + li * dli)
            k.small_sum[16:32, :] = lr * dli - li * dlr
            k.small_sum[32:48, :] = k.tab[6] * dcr
            k.small_sum[48:64, :] = k.tab[6] * dci
            small_x.start()

    tasks[SMALL] = small
    at(DN1_X)
    s_dn1.near_half()
    at(DN1_1)
    s_dn1.far_half()
    at(DN1_2)
    s_dn1.end()

    def d_norm_one(i):
        rows = pl.ds(pl.multiple_of(i * 16, 16), 16)
        here = pl.ds(pl.multiple_of(x * 32 + i * 16, 16), 16)
        a = k.tok[here, :].astype(F32)
        s = lax.rsqrt(jnp.mean(a * a, axis=-1, keepdims=True) + EPSILON)
        hat = a * s
        dn = s_dn1.result(rows)
        dng = dn * k.gains[0:1, :]
        k.gt[here, :] = (
            k.dhf[rows, :] + s * (dng - hat * jnp.mean(dng * hat, axis=-1, keepdims=True))
        ).astype(BF16)
        t = jnp.sum(dn * hat, axis=0, keepdims=True)

        @pl.when(i == 0)
        def _():
            k.ggain[0:1, :] = t

        @pl.when(i > 0)
        def _():
            k.ggain[0:1, :] += t
    loop(2, d_norm_one)
    g_gt = CrossGather(r, k.gt, False, S.cg.at[3], R.cg.at[3])
    g_gt.begin()

    def piece(ref, width):
        return lambda i: ref.at[:, pl.ds(pl.multiple_of(i * width, width), width)]

    gg_1 = trade(0, piece(k.ggain, 512), k.gg_z)
    gg_2 = trade(1, piece(k.gg_1, 128), k.gg_y)
    gg_3 = trade(2, k.gg_s, k.gg_x)
    gg_sib = remote(k.gg_2, k.gg_s, S.gg_s, R.gg_s, r.sib)
    gg_1.begin()
    k.gg_z[z] = k.ggain[:, span(z * 512, 512)]
    at(GT_0)
    gg_1.end()
    k.gg_1[...] = sum(k.gg_z[j] for j in range(4))
    gg_2.begin()
    k.gg_y[y] = k.gg_1[:, span(y * 128, 128)]
    at(GT_1)
    g_gt.middle()
    at(GT_2)
    gg_2.end()
    k.gg_2[...] = sum(k.gg_y[j] for j in range(4))
    gg_sib.start()
    at(GT_3)
    gg_sib.wait()
    k.gg_s[...] = k.gg_s[...] + k.gg_2[...]
    gg_3.begin()
    k.gg_x[x] = k.gg_s[...]
    g_gt.end()
    out_gt = pltpu.make_async_copy(k.gt, k.grad_tok, local.at[1])
    out_gt.start()
    at(GT_4)
    small_x.wait()
    gg_3.end()
    k.gg_out[...] = sum(k.gg_x[j] for j in range(4))

    for n in range(S_IN, 11):
        both = k.other.at[:, 0:SECOND[n - S_IN][0][1] + SECOND[n - S_IN][1][1]]
        waiting(both, S.rs_sib.at[n - S_IN]).wait_send()
        waiting(both, R.rs_sib.at[n - S_IN]).wait_recv()
        for h in range(2):
            (ref, here, at), (o, w) = finished(n, h), SECOND[n - S_IN][h]
            there = pl.ds(o + (LANES_A if h else 0), w)
            pltpu.make_async_copy(ref.at[z, y, my64, here], k.grad_w.at[0, :, there], local.at[2]).start()
            pltpu.make_async_copy(sib_bufs[h].at[:, at], k.grad_w.at[1, :, there], local.at[2]).start()
    for j, src in enumerate((k.small_sum, k.small_sib)):
        pltpu.make_async_copy(src, k.grad_small.at[j], local.at[3]).start()
    out_gain = pltpu.make_async_copy(k.gg_out, k.grad_gain, local.at[4])
    out_gain.start()
    out_bo.wait()
    out_gt.wait()
    pltpu.make_async_copy(k.grad_w, k.grad_w, local.at[2]).wait()
    pltpu.make_async_copy(k.grad_small, k.grad_small, local.at[3]).wait()
    out_gain.wait()
    for n in (A_IN, A_REST):
        waiting(k.other.at[:, 0:(768, 2432)[n]], S.w_sib.at[n]).wait_send()
    for piece in sum(gather + scatter, []):
        piece.drain()
    for copy in [gain_sib, keep_sib, gy_sib, n1_sib, edge]:
        copy.wait_send()
    for group in trades + [s_dn1, g_n2, g_bo, g_dh, g_gt]:
        group.drain()


def block(*arrays):
    sems = []
    for _, shape in fields(Sems):
        sems += [pltpu.SemaphoreType.DMA(a) for a in shape]
    vmem = pl.BlockSpec(memory_space=pltpu.VMEM)
    return pl.pallas_call(
        kernel,
        out_shape=(
            jax.ShapeDtypeStruct((128, 2048), BF16),
            jax.ShapeDtypeStruct((128, 2048), BF16),
            jax.ShapeDtypeStruct((2, 64, LANES_A + LANES_B), BF16),
            jax.ShapeDtypeStruct((2, 80, 256), F32),
            jax.ShapeDtypeStruct((8, 128), F32),
        ),
        in_specs=[vmem] * len(arrays),
        out_specs=[pl.BlockSpec(memory_space=pl.ANY)] * 5,
        scratch_shapes=[pltpu.VMEM(*value) for _, value in fields(Scratch)] + sems + [pltpu.SemaphoreType.DMA((5,))],
        compiler_params=pltpu.CompilerParams(
            collective_id=0, has_side_effects=True, vmem_limit_bytes=63 * 2**20
        ),
        name="block",
    )(*arrays)


def results(*refs):
    sources, refs = refs[:5], refs[5:]
    (bo, gt, g_gain_1, g_in, g_taps, g_decay, g_angle, g_re, g_im, g_out, g_gain_2, g_gate, g_up, g_down) = refs[:14]
    grad_w, small, gain, sems = refs[14:]
    c = lax.rem(lax.axis_index("seq"), 2)
    copies = [
        pltpu.make_async_copy(source, ref, sems.at[i])
        for i, (source, ref) in enumerate(zip(sources, (bo, gt, grad_w, small, gain)))
    ]
    for copy in copies[::-1]:
        copy.start()
    for copy in copies[2:]:
        copy.wait()

    def cols(core, n, start, stop):
        wa = WHOLE[n][0][1]
        parts = []
        if start < wa:
            parts.append(grad_w[core, :, WHOLE[n][0][0] + start:WHOLE[n][0][0] + min(stop, wa)])
        if stop > wa:
            o = LANES_A + WHOLE[n][1][0]
            parts.append(grad_w[core, :, o + max(start - wa, 0):o + stop - wa])
        return jnp.concatenate(parts, 1).astype(F32)

    for at, core in ((0, c), (1, 1 - c)):
        g_in[0, :, at * 256:at * 256 + 256] = cols(core, IN, 0, 256)
        for b in (1, 2):
            g_in[b, :, at * 256:at * 256 + 256] = cols(core, IN_2, b * 256 - 256, b * 256)
        g_out[:, at * 256:at * 256 + 256] = cols(core, OUT, 0, 256)
        g_gate[:, at * 640:at * 640 + 640] = cols(core, GU, 0, 640)
        g_up[:, at * 640:at * 640 + 640] = cols(core, GU, 640, 1280)
        g_down[:, at * 640:at * 640 + 640] = cols(core, DOWN, 0, 640)
        here = slice(at * 256, at * 256 + 256)
        for i, ref in enumerate((g_decay, g_angle, g_re, g_im)):
            ref[:, here] = small[core, 16 * i:16 * i + 16, :]
        for i in range(3):
            g_taps[i, :, here] = small[core, 64 + 3 * i:67 + 3 * i, :]
    first, second = cols(c, GU, 1280, 1408), cols(1 - c, GU, 1280, 1408)
    g_gate[:, 1280:1408] = jnp.concatenate([first[:, 0:64], second[:, 0:64]], 1)
    g_up[:, 1280:1408] = jnp.concatenate([first[:, 64:128], second[:, 64:128]], 1)
    first, second = cols(c, DOWN, 640, 768), cols(1 - c, DOWN, 640, 768)
    g_down[:, 1280:1408] = jnp.concatenate([first[:, 0:64], second[:, 0:64]], 1)
    for i, ref in enumerate((g_gain_1, g_gain_2)):
        a = gain[i:i + 1, :]
        ref[...] = jnp.where(c == 0, a[:, 0:64], a[:, 64:128])
    for copy in copies[:2]:
        copy.wait()


def on_device(
    tokens, cotangent, resets, norm1_gain, in_weight, conv_weight, pole_decay, pole_angle, residue_re, residue_im,
    out_weight, norm2_gain, gate_weight, up_weight, down_weight,
):
    raw = block(
        in_weight.transpose(1, 0, 2), out_weight, gate_weight, up_weight, down_weight, norm1_gain.reshape(1, 64),
        norm2_gain.reshape(1, 64), resets.reshape(1, 128), tokens, cotangent, conv_weight, pole_decay, pole_angle,
        residue_re, residue_im,
    )
    vmem = pl.BlockSpec(memory_space=pltpu.VMEM)
    shapes = [
        ((128, 2048), BF16), ((128, 2048), BF16), ((1, 64), F32), ((3, 64, 512), F32), ((3, 3, 512), F32),
        ((16, 512), F32), ((16, 512), F32), ((16, 512), F32), ((16, 512), F32), ((64, 512), F32), ((1, 64), F32),
        ((64, 1408), F32), ((64, 1408), F32), ((64, 1408), F32),
    ]
    outs = list(pl.pallas_call(
        results,
        out_shape=[jax.ShapeDtypeStruct(s, t) for s, t in shapes],
        in_specs=[pl.BlockSpec(memory_space=pl.ANY)] * len(raw),
        out_specs=[vmem] * len(shapes),
        scratch_shapes=[pltpu.VMEM(a.shape, a.dtype) for a in raw[2:]] + [pltpu.SemaphoreType.DMA((5,))],
        compiler_params=pltpu.CompilerParams(vmem_limit_bytes=60 * 2**20),
        name="results",
    )(*raw))
    outs[2], outs[10] = outs[2].reshape(64), outs[10].reshape(64)
    outs[3] = outs[3].transpose(1, 0, 2)
    return tuple(outs)


def solution(mesh):
    row, cols = P("seq", "mp"), P(None, "mp")
    return jax.shard_map(
        on_device,
        mesh=mesh,
        in_specs=(
            P("seq", None), P("seq", None), P("seq"), P("seq"), P("seq", None, "mp"), P(None, None, "mp"),
            cols, cols, cols, cols, row, P("seq"), row, row, row,
        ),
        out_specs=(
            P("seq", None), P("seq", None), P("seq"), P("seq", None, "mp"), P(None, None, "mp"),
            cols, cols, cols, cols, row, P("seq"), row, row, row,
        ),
        check_vma=False,
    )
```

```python
import functools

import jax
import jax.numpy as jnp
from jax import lax
from jax.experimental import pallas as pl
from jax.experimental.pallas import tpu as pltpu
from jax.sharding import PartitionSpec as P

EPSILON = 1e-05
BF16, F32 = jnp.bfloat16, jnp.float32
MESH = pl.DeviceIdType.MESH
LANES_A, LANES_B = 1664, 1536
CHUNKS = (
    ((0, 128), (0, 128)),
    ((128, 256), (128, 256)),
    ((384, 128), (384, 128)),
    ((512, 384), (512, 384)),
    ((896, 384), (896, 256)),
    ((1280, 384), (1152, 384)),
)
IN, IN_2, OUT, GU, GU_2, DOWN = range(6)
def pieces(a, b, last=False):
    both = [(0, 0, *a, 0, 128), (1, 1, *b, 0, 128)]
    return both + [(0, 0, 1536, 128, 0, 64), (1, 0, 1536, 128, 64, 64)] * last


GATHERS = (
    (0, False, pieces((0, 384), (0, 384))),
    (0, False, pieces((384, 1152), (384, 1152), True)),
    (1, True, pieces((0, 384), (0, 384))),
    (1, False, pieces((384, 128), (384, 128))),
    (1, True, pieces((512, 384), (512, 384))),
    (1, True, pieces((896, 384), (896, 256))),
    (1, True, pieces((1280, 256), (1152, 384), True)),
)
A_IN, A_REST, B_IN, B_OUT, B_GU, B_GU_2, B_DOWN = range(7)
SECOND = (CHUNKS[0], CHUNKS[1], CHUNKS[2], ((512, 768), (512, 640)), CHUNKS[5])
SCATTERS = [pieces(*parts) for parts in CHUNKS[:5] + SECOND[:4]]
SCATTERS = SCATTERS[:5] + [pieces((1280, 256), (1152, 384), True)] + SCATTERS[5:] + [pieces((1280, 256), (1152, 384), True)]
S_IN, S_IN_2, S_OUT, S_GU, S_DOWN = range(6, 11)
WHOLE = {n: CHUNKS[n] for n in (IN, IN_2, OUT, DOWN)} | {GU: ((512, 768), (512, 640))}


def where():
    place = lax.axis_index("seq")
    chip = place // 2
    return chip // 4, lax.rem(chip, 4), lax.rem(place, 2), lax.axis_index("mp")


def device(z, y, c, x):
    return ((z * 4 + y) * 2 + c, x)


def rem4(a):
    return lax.rem(a + 4, 4)


def remote(src, dst, send, recv, to):
    return pltpu.make_async_remote_copy(
        src_ref=src, dst_ref=dst, send_sem=send, recv_sem=recv, device_id=to, device_id_type=MESH
    )


def waiting(ref, sem):
    return remote(ref, ref, sem, sem, device(0, 0, 0, 0))


def nn(a, b):
    return jnp.dot(a, b, preferred_element_type=F32)


def nt(a, b):
    return lax.dot_general(a, b, (((1,), (1,)), ((), ())), preferred_element_type=F32)


def tn(a, b):
    return lax.dot_general(a, b, (((0,), (0,)), ((), ())), preferred_element_type=F32)


def expm1(x):
    series = x / 8.0 + 1.0
    for n in range(7, 1, -1):
        series = series * (x / n) + 1.0
    return jnp.where(jnp.abs(x) < 0.25, x * series, jnp.exp(x) - 1.0)


def fold(count, body, state):
    return lax.fori_loop(0, count, body, state)


def loop(count, body):
    lax.fori_loop(0, count, lambda i, _: (body(i), 0)[1], 0)


def span(start, size):
    return pl.ds(pl.multiple_of(start, size), size)


(
    START, GAIN_Y, GAIN_Z, NORM_1, EDGE, PROJECT, SHORT, ENDS_Y,
    ENDS_Z, SCAN, MIX, MIX_0, MIX_1, MIX_2, N2_0, N2_1,
    FF, ACT, DA, DN2_0, DN2_1, DN2_2, DH_0, DH_1,
    DZ, BACKS_Y, BACKS_Z, ADJOINT, DQ, DN1_0, DN1_X, DN1_1,
    DN1_2, GT_0, GT_1, GT_2, GT_3, GT_4,
) = range(38)
AG, RS, WG, FFN, SMALL, SHORT_1 = range(6)
PLAN = {
    START: ((AG, A_IN, 1),),
    GAIN_Y: ((AG, A_REST, 1), (AG, A_IN, 3),),
    GAIN_Z: ((AG, A_REST, 3), (AG, A_IN, 4), (AG, B_IN, 1), (AG, B_IN, 2),),
    EDGE: ((AG, B_IN, 3),),
    PROJECT: ((AG, A_REST, 4), (AG, B_OUT, 1), (AG, B_GU_2, 1), (AG, B_IN, 4),),
    ENDS_Y: ((AG, B_DOWN, 1),),
    ENDS_Z: ((AG, B_OUT, 3), (AG, B_GU_2, 2), (AG, B_GU, 1), (AG, B_GU_2, 3),),
    MIX: ((AG, B_OUT, 4),),
    MIX_2: ((AG, B_GU, 2), (AG, B_GU, 3),),
    N2_0: ((AG, B_DOWN, 2), (AG, B_DOWN, 3), (AG, B_GU_2, 4),),
    FF: ((AG, B_GU, 4),),
    ACT: ((WG, DOWN), (RS, DOWN, 0), (RS, DOWN, 1), (AG, B_DOWN, 4),),
    DN2_1: ((RS, DOWN, 2), (WG, GU),),
    DN2_2: ((RS, GU, 0), (RS, GU_2, 0), (FFN, 0), (RS, GU, 1),),
    DH_1: ((RS, GU_2, 1), (FFN, 1),),
    BACKS_Y: ((RS, GU, 2), (RS, DOWN, 3), (SHORT_1,), (WG, IN),),
    BACKS_Z: ((RS, IN, 0), (FFN, 2), (WG, OUT), (RS, GU_2, 2), (RS, OUT, 0), (FFN, 3), (RS, OUT, 1),),
    DQ: ((RS, IN, 1), (RS, IN, 2), (RS, GU_2, 3), (RS, GU, 3), (RS, S_GU, 0), (RS, OUT, 2),),
    DN1_0: ((WG, IN_2), (RS, IN_2, 0), (RS, IN_2, 1),),
    DN1_1: ((SMALL, 0),),
    DN1_2: ((RS, IN, 3), (RS, S_IN, 0), (RS, OUT, 3), (RS, IN_2, 2),),
    GT_0: ((RS, S_DOWN, 0), (SMALL, 1), (FFN, 4),),
    GT_2: ((RS, S_OUT, 0), (RS, IN_2, 3), (RS, S_IN_2, 0), (RS, S_GU, 1), (RS, S_DOWN, 1), (RS, S_IN, 1),),
    GT_3: ((RS, S_IN_2, 1), (SMALL, 2),),
    GT_4: ((RS, S_OUT, 1), (RS, S_GU, 2), (FFN, 5), (RS, S_DOWN, 2), (RS, S_IN_2, 2), (RS, S_IN, 2),
        (RS, S_OUT, 2),),
}


class Rings:
    def __init__(self):
        self.z, self.y, self.c, self.x = where()
        self.chip = self.z * 4 + self.y
        self.sib = device(self.z, self.y, 1 - self.c, self.x)

    def near(self, axis, d, other=False):
        c = 1 - self.c if other else self.c
        if axis == 0:
            return device(rem4(self.z + d), self.y, c, self.x)
        if axis == 1:
            return device(self.z, rem4(self.y + d), c, self.x)
        return device(self.z, self.y, c, rem4(self.x + d))

    def along(self, d):
        return (lax.rem(self.chip + d + 16, 16) * 2 + self.c, self.x)


class Gather:
    def __init__(self, r, ref, lanes, rows, phase, axis, split, send, recv, own=None):
        self.r, self.ref, self.lanes, self.rows, self.own = r, ref, lanes, rows, own
        self.phase, self.axis, self.split = phase, axis, split
        self.send, self.recv, self.sent = send, recv, []

    def copy(self, d, part, to, i):
        r, axis = self.r, self.axis
        z, y = (rem4(r.z + d), r.y) if axis == 0 else (r.z, rem4(r.y + d))
        if self.phase == 0:
            o, n = self.rows
            rows = (pl.ds(o, n), pl.ds(o, n // 2), pl.ds(o + n // 2, n // 2))[part]
            ref = self.ref.at[z, y, rows, self.lanes]
        else:
            many, rows = (pl.ds(0, 4), pl.ds(0, 2), pl.ds(2, 2))[part], pl.ds(*self.rows)
            ref = self.ref.at[z, many, rows, self.lanes] if axis == 0 else self.ref.at[many, y, rows, self.lanes]
        return remote(ref, ref, self.send, self.recv.at[i], r.near(axis, to))

    def start(self, *a):
        copy = self.copy(*a)
        copy.start()
        self.sent.append(copy)

    def step(self, i):
        if i == 1 and self.own:
            there = self.ref.at[self.r.z, self.r.y, self.own[1], self.lanes]
            for j, d in enumerate((1, -1)):
                for other, src in enumerate((there, self.own[0])):
                    to = self.r.near(self.axis, d, bool(other))
                    self.sent.append(remote(src, there, self.send, self.recv.at[j], to))
                    self.sent[-1].start()
        elif i == 1 and not self.split:
            self.start(0, 0, 1, 0)
            self.start(0, 0, -1, 1)
        elif i == 1:
            self.start(0, 1, 1, 0)
            self.start(0, 2, -1, 1)
        elif i == 2 and not self.split:
            pass
        elif i == 2:
            self.start(0, 2, 1, 2)
            self.start(0, 1, -1, 2)
        elif i == 3:
            self.copy(-1, 1 if self.split else 0, 1, 0).wait_recv()
            self.start(-1, 1, 1, 2)
            self.copy(1, 2 if self.split else 0, -1, 1).wait_recv()
            self.start(1, 2, -1, 2)
        else:
            waiting(self.units(2 if self.split else 1), self.recv.at[2]).wait_recv()

    def units(self, count):
        rows = pl.ds(*self.rows)
        if self.phase == 0:
            return self.ref.at[0, pl.ds(0, count), rows, self.lanes]
        return self.ref.at[pl.ds(0, count), :, rows, self.lanes]

    def drain(self):
        if self.sent:
            waiting(self.units(3), self.send).wait_send()
        self.sent = []


class Trade:
    def __init__(self, r, axis, src, land, send, recv):
        self.r, self.axis, self.src, self.land, self.send, self.recv = r, axis, src, land, send, recv
        self.me, self.sent = (r.z, r.y, r.x)[axis], []

    def copy(self, d):
        return remote(
            self.src(rem4(self.me + d)), self.land.at[self.me], self.send, self.recv,
            self.r.near(self.axis, d),
        )

    def begin(self):
        for d in (2, 1, 3):
            copy = self.copy(d)
            copy.start()
            self.sent.append(copy)

    def end(self):
        waiting(self.land.at[0:3], self.recv).wait_recv()

    def drain(self):
        if self.sent:
            waiting(self.land.at[0:3], self.send).wait_send()


class Scatter:
    def __init__(self, r, ref, lanes, rows, at, phase, axis, buf, send, recv):
        self.r, self.ref, self.lanes, self.rows, self.at = r, ref, lanes, rows, at
        self.phase, self.axis, self.buf, self.send, self.recv, self.sent = phase, axis, buf, send, recv, []

    def unit(self, d, part):
        r, axis = self.r, self.axis
        z, y = (rem4(r.z + d), r.y) if axis == 0 else (r.z, rem4(r.y + d))
        if self.phase == 1:
            o, n = self.rows
            return self.ref.at[z, y, pl.ds(o + n // 2 * part, n // 2), self.lanes]
        many, rows = pl.ds(2 * part, 2), pl.ds(*self.rows)
        return self.ref.at[z, many, rows, self.lanes] if axis == 0 else self.ref.at[many, y, rows, self.lanes]

    def landing(self, i):
        o, n = self.rows
        if self.phase == 0:
            return self.buf.at[i, :, pl.ds(o, n), self.at]
        return self.buf.at[i, pl.ds(o // 2, n // 2), self.at]

    def copy(self, d, part, to, i):
        return remote(
            self.unit(d, part), self.landing(i), self.send, self.recv.at[min(i, 2)],
            self.r.near(self.axis, to),
        )

    def start(self, *a):
        copy = self.copy(*a)
        copy.start()
        self.sent.append(copy)

    def arrived(self, i):
        self.copy(0, 0, 1, i).wait_recv()

    def add(self, d, part, many):
        unit = self.unit(d, part)
        lands, many = [self.landing(i) for i in many], self.rows[1] // 32
        if self.phase == 0:
            def body(i):
                k, rows = i // many, span(lax.rem(i, many) * 32, 32)
                total = unit[k, rows, :].astype(F32)
                for l in lands:
                    total = total + l[k, rows, :].astype(F32)
                unit[k, rows, :] = total.astype(BF16)
            loop(2 * many, body)
        else:
            def body(i):
                rows = span(i * 32, 32)
                total = unit[rows, :].astype(F32)
                for l in lands:
                    total = total + l[rows, :].astype(F32)
                unit[rows, :] = total.astype(BF16)
            loop(many // 2, body)

    def far(self):
        self.start(2, 0, 1, 0)
        self.start(2, 1, -1, 1)

    def early(self):
        self.start(1, 1, 1, 3)
        self.start(-1, 0, -1, 4)

    def forward(self):
        self.arrived(0)
        self.add(1, 0, (0,))
        self.start(1, 0, 1, 2)
        self.arrived(1)
        self.add(-1, 1, (1,))
        self.start(-1, 1, -1, 5)

    def units(self, count):
        o, n = self.rows
        if self.phase == 0:
            return self.buf.at[pl.ds(0, 2 * count), :, pl.ds(o, n), self.at]
        return self.buf.at[pl.ds(0, 2 * count), pl.ds(o // 2, n // 2), self.at]

    def finish(self):
        waiting(self.units(2), self.recv.at[2]).wait_recv()
        self.add(0, 0, (2, 4))
        self.add(0, 1, (3, 5))

    def drain(self):
        if self.sent:
            waiting(self.units(3), self.send).wait_send()
        self.sent = []


class CrossSum:
    def __init__(self, r, part, got, mid, one, two, send, recv):
        self.r, self.part, self.got, self.mid, self.one, self.two = r, part, got, mid, one, two
        self.send, self.recv, self.sent = send, recv, []

    def start(self, copy):
        copy.start()
        self.sent.append(copy)

    def rows(self, c, x):
        return span((c * 4 + x) * 32, 32)

    def pair(self, d):
        x = rem4(self.r.x + d)
        return remote(
            self.part.at[self.rows(1 - self.r.c, x)], self.got.at[x],
            self.send, self.recv.at[(4, 1, 0, 1)[d]], self.r.sib,
        )

    def begin(self):
        for d in (2, 1, 3, 0):
            self.start(self.pair(d))

    def pairsum(self, d):
        x = rem4(self.r.x + d)
        rows = self.rows(self.r.c, x)
        self.mid[x] = (self.part[rows].astype(F32) + self.got[x].astype(F32)).astype(BF16)

    def far(self, side):
        x = rem4(self.r.x + 2)
        return remote(
            self.mid.at[x, pl.ds(16 * side, 16)], self.one.at[side],
            self.send, self.recv.at[2 + side], self.r.near(2, 1 - 2 * side),
        )

    def late(self, side, summed):
        d = 1 - 2 * side
        x = rem4(self.r.x + d)
        half = side if summed else 1 - side
        return remote(
            self.mid.at[x, pl.ds(16 * half, 16)], self.two.at[side, pl.ds(16 * half, 16)],
            self.send, self.recv.at[4], self.r.near(2, d),
        )

    def middle(self):
        self.near_half()
        self.far_half()

    def near_half(self):
        self.pair(2).wait_recv()
        self.pairsum(2)
        self.start(self.far(0))
        self.start(self.far(1))
        waiting(self.part.at[0:64], self.recv.at[1]).wait_recv()
        self.pairsum(1)
        self.start(self.late(0, 0))
        self.pairsum(3)
        self.start(self.late(1, 0))

    def far_half(self):
        for side in range(2):
            self.far(side).wait_recv()
            x = rem4(self.r.x + 1 - 2 * side)
            rows = pl.ds(16 * side, 16)
            self.mid[x, rows] = (self.mid[x, rows].astype(F32) + self.one[side].astype(F32)).astype(BF16)
            self.start(self.late(side, 1))

    def end(self):
        waiting(self.part.at[0:96], self.recv.at[4]).wait_recv()

    def result(self, rows):
        base = (self.r.c * 4 + self.r.x) * 32
        own = self.part[pl.ds(pl.multiple_of(base + rows.start, rows.size), rows.size)].astype(F32)
        own = own + self.got[self.r.x, rows].astype(F32)
        return own + self.two[0, rows].astype(F32) + self.two[1, rows].astype(F32)

    def drain(self):
        if self.sent:
            waiting(self.part.at[0:224], self.send).wait_send()
        self.sent = []


class CrossGather:
    def __init__(self, r, ref, both, send, recv):
        self.r, self.ref, self.both, self.send, self.recv, self.sent = r, ref, both, send, recv, []

    def start(self, copy):
        copy.start()
        self.sent.append(copy)

    def rows(self, d, part):
        base = rem4(self.r.x + d) * 32
        if self.both:
            base = base + self.r.c * 128
        if part is None:
            return self.ref.at[pl.ds(pl.multiple_of(base, 32), 32)]
        return self.ref.at[pl.ds(pl.multiple_of(base + 16 * part, 16), 16)]

    def ring(self, d, part, to, i):
        ref = self.rows(d, part)
        return remote(ref, ref, self.send, self.recv.at[i], self.r.near(2, to))

    def pair(self, d):
        ref = self.rows(d, None)
        return remote(ref, ref, self.send, self.recv.at[4], self.r.sib)

    def begin(self):
        self.start(self.ring(0, 0, 1, 0))
        self.start(self.ring(0, 1, -1, 1))
        self.start(self.ring(0, 1, 1, 2))
        self.start(self.ring(0, 0, -1, 2))
        if self.both:
            self.start(self.pair(0))

    def middle(self):
        self.ring(-1, 0, 1, 0).wait_recv()
        self.start(self.ring(-1, 0, 1, 3))
        self.ring(1, 1, -1, 1).wait_recv()
        self.start(self.ring(1, 1, -1, 3))
        waiting(self.ref.at[0:32], self.recv.at[2]).wait_recv()
        if self.both:
            self.start(self.pair(-1))
            self.start(self.pair(1))

    def end(self):
        waiting(self.ref.at[0:32], self.recv.at[3]).wait_recv()
        if self.both:
            self.start(self.pair(2))
            waiting(self.ref.at[0:128], self.recv.at[4]).wait_recv()

    def drain(self):
        waiting(self.ref.at[0:224 if self.both else 96], self.send).wait_send()


class Refs:
    pass


class Inputs:
    in_w = out_w = gate_w = up_w = down_w = gain_1 = gain_2 = resets = tok = cot = conv_w = 0
    decay = angle = res_re = res_im = 0


class Outputs:
    block_out = grad_tok = grad_w = grad_small = grad_gain = 0


class Scratch:
    other = ((64, LANES_A + LANES_B), BF16)
    tab = ((8, 16, 256), F32)
    ga = ((4, 4, 128, LANES_A), BF16)
    gb = ((4, 4, 128, LANES_B), BF16)
    s0a = ((6, 2, 128, LANES_A), BF16)
    s0b = ((6, 2, 128, LANES_B), BF16)
    s1a = ((6, 64, LANES_A), BF16)
    s1b = ((6, 64, LANES_B), BF16)
    da = ((4, 4, 128, 384), BF16)
    ia = ((4, 4, 128, 128), BF16)
    ib = ((4, 4, 128, 128), BF16)
    db = ((4, 4, 128, 384), BF16)
    sib_a = ((64, LANES_A), BF16)
    sib_b = ((64, LANES_B), BF16)
    gain_pair = ((2, 8, 128), F32)
    gains_y = ((4, 8, 128), F32)
    gains_all = ((4, 4, 8, 128), F32)
    gains = ((8, 2048), F32)
    gain_in = ((8, 128), F32)
    taps = ((8, 768), F32)
    keep = ((256, 256), F32)
    gy = ((256, 2048), BF16)
    n1 = ((272, 2048), BF16)
    n2 = ((256, 2048), BF16)
    dh = ((256, 2048), BF16)
    part = ((256, 2048), BF16)
    mid = ((4, 32, 2048), BF16)
    part_f = ((256, 2048), BF16)
    mid_f = ((4, 32, 2048), BF16)
    got = ((4, 4, 32, 2048), BF16)
    one = ((4, 2, 16, 2048), BF16)
    two = ((4, 2, 32, 2048), BF16)
    bo = ((128, 2048), BF16)
    gt = ((128, 2048), BF16)
    h = ((32, 2048), F32)
    dhf = ((32, 2048), F32)
    p = ((272, 768), F32)
    q0 = ((256, 256), F32)
    q1 = ((256, 256), F32)
    q2 = ((256, 256), F32)
    u = ((256, 256), F32)
    v = ((256, 256), F32)
    z = ((256, 256), BF16)
    st_re = ((257, 16, 256), F32)
    st_im = ((257, 16, 256), F32)
    ends_y = ((4, 32, 256), BF16)
    ends_z = ((4, 32, 256), BF16)
    backs_y = ((4, 32, 256), BF16)
    backs_z = ((4, 32, 256), BF16)
    gu = ((256, 1408), F32)
    act = ((256, 768), BF16)
    dgu = ((256, 1408), BF16)
    dv = ((256, 256), F32)
    dq = ((264, 768), F32)
    dp = ((256, 768), BF16)
    small_y = ((4, 80, 256), BF16)
    small_z = ((4, 80, 256), BF16)
    small_sum = ((80, 256), F32)
    small_sib = ((80, 256), F32)
    ggain = ((8, 2048), F32)
    gg_z = ((4, 8, 512), F32)
    gg_1 = ((8, 512), F32)
    gg_y = ((4, 8, 128), F32)
    gg_2 = ((8, 128), F32)
    gg_s = ((8, 128), F32)
    gg_x = ((4, 8, 128), F32)
    gg_out = ((8, 128), F32)


def fields(group):
    return [(name, value) for name, value in vars(group).items() if name[0] != "_"]


class Sems:
    w = (18,), (18, 3)
    w_sib = (2,), (2,)
    gain_sib = keep_s = gy_s = n1_s = edge = dq_s = dq_1 = small_x = gg_s = (), ()
    trade = (11,), (11,)
    sum = (4,), (4, 5)
    cg = (4,), (4, 5)
    rs = (26,), (26, 3)
    rs_sib = (5,), (5,)


def kernel(*refs):
    names = [name for group in (Inputs, Outputs, Scratch) for name, _ in fields(group)]
    k, S, R = Refs(), Refs(), Refs()
    for name, ref in zip(names, refs):
        setattr(k, name, ref)
    rest = refs[len(names):]
    for i, (name, _) in enumerate(fields(Sems)):
        setattr(S, name, rest[2 * i])
        setattr(R, name, rest[2 * i + 1])
    local = rest[-1]
    r = Rings()
    g = (k.ga, k.gb)
    z, y, c, x = r.z, r.y, r.c, r.x

    barrier = pltpu.get_barrier_semaphore()
    peers = [r.sib] + [r.near(a, d) for a in range(3) for d in (1, 2, 3)] + [r.along(1), r.along(-1)]
    peers += [r.near(a, d, True) for a in range(2) for d in (1, -1)]
    for peer in peers:
        pl.semaphore_signal(barrier, inc=1, device_id=peer, device_id_type=MESH)

    def lanes(n, h):
        o, w = CHUNKS[n][h]
        return pl.ds(o, w)

    def columns(n, start, stop):
        (oa, wa), (ob, _) = WHOLE[n]
        parts = []
        if start < wa:
            parts.append(g[0][:, :, :, oa + start:oa + min(stop, wa)])
        if stop > wa:
            parts.append(g[1][:, :, :, ob + max(start - wa, 0):ob + stop - wa])
        return jnp.concatenate([p.reshape(2048, p.shape[-1]) for p in parts], 1)

    def weight(n, h, i):
        o, w = WHOLE[n][h]
        return g[h][i, :, :, o:o + w].reshape(512, w)

    trades = []

    def trade(axis, src, land):
        i = len(trades)
        trades.append(Trade(r, axis, src if callable(src) else lambda _: src, land, S.trade.at[i], R.trade.at[i]))
        return trades[-1]

    my64 = span(c * 64, 64)
    my128 = span(c * 128, 128)
    gather = []
    for n, (phase, split, parts) in enumerate(GATHERS):
        first = sum(len(group) for group in gather)
        gather.append([
            Gather(r, g[b], pl.ds(o, w), rows, phase, 1 - way if phase == 0 else way, split and rows[1] == 128,
                   S.w.at[first + i], R.w.at[first + i],
                   (k.other.at[:, pl.ds(o + (LANES_A if b else 0), w)], my64) if n == A_IN else None)
            for i, (way, b, o, w, *rows) in enumerate(parts)
        ])

    def put(cc, n, sink):
        wa = WHOLE[n][0][1]

        def store(start, value):
            stop = start + value.shape[1]
            if start < wa:
                sink(0, WHOLE[n][0][0] + start, value[:, :min(stop, wa) - start])
            if stop > wa:
                sink(1, WHOLE[n][1][0] + max(start - wa, 0), value[:, max(wa - start, 0):])

        def main(ref):
            return ref[:, pl.ds(pl.multiple_of(cc * 640, 128), 640)]

        def tail(ref):
            a = ref[:, 1280:1408].astype(F32)
            return jnp.where(cc == 0, a[:, 0:64], a[:, 64:128])

        channels = pl.ds(pl.multiple_of(cc * 256, 256), 256)
        if n == IN:
            store(0, k.in_w[0, :, channels])
        elif n == IN_2:
            store(0, k.in_w[1, :, channels])
            store(256, k.in_w[2, :, channels])
        elif n == OUT:
            store(0, k.out_w[:, channels])
        elif n == GU:
            store(0, main(k.gate_w))
            store(640, main(k.up_w))
            store(1280, jnp.concatenate([tail(k.gate_w), tail(k.up_w)], 1).astype(BF16))
        else:
            store(0, main(k.down_w))
            store(640, jnp.concatenate([tail(k.down_w), jnp.zeros((64, 64), F32)], 1).astype(BF16))

    def to_other(h, at, value):
        at = at + (LANES_A if h else 0)
        k.other[:, at:at + value.shape[1]] = value

    def to_own(h, at, value):
        g[h][z, y, my64, at:at + value.shape[1]] = value

    def weight_sib(n, h):
        o, w = ((0, 384), (384, (1280, 1152)[h]))[n]
        return remote(
            k.other.at[:, pl.ds(o + (LANES_A if h else 0), w)], g[h].at[z, y, my64, pl.ds(o, w)],
            S.w_sib.at[n], R.w_sib.at[n], r.sib,
        )

    side = lax.broadcasted_iota(jnp.int32, (1, 128), 1) // 64 == c
    for i, ref in enumerate((k.gain_1, k.gain_2)):
        a = ref[...].astype(F32)
        k.gain_in[i:i + 1, :] = jnp.where(side, jnp.concatenate([a, a], 1), 0.0)
    k.gain_in[2:8, :] = jnp.zeros((6, 128), F32)
    for n in (IN, IN_2):
        put(1 - c, n, to_other)
        put(c, n, to_own)
    keep = 1.0 - k.resets[...].astype(F32)
    keep = jnp.broadcast_to(keep, (128, 128)).T
    k.keep[my128] = jnp.concatenate([keep, keep], 1)
    pl.semaphore_wait(barrier, len(peers))

    gain_sib = remote(k.gain_in, k.gain_pair.at[c], S.gain_sib, R.gain_sib, r.sib)
    keep_sib = remote(k.keep.at[my128], k.keep.at[my128], S.keep_s, R.keep_s, r.sib)
    gy_sib = remote(k.cot, k.gy.at[my128], S.gy_s, R.gy_s, r.sib)
    def share(n):
        for h in range(2):
            weight_sib(n, h).start()

    share(A_IN)
    gain_sib.start()

    def ag(n, i):
        if (n, i) in ((A_IN, 4), (A_REST, 1)):
            waiting(k.other.at[:, 0:(768, 2432)[n]], R.w_sib.at[n]).wait_recv()
        for piece in gather[n]:
            piece.step(i)

    tasks = {}

    def at(point):
        for name, *rest in PLAN.get(point, ()):
            tasks[name](*rest)

    tasks[AG] = ag
    at(START)
    gain_y = trade(1, k.gains_y.at[y], k.gains_y)
    gain_z = trade(0, k.gains_y, k.gains_all)
    gain_sib.wait_recv()
    k.gains_y[y] = k.gain_in[...] + k.gain_pair[1 - c]
    gain_y.begin()

    for n in (OUT, GU, DOWN):
        put(1 - c, n, to_other)
        put(c, n, to_own)
    share(A_REST)
    keep_sib.start()
    at(GAIN_Y)
    gain_y.end()
    gain_z.begin()
    k.gains_all[z] = k.gains_y[...]
    at(GAIN_Z)
    k.gy[my128] = k.cot[...]

    channels = pl.ds(pl.multiple_of(c * 256, 256), 256)
    decay, angle = k.decay[:, channels], k.angle[:, channels]
    size = jnp.exp(-decay)
    gin = jnp.sqrt(-expm1(-2.0 * decay))
    power = (size * jnp.cos(angle), size * jnp.sin(angle))
    k.tab[0], k.tab[1] = power
    k.tab[2] = gin * k.res_re[:, channels]
    k.tab[3] = gin * k.res_im[:, channels]
    for _ in range(8):
        power = (power[0] * power[0] - power[1] * power[1], 2.0 * power[0] * power[1])
    k.tab[4], k.tab[5] = power
    k.tab[6] = gin
    k.tab[7] = size * size / gin
    for i in range(3):
        for b in range(3):
            k.taps[i:i + 1, b * 256:b * 256 + 256] = k.conv_w[i, b:b + 1, channels]

    gain_z.end()
    for i in range(16):
        k.gains[:, i * 128:(i + 1) * 128] = k.gains_all[i // 4, i % 4]

    def norm_one(i):
        rows = span(i * 16, 16)
        a = k.tok[rows, :].astype(F32)
        s = lax.rsqrt(jnp.mean(a * a, axis=-1, keepdims=True) + EPSILON)
        k.n1[pl.ds(pl.multiple_of(16 + c * 128 + i * 16, 16), 16), :] = (a * s * k.gains[0:1, :]).astype(BF16)
    loop(8, norm_one)

    def n1_rows(c):
        return k.n1.at[pl.ds(pl.multiple_of(16 + c * 128, 16), 128)]

    n1_sib = remote(n1_rows(c), n1_rows(c), S.n1_s, R.n1_s, r.sib)
    n1_sib.start()
    at(NORM_1)
    k_other = span((1 - c) * 128, 128)
    remote(n1_rows(1 - c), n1_rows(1 - c), S.n1_s, R.n1_s, r.sib).wait_recv()
    edge = remote(k.n1.at[256:272], k.n1.at[0:16], S.edge, R.edge, r.along(1))
    edge.start()
    gy_sib.start()
    at(EDGE)

    edge.wait_recv()
    at(PROJECT)

    def project(_):
        for o in range(0, 512, 256):
            k.p[:, 256 + o:512 + o] = nn(k.n1[...], columns(IN_2, o, o + 256))
        k.p[:, 0:256] = nn(k.n1[...], columns(IN, 0, 256))
    loop(1, project)

    def round_p(i):
        rows = span(i * 16, 16)
        k.p[rows, :] = k.p[rows, :].astype(BF16).astype(F32)
    loop(17, round_p)
    remote(k.keep.at[k_other], k.keep.at[k_other], S.keep_s, R.keep_s, r.sib).wait_recv()
    at(SHORT)

    def masks(i):
        rows = span(i * 16, 16)
        near = k.keep[rows, :]
        before = k.keep[span(jnp.maximum(i * 16 - 8, 0), 8), :]
        first = jnp.where(i == 0, 1.0, before[7:8, :])
        shifted = jnp.concatenate([first, near[0:15, :]], 0)
        return near, near * shifted

    def short(i):
        near, far = masks(i)
        ext = k.p[pl.ds(pl.multiple_of(i * 16 + 8, 8), 24), :]
        q = []
        for b in range(3):
            l = slice(b * 256, b * 256 + 256)
            e = ext[:, l]
            q.append(
                k.taps[0:1, l] * e[8:24] + near * k.taps[1:2, l] * e[7:23] + far * k.taps[2:3, l] * e[6:22]
            )
        rows = span(i * 16, 16)
        k.q0[rows, :] = q[0]
        k.q1[rows, :] = q[1]
        k.q2[rows, :] = q[2]
        k.u[rows, :] = q[1] * q[2]
    loop(16, short)

    zero = jnp.zeros((16, 256), F32)
    lr, li, cr, ci, pr, pi = (k.tab[i] for i in range(6))

    def advance(re, im, u, keep):
        kr, ki = keep * re, keep * im
        return lr * kr - li * ki + u, lr * ki + li * kr

    def end_state(i, state):
        rows = span(i * 8, 8)
        u, keep = k.u[rows, :], k.keep[rows, :]
        for j in range(8):
            state = advance(*state, u[j:j + 1, :], keep[j:j + 1, :])
        return state

    def times(a, b, g, h):
        return a * g - b * h, a * h + b * g

    def chain(own, ref_y, ref_z, sign, between):
        order = range(4) if sign > 0 else range(3, -1, -1)
        qr, qi = pr, sign * pi

        def put(ref, at, state):
            ref[at, 0:16] = state[0].astype(BF16)
            ref[at, 16:32] = state[1].astype(BF16)

        def horner(ref, wr, wi, state, here, every):
            for i in order:
                nr, ni = times(wr, wi, *state)
                nr, ni = nr + ref[i, 0:16].astype(F32), ni + ref[i, 16:32].astype(F32)
                use = (i < here) if sign > 0 else (i > here)
                state = (nr, ni) if every else (jnp.where(use, nr, state[0]), jnp.where(use, ni, state[1]))
            return state

        put(ref_y, y, own)
        t = trade(1, ref_y.at[y], ref_y)
        t.begin()
        at(between[0])
        t.end()
        put(ref_z, z, horner(ref_y, qr, qi, (zero, zero), y, True))
        t = trade(0, ref_z.at[z], ref_z)
        t.begin()
        at(between[1])
        t.end()
        w = times(*times(qr, qi, qr, qi), *times(qr, qi, qr, qi))
        return horner(ref_y, qr, qi, horner(ref_z, *w, (zero, zero), z, False), y, False)

    end = fold(32, end_state, (zero, zero))
    enter = chain(end, k.ends_y, k.ends_z, 1, (ENDS_Y, ENDS_Z))
    k.st_re[0] = enter[0]
    k.st_im[0] = enter[1]
    at(SCAN)

    def scan(i, state):
        rows = span(i * 8, 8)
        u, keep = k.u[rows, :], k.keep[rows, :]
        for j in range(8):
            state = advance(*state, u[j:j + 1, :], keep[j:j + 1, :])
            k.st_re[i * 8 + j + 1] = state[0]
            k.st_im[i * 8 + j + 1] = state[1]
            k.v[pl.ds(i * 8 + j, 1), :] = jnp.sum(cr * state[0] - ci * state[1], axis=0, keepdims=True)
        return state
    fold(32, scan, enter)

    def gated(i):
        rows = span(i * 32, 32)
        k.z[rows, :] = (k.q0[rows, :] * k.v[rows, :]).astype(BF16)
    loop(8, gated)

    at(MIX)
    def out_weight(i):
        return jnp.concatenate([weight(OUT, 0, i), weight(OUT, 1, i)], 1)

    def mix(i):
        k.part[:, span(i * 512, 512)] = nt(k.z[...], out_weight(i)).astype(BF16)
    loop(4, mix)

    def cross(i):
        part, mid = (k.part_f, k.mid_f) if i == 1 else (k.part, k.mid)
        return CrossSum(r, part, k.got.at[i], mid, k.one.at[i], k.two.at[i], S.sum.at[i], R.sum.at[i])

    s_mix = cross(0)
    s_mix.begin()
    at(MIX_0)
    s_mix.near_half()
    at(MIX_1)
    s_mix.far_half()
    at(MIX_2)
    s_mix.end()

    own = (c * 4 + x) * 32

    def norm_two(i):
        rows = pl.ds(pl.multiple_of(i * 16, 16), 16)
        a = k.tok[pl.ds(pl.multiple_of(x * 32 + i * 16, 16), 16), :].astype(F32) + s_mix.result(rows)
        k.h[rows, :] = a
        s = lax.rsqrt(jnp.mean(a * a, axis=-1, keepdims=True) + EPSILON)
        k.n2[pl.ds(pl.multiple_of(own + i * 16, 16), 16), :] = (a * s * k.gains[1:2, :]).astype(BF16)
    loop(2, norm_two)
    g_n2 = CrossGather(r, k.n2, True, S.cg.at[0], R.cg.at[0])
    g_n2.begin()
    at(N2_0)
    g_n2.middle()
    at(N2_1)
    g_n2.end()
    s_mix.drain()
    at(FF)

    def gate_up(_):
        for o in range(0, 1408, 256):
            e = min(o + 256, 1408)
            k.gu[:, o:e] = nn(k.n2[...], columns(GU, o, e))
    loop(1, gate_up)
    def halves(t):
        last = t[:, 1280:1408]
        turned = jnp.concatenate([last[:, 64:128], last[:, 0:64]], 1)
        return jnp.concatenate([t[:, 0:640], last], 1), jnp.concatenate([t[:, 640:1280], turned], 1)

    used = lax.broadcasted_iota(jnp.int32, (1, 768), 1) < 704

    def activate(i):
        rows = span(i * 16, 16)
        gate, up = halves(k.gu[rows, :])
        k.act[rows, :] = jnp.where(used, gate * jax.nn.sigmoid(gate) * up, 0.0).astype(BF16)
    loop(16, activate)

    def down_weight(i):
        return jnp.concatenate([weight(DOWN, 0, i), weight(DOWN, 1, i)], 1)

    s_ffn = cross(1)
    g_bo = CrossGather(r, k.bo, False, S.cg.at[1], R.cg.at[1])
    out_bo = pltpu.make_async_copy(k.bo, k.block_out, local.at[0])

    def ffn_step(i):
        if i == 0:
            def ffn(i):
                k.part_f[:, span(i * 512, 512)] = nt(k.act[...], down_weight(i)).astype(BF16)
            loop(4, ffn)
            s_ffn.begin()
        elif i == 1:
            s_ffn.near_half()
        elif i == 2:
            s_ffn.far_half()
        elif i == 3:
            s_ffn.end()

            def top(i):
                rows = pl.ds(pl.multiple_of(i * 16, 16), 16)
                here = pl.ds(pl.multiple_of(x * 32 + i * 16, 16), 16)
                k.bo[here, :] = (k.h[rows, :] + s_ffn.result(rows)).astype(BF16)
            loop(2, top)
            s_ffn.drain()
            g_bo.begin()
        elif i == 4:
            g_bo.middle()
        else:
            g_bo.end()
            out_bo.start()

    tasks[FFN] = ffn_step

    apart = {DOWN: (k.da, k.db), IN: (k.ia, k.ib)}
    scatter = []
    for n, parts in enumerate(SCATTERS):
        phase = 0 if n < S_IN else 1
        m = {S_IN: IN, S_DOWN: DOWN}.get(n, n if phase == 0 else None)
        first = sum(len(group) for group in scatter)
        scatter.append([])
        for i, (way, b, o, w, *rows) in enumerate(parts):
            ref, here = g[b], pl.ds(o, w)
            if m in apart:
                ref, here = apart[m][b], pl.ds(o - CHUNKS[m][b][0], w)
            buf = ((k.s0a, k.s0b), (k.s1a, k.s1b))[phase][b]
            axis = 1 - way if phase == 0 else way
            scatter[n].append(
                Scatter(r, ref, here, rows, pl.ds(o, w), phase, axis, buf, S.rs.at[first + i], R.rs.at[first + i])
            )

    def finished(n, h):
        o, w = SECOND[n - S_IN][h]
        m = {S_IN: IN, S_DOWN: DOWN}.get(n)
        return (apart[m][h], pl.ds(0, w), pl.ds(o, w)) if m in apart else (g[h], pl.ds(o, w), pl.ds(o, w))

    sib_bufs = (k.sib_a, k.sib_b)

    def rs_sib(n, h):
        ref, here, at = finished(n, h)
        return remote(
            ref.at[z, y, span((1 - c) * 64, 64), here], sib_bufs[h].at[:, at],
            S.rs_sib.at[n - S_IN], R.rs_sib.at[n - S_IN], r.sib,
        )

    def rs(n, i):
        for s in scatter[n]:
            if n < S_IN:
                (s.far, s.early, s.forward, s.finish)[i]()
            elif i == 0:
                s.far()
                s.early()
            elif i == 1:
                s.forward()
            else:
                s.finish()
        if n >= S_IN and i == 2:
            for h in range(2):
                rs_sib(n, h).start()

    tasks[RS] = rs

    def wg(n):
        a, b, first = {
            IN: (k.n1, k.dp.at[:, 0:256], 16), IN_2: (k.n1, k.dp.at[:, 256:768], 16), OUT: (k.dh, k.z, 0),
            GU: (k.n2, k.dgu, 0), DOWN: (k.gy, k.act, 0),
        }[n]
        for m in {GU: (B_GU, B_GU_2), OUT: (B_OUT,), IN_2: (B_IN,)}.get(n, ()) + ((A_IN, A_REST) if n == GU else ()):
            for piece in gather[m]:
                piece.drain()
        (oa, wa), (ob, wb) = [(0, CHUNKS[n][h][1]) for h in range(2)] if n in apart else WHOLE[n]
        into = apart.get(n, g)

        def weight_grad(i):
            t = tn(a[pl.ds(first, 256), pl.ds(pl.multiple_of(i * 512, 512), 512)], b[...]).astype(BF16)
            into[0][i, :, :, oa:oa + wa] = t[:, 0:wa].reshape(4, 128, wa)
            into[1][i, :, :, ob:ob + wb] = t[:, wa:wa + wb].reshape(4, 128, wb)
        weight_grad.width = wa + wb
        loop(4, weight_grad)

    tasks[WG] = wg

    remote(k.gy.at[k_other], k.gy.at[k_other], S.gy_s, R.gy_s, r.sib).wait_recv()
    at(ACT)

    def d_act(_):
        for o in range(0, 768, 256):
            k.dq[0:256, o:o + 256] = nn(k.gy[...], columns(DOWN, o, o + 256))
    loop(1, d_act)
    at(DA)

    def d_gates(i):
        rows = span(i * 16, 16)
        gate, up = halves(k.gu[rows, :])
        da = k.dq[rows, :]
        sg = jax.nn.sigmoid(gate)
        dgate = da * up * sg * (1.0 + gate * (1.0 - sg))
        dup = da * (gate * sg)
        last = jnp.concatenate([dgate[:, 640:704], dup[:, 640:704]], 1)
        k.dgu[rows, :] = jnp.concatenate([dgate[:, 0:640], dup[:, 0:640], last], 1).astype(BF16)
    loop(16, d_gates)

    def d_n2(i):
        w = jnp.concatenate([weight(GU, 0, i), weight(GU, 1, i)], 1)
        k.part[:, span(i * 512, 512)] = nt(k.dgu[...], w).astype(BF16)
    loop(4, d_n2)
    s_dn2 = cross(2)
    s_dn2.begin()
    at(DN2_0)
    s_dn2.near_half()
    at(DN2_1)
    s_dn2.far_half()
    at(DN2_2)
    s_dn2.end()

    def d_norm_two(i):
        rows = pl.ds(pl.multiple_of(i * 16, 16), 16)
        a = k.h[rows, :]
        s = lax.rsqrt(jnp.mean(a * a, axis=-1, keepdims=True) + EPSILON)
        hat = a * s
        dn = s_dn2.result(rows)
        dng = dn * k.gains[1:2, :]
        gy = k.gy[pl.ds(pl.multiple_of(own + i * 16, 16), 16), :].astype(F32)
        dh = gy + s * (dng - hat * jnp.mean(dng * hat, axis=-1, keepdims=True))
        k.dhf[rows, :] = dh
        k.dh[pl.ds(pl.multiple_of(own + i * 16, 16), 16), :] = dh.astype(BF16)
        t = jnp.sum(dn * hat, axis=0, keepdims=True)

        @pl.when(i == 0)
        def _():
            k.ggain[...] = jnp.zeros((8, 2048), F32)
            k.ggain[1:2, :] = t

        @pl.when(i > 0)
        def _():
            k.ggain[1:2, :] += t
    loop(2, d_norm_two)
    s_dn2.drain()
    g_dh = CrossGather(r, k.dh, True, S.cg.at[2], R.cg.at[2])
    g_dh.begin()
    at(DH_0)
    g_dh.middle()
    at(DH_1)
    g_dh.end()
    at(DZ)

    def d_z(_):
        k.dv[...] = nn(k.dh[...], columns(OUT, 0, 256))
    loop(1, d_z)

    def d_gated(i):
        rows = span(i * 32, 32)
        dz = k.dv[rows, :]
        k.dq[rows, 0:256] = dz * k.v[rows, :]
        k.dv[rows, :] = dz * k.q0[rows, :]
    loop(8, d_gated)

    first = slice(0, 256)
    others = slice(256, 768)

    def dq_edge(at, send, recv):
        return remote(k.dq.at[0:8, at], k.dq.at[256:264, at], send, recv, r.along(-1))

    dq_first = dq_edge(first, S.dq_1, R.dq_1)
    dq_first.start()

    last = jnp.where(r.chip < 15, 1.0, 0.0)

    def d_short(i, taps, branches):
        near, far = masks(i)
        j = jnp.minimum(i * 16 + 16, 248)
        after = k.keep[span(j, 8), :]
        inside = i < 15
        tail_near = jnp.where(inside, after, last)
        tail_far = jnp.where(
            inside, after * jnp.concatenate([near[15:16, :], after[0:7, :]], 0), last
        )
        near = jnp.concatenate([near, tail_near], 0)
        far = jnp.concatenate([far, tail_far], 0)
        ext = k.p[pl.ds(pl.multiple_of(i * 16 + 8, 8), 24), :]
        rows = span(i * 16, 16)
        new = []
        for n, b in enumerate(branches):
            l = slice(b * 256, b * 256 + 256)
            e, db = ext[:, l], k.dq[pl.ds(pl.multiple_of(i * 16, 16), 24), l]
            dn, df = near * db, far * db
            k.dp[rows, l] = (
                k.taps[0:1, l] * db[0:16] + k.taps[1:2, l] * dn[1:17] + k.taps[2:3, l] * df[2:18]
            ).astype(BF16)
            new.append(taps[3 * n + 0] + jnp.sum(e[8:24] * db[0:16], axis=0, keepdims=True))
            new.append(taps[3 * n + 1] + jnp.sum(e[7:23] * dn[0:16], axis=0, keepdims=True))
            new.append(taps[3 * n + 2] + jnp.sum(e[6:22] * df[0:16], axis=0, keepdims=True))
        return tuple(new)

    line = jnp.zeros((1, 256), F32)
    def d_short_1(i, taps):
        return d_short(i, taps, (0,))

    def d_short_2(i, taps):
        return d_short(i, taps, (1, 2))

    d_taps = []

    def short_1():
        dq_first.wait()
        d_taps.extend(fold(16, d_short_1, (line,) * 3))

    tasks[SHORT_1] = short_1

    def retreat(a, b, keep):
        ka, kb = keep * a, keep * b
        return ka, kb, lr * ka + li * kb, lr * kb - li * ka

    def start_state(i, state):
        rows = span((31 - i) * 8, 8)
        dv, keep = k.dv[rows, :], k.keep[rows, :]
        for j in reversed(range(8)):
            a = cr * dv[j:j + 1, :] + state[0]
            b = state[1] - ci * dv[j:j + 1, :]
            _, _, pa, pb = retreat(a, b, keep[j:j + 1, :])
            state = (pa, pb)
        return state

    begin = fold(32, start_state, (zero, zero))
    arrive = chain(begin, k.backs_y, k.backs_z, -1, (BACKS_Y, BACKS_Z))
    at(ADJOINT)

    def adjoint(i, carry):
        rows = span((31 - i) * 8, 8)
        dv, keep = k.dv[rows, :], k.keep[rows, :]
        for j in reversed(range(8)):
            t = (31 - i) * 8 + j
            d = dv[j:j + 1, :]
            a = cr * d + carry[0]
            b = carry[1] - ci * d
            k.u[pl.ds(t, 1), :] = jnp.sum(a, axis=0, keepdims=True)
            _, _, pa, pb = retreat(a, b, keep[j:j + 1, :])
            carry = (pa, pb)
        return carry

    fold(32, adjoint, arrive)

    def d_poles(i, carry):
        pa, pb, dcr, dci, dlr, dli = carry
        rows = span((31 - i) * 8, 8)
        dv, keep = k.dv[rows, :], k.keep[rows, :]
        for j in reversed(range(8)):
            t = (31 - i) * 8 + j
            d = dv[j:j + 1, :]
            a = cr * d + pa
            b = pb - ci * d
            dcr = dcr + d * k.st_re[t + 1]
            dci = dci - d * k.st_im[t + 1]
            ka, kb, pa, pb = retreat(a, b, keep[j:j + 1, :])
            sr, si = k.st_re[t], k.st_im[t]
            dlr = dlr + ka * sr + kb * si
            dli = dli + kb * sr - ka * si
        return pa, pb, dcr, dci, dlr, dli

    def d_branches(i):
        rows = span(i * 32, 32)
        du = k.u[rows, :]
        k.dq[rows, 256:512] = du * k.q2[rows, :]
        k.dq[rows, 512:768] = du * k.q1[rows, :]
    loop(8, d_branches)
    dq_next = dq_edge(others, S.dq_s, R.dq_s)
    dq_next.start()
    at(DQ)
    dq_next.wait()
    d_taps.extend(fold(16, d_short_2, (line,) * 6))

    def d_n1(i):
        w = jnp.concatenate([weight(n, h, i) for n in (IN, IN_2) for h in range(2)], 1)
        k.part[:, span(i * 512, 512)] = nt(k.dp[...], w).astype(BF16)
    loop(4, d_n1)
    s_dn1 = cross(3)
    s_dn1.begin()
    at(DN1_0)

    small_1 = trade(1, k.small_y.at[y], k.small_y)
    small_2 = trade(0, k.small_z.at[z], k.small_z)

    def small_total(ref):
        return sum(ref[j].astype(F32) for j in range(4))

    small_x = remote(k.small_sum, k.small_sib, S.small_x, R.small_x, r.sib)

    def small(i):
        if i == 0:
            _, _, *dpoles = fold(32, d_poles, (*arrive, zero, zero, zero, zero))
            for j in range(4):
                k.small_y[y, 16 * j:16 * j + 16] = dpoles[j].astype(BF16)
            k.small_y[y, 64:80] = jnp.concatenate([d_taps[3 * b + t] for t in range(3) for b in range(3)] + [jnp.zeros((7, 256), F32)], 0).astype(BF16)
            small_1.begin()
        elif i == 1:
            small_1.end()
            k.small_z[z] = small_total(k.small_y).astype(BF16)
            small_2.begin()
        else:
            small_2.end()
            k.small_sum[...] = small_total(k.small_z)
            dcr, dci, dlr, dli = (k.small_sum[16 * j:16 * j + 16, :] for j in range(4))
            dgin = k.res_re[:, channels] * dcr + k.res_im[:, channels] * dci
            k.small_sum[0:16, :] = dgin * k.tab[7] - (lr * dlr + li * dli)
            k.small_sum[16:32, :] = lr * dli - li * dlr
            k.small_sum[32:48, :] = k.tab[6] * dcr
            k.small_sum[48:64, :] = k.tab[6] * dci
            small_x.start()

    tasks[SMALL] = small
    at(DN1_X)
    s_dn1.near_half()
    at(DN1_1)
    s_dn1.far_half()
    at(DN1_2)
    s_dn1.end()

    def d_norm_one(i):
        rows = pl.ds(pl.multiple_of(i * 16, 16), 16)
        here = pl.ds(pl.multiple_of(x * 32 + i * 16, 16), 16)
        a = k.tok[here, :].astype(F32)
        s = lax.rsqrt(jnp.mean(a * a, axis=-1, keepdims=True) + EPSILON)
        hat = a * s
        dn = s_dn1.result(rows)
        dng = dn * k.gains[0:1, :]
        k.gt[here, :] = (
            k.dhf[rows, :] + s * (dng - hat * jnp.mean(dng * hat, axis=-1, keepdims=True))
        ).astype(BF16)
        t = jnp.sum(dn * hat, axis=0, keepdims=True)

        @pl.when(i == 0)
        def _():
            k.ggain[0:1, :] = t

        @pl.when(i > 0)
        def _():
            k.ggain[0:1, :] += t
    loop(2, d_norm_one)
    g_gt = CrossGather(r, k.gt, False, S.cg.at[3], R.cg.at[3])
    g_gt.begin()

    def piece(ref, width):
        return lambda i: ref.at[:, pl.ds(pl.multiple_of(i * width, width), width)]

    gg_1 = trade(0, piece(k.ggain, 512), k.gg_z)
    gg_2 = trade(1, piece(k.gg_1, 128), k.gg_y)
    gg_3 = trade(2, k.gg_s, k.gg_x)
    gg_sib = remote(k.gg_2, k.gg_s, S.gg_s, R.gg_s, r.sib)
    gg_1.begin()
    k.gg_z[z] = k.ggain[:, span(z * 512, 512)]
    at(GT_0)
    gg_1.end()
    k.gg_1[...] = sum(k.gg_z[j] for j in range(4))
    gg_2.begin()
    k.gg_y[y] = k.gg_1[:, span(y * 128, 128)]
    at(GT_1)
    g_gt.middle()
    at(GT_2)
    gg_2.end()
    k.gg_2[...] = sum(k.gg_y[j] for j in range(4))
    gg_sib.start()
    at(GT_3)
    gg_sib.wait()
    k.gg_s[...] = k.gg_s[...] + k.gg_2[...]
    gg_3.begin()
    k.gg_x[x] = k.gg_s[...]
    g_gt.end()
    out_gt = pltpu.make_async_copy(k.gt, k.grad_tok, local.at[1])
    out_gt.start()
    at(GT_4)
    small_x.wait()
    gg_3.end()
    k.gg_out[...] = sum(k.gg_x[j] for j in range(4))

    for n in range(S_IN, 11):
        both = k.other.at[:, 0:SECOND[n - S_IN][0][1] + SECOND[n - S_IN][1][1]]
        waiting(both, S.rs_sib.at[n - S_IN]).wait_send()
        waiting(both, R.rs_sib.at[n - S_IN]).wait_recv()
        for h in range(2):
            (ref, here, at), (o, w) = finished(n, h), SECOND[n - S_IN][h]
            there = pl.ds(o + (LANES_A if h else 0), w)
            pltpu.make_async_copy(ref.at[z, y, my64, here], k.grad_w.at[0, :, there], local.at[2]).start()
            pltpu.make_async_copy(sib_bufs[h].at[:, at], k.grad_w.at[1, :, there], local.at[2]).start()
    for j, src in enumerate((k.small_sum, k.small_sib)):
        pltpu.make_async_copy(src, k.grad_small.at[j], local.at[3]).start()
    out_gain = pltpu.make_async_copy(k.gg_out, k.grad_gain, local.at[4])
    out_gain.start()
    out_bo.wait()
    out_gt.wait()
    pltpu.make_async_copy(k.grad_w, k.grad_w, local.at[2]).wait()
    pltpu.make_async_copy(k.grad_small, k.grad_small, local.at[3]).wait()
    out_gain.wait()
    for n in (A_IN, A_REST):
        waiting(k.other.at[:, 0:(768, 2432)[n]], S.w_sib.at[n]).wait_send()
    for piece in sum(gather + scatter, []):
        piece.drain()
    for copy in [gain_sib, keep_sib, gy_sib, n1_sib, edge]:
        copy.wait_send()
    for group in trades + [s_dn1, g_n2, g_bo, g_dh, g_gt]:
        group.drain()


def block(*arrays):
    sems = []
    for _, shape in fields(Sems):
        sems += [pltpu.SemaphoreType.DMA(a) for a in shape]
    vmem = pl.BlockSpec(memory_space=pltpu.VMEM)
    return pl.pallas_call(
        kernel,
        out_shape=(
            jax.ShapeDtypeStruct((128, 2048), BF16),
            jax.ShapeDtypeStruct((128, 2048), BF16),
            jax.ShapeDtypeStruct((2, 64, LANES_A + LANES_B), BF16),
            jax.ShapeDtypeStruct((2, 80, 256), F32),
            jax.ShapeDtypeStruct((8, 128), F32),
        ),
        in_specs=[vmem] * len(arrays),
        out_specs=[pl.BlockSpec(memory_space=pl.ANY)] * 5,
        scratch_shapes=[pltpu.VMEM(*value) for _, value in fields(Scratch)] + sems + [pltpu.SemaphoreType.DMA((5,))],
        compiler_params=pltpu.CompilerParams(
            collective_id=0, has_side_effects=True, vmem_limit_bytes=63 * 2**20
        ),
        name="block",
    )(*arrays)


def results(*refs):
    sources, refs = refs[:5], refs[5:]
    outs, refs = refs[:14], refs[14:]
    (bo, gt, g_gain_1, g_in, g_taps, g_decay, g_angle, g_re, g_im, g_out, g_gain_2, g_gate, g_up, g_down) = refs[:14]
    grad_w, small, gain, sems = refs[14:]
    c = lax.rem(lax.axis_index("seq"), 2)
    copies = [
        pltpu.make_async_copy(source, ref, sems.at[i])
        for i, (source, ref) in enumerate(zip(sources, (bo, gt, grad_w, small, gain)))
    ]
    leaving = [pltpu.make_async_copy(ref, out, sems.at[5 + i]) for i, (ref, out) in enumerate(zip(refs, outs))]
    for copy in copies[::-1]:
        copy.start()
    for copy in copies[2:]:
        copy.wait()

    def cols(core, n, start, stop):
        wa = WHOLE[n][0][1]
        parts = []
        if start < wa:
            parts.append(grad_w[core, :, WHOLE[n][0][0] + start:WHOLE[n][0][0] + min(stop, wa)])
        if stop > wa:
            o = LANES_A + WHOLE[n][1][0]
            parts.append(grad_w[core, :, o + max(start - wa, 0):o + stop - wa])
        return jnp.concatenate(parts, 1).astype(F32)

    cores = ((0, c), (1, 1 - c))
    for at, core in cores:
        g_in[0, :, at * 256:at * 256 + 256] = cols(core, IN, 0, 256)
        for b in (1, 2):
            g_in[b, :, at * 256:at * 256 + 256] = cols(core, IN_2, b * 256 - 256, b * 256)
    leaving[3].start()
    for at, core in cores:
        g_gate[:, at * 640:at * 640 + 640] = cols(core, GU, 0, 640)
        g_up[:, at * 640:at * 640 + 640] = cols(core, GU, 640, 1280)
    first, second = cols(c, GU, 1280, 1408), cols(1 - c, GU, 1280, 1408)
    g_gate[:, 1280:1408] = jnp.concatenate([first[:, 0:64], second[:, 0:64]], 1)
    g_up[:, 1280:1408] = jnp.concatenate([first[:, 64:128], second[:, 64:128]], 1)
    leaving[11].start()
    leaving[12].start()
    for copy in copies[:2]:
        copy.wait()
    leaving[0].start()
    leaving[1].start()
    for at, core in cores:
        g_down[:, at * 640:at * 640 + 640] = cols(core, DOWN, 0, 640)
    first, second = cols(c, DOWN, 640, 768), cols(1 - c, DOWN, 640, 768)
    g_down[:, 1280:1408] = jnp.concatenate([first[:, 0:64], second[:, 0:64]], 1)
    leaving[13].start()
    for at, core in cores:
        here = slice(at * 256, at * 256 + 256)
        g_out[:, here] = cols(core, OUT, 0, 256)
        for i, ref in enumerate((g_decay, g_angle, g_re, g_im)):
            ref[:, here] = small[core, 16 * i:16 * i + 16, :]
        for i in range(3):
            g_taps[i, :, here] = small[core, 64 + 3 * i:67 + 3 * i, :]
    for i, ref in enumerate((g_gain_1, g_gain_2)):
        a = gain[i:i + 1, :]
        ref[...] = jnp.where(c == 0, a[:, 0:64], a[:, 64:128])
    for i in (9, 4, 5, 6, 7, 8, 2, 10):
        leaving[i].start()
    for copy in leaving:
        copy.wait()


def on_device(
    tokens, cotangent, resets, norm1_gain, in_weight, conv_weight, pole_decay, pole_angle, residue_re, residue_im,
    out_weight, norm2_gain, gate_weight, up_weight, down_weight,
):
    raw = block(
        in_weight.transpose(1, 0, 2), out_weight, gate_weight, up_weight, down_weight, norm1_gain.reshape(1, 64),
        norm2_gain.reshape(1, 64), resets.reshape(1, 128), tokens, cotangent, conv_weight, pole_decay, pole_angle,
        residue_re, residue_im,
    )
    shapes = [
        ((128, 2048), BF16), ((128, 2048), BF16), ((1, 64), F32), ((3, 64, 512), F32), ((3, 3, 512), F32),
        ((16, 512), F32), ((16, 512), F32), ((16, 512), F32), ((16, 512), F32), ((64, 512), F32), ((1, 64), F32),
        ((64, 1408), F32), ((64, 1408), F32), ((64, 1408), F32),
    ]
    outs = list(pl.pallas_call(
        results,
        out_shape=[jax.ShapeDtypeStruct(s, t) for s, t in shapes],
        in_specs=[pl.BlockSpec(memory_space=pl.ANY)] * len(raw),
        out_specs=[pl.BlockSpec(memory_space=pl.ANY)] * len(shapes),
        scratch_shapes=[pltpu.VMEM(*a) for a in shapes] + [pltpu.VMEM(a.shape, a.dtype) for a in raw[2:]]
        + [pltpu.SemaphoreType.DMA((19,))],
        compiler_params=pltpu.CompilerParams(vmem_limit_bytes=60 * 2**20),
        name="results",
    )(*raw))
    outs[2], outs[10] = outs[2].reshape(64), outs[10].reshape(64)
    outs[3] = outs[3].transpose(1, 0, 2)
    return tuple(outs)


def solution(mesh):
    row, cols = P("seq", "mp"), P(None, "mp")
    return jax.shard_map(
        on_device,
        mesh=mesh,
        in_specs=(
            P("seq", None), P("seq", None), P("seq"), P("seq"), P("seq", None, "mp"), P(None, None, "mp"),
            cols, cols, cols, cols, row, P("seq"), row, row, row,
        ),
        out_specs=(
            P("seq", None), P("seq", None), P("seq"), P("seq", None, "mp"), P(None, None, "mp"),
            cols, cols, cols, cols, row, P("seq"), row, row, row,
        ),
        check_vma=False,
    )
```

```python
import functools

import jax
import jax.numpy as jnp
from jax import lax
from jax.experimental import pallas as pl
from jax.experimental.pallas import tpu as pltpu
from jax.sharding import PartitionSpec as P

EPSILON = 1e-05
BF16, F32 = jnp.bfloat16, jnp.float32
MESH = pl.DeviceIdType.MESH
LANES_A, LANES_B = 1664, 1536
CHUNKS = (
    ((0, 128), (0, 128)),
    ((128, 256), (128, 256)),
    ((384, 128), (384, 128)),
    ((512, 384), (512, 384)),
    ((896, 384), (896, 256)),
    ((1280, 384), (1152, 384)),
)
IN, IN_2, OUT, GU, GU_2, DOWN = range(6)
def pieces(a, b, last=False):
    both = [(0, 0, *a, 0, 128), (1, 1, *b, 0, 128)]
    return both + [(0, 0, 1536, 128, 0, 64), (1, 0, 1536, 128, 64, 64)] * last


GATHERS = (
    (0, False, pieces((0, 384), (0, 384))),
    (0, False, pieces((384, 1152), (384, 1152), True)),
    (1, True, pieces((0, 384), (0, 384))),
    (1, False, pieces((384, 128), (384, 128))),
    (1, True, pieces((512, 384), (512, 384))),
    (1, True, pieces((896, 384), (896, 256))),
    (1, True, pieces((1280, 256), (1152, 384), True)),
)
A_IN, A_REST, B_IN, B_OUT, B_GU, B_GU_2, B_DOWN = range(7)
SECOND = (CHUNKS[0], CHUNKS[1], CHUNKS[2], ((512, 768), (512, 640)), CHUNKS[5])
SCATTERS = [pieces(*parts) for parts in CHUNKS[:5] + SECOND[:4]]
SCATTERS = SCATTERS[:5] + [pieces((1280, 256), (1152, 384), True)] + SCATTERS[5:] + [pieces((1280, 256), (1152, 384), True)]
S_IN, S_IN_2, S_OUT, S_GU, S_DOWN = range(6, 11)
WHOLE = {n: CHUNKS[n] for n in (IN, IN_2, OUT, DOWN)} | {GU: ((512, 768), (512, 640))}


def where():
    place = lax.axis_index("seq")
    chip = place // 2
    return chip // 4, lax.rem(chip, 4), lax.rem(place, 2), lax.axis_index("mp")


def device(z, y, c, x):
    return ((z * 4 + y) * 2 + c, x)


def rem4(a):
    return lax.rem(a + 4, 4)


def remote(src, dst, send, recv, to):
    return pltpu.make_async_remote_copy(
        src_ref=src, dst_ref=dst, send_sem=send, recv_sem=recv, device_id=to, device_id_type=MESH
    )


def waiting(ref, sem):
    return remote(ref, ref, sem, sem, device(0, 0, 0, 0))


def nn(a, b):
    return jnp.dot(a, b, preferred_element_type=F32)


def nt(a, b):
    return lax.dot_general(a, b, (((1,), (1,)), ((), ())), preferred_element_type=F32)


def tn(a, b):
    return lax.dot_general(a, b, (((0,), (0,)), ((), ())), preferred_element_type=F32)


def expm1(x):
    series = x / 8.0 + 1.0
    for n in range(7, 1, -1):
        series = series * (x / n) + 1.0
    return jnp.where(jnp.abs(x) < 0.25, x * series, jnp.exp(x) - 1.0)


def fold(count, body, state):
    return lax.fori_loop(0, count, body, state)


def loop(count, body):
    lax.fori_loop(0, count, lambda i, _: (body(i), 0)[1], 0)


def span(start, size):
    return pl.ds(pl.multiple_of(start, size), size)


(
    START, GAIN_Y, GAIN_Z, NORM_1, EDGE, PROJECT, SHORT, ENDS_Y,
    ENDS_Z, SCAN, MIX, MIX_0, MIX_1, MIX_2, N2_0, N2_1,
    FF, ACT, DA, DN2_0, DN2_1, DN2_2, DH_0, DH_1,
    DZ, BACKS_Y, BACKS_Z, ADJOINT, DQ, DN1_0, DN1_X, DN1_1,
    DN1_2, GT_0, GT_1, GT_2, GT_3, GT_4,
) = range(38)
AG, RS, WG, FFN, SMALL, SHORT_1 = range(6)
PLAN = {
    START: ((AG, A_IN, 1),),
    GAIN_Y: ((AG, A_REST, 1), (AG, A_IN, 3),),
    GAIN_Z: ((AG, A_REST, 3), (AG, A_IN, 4), (AG, B_IN, 1),),
    NORM_1: ((AG, B_IN, 2),),
    EDGE: ((AG, B_IN, 3), (AG, A_REST, 4), (AG, B_GU_2, 1), (AG, B_OUT, 1),),
    PROJECT: ((AG, B_IN, 4),),
    ENDS_Y: ((AG, B_GU, 1),),
    ENDS_Z: ((AG, B_OUT, 3), (AG, B_DOWN, 1), (AG, B_GU, 2), (AG, B_GU, 3), (AG, B_GU_2, 2),),
    MIX: ((AG, B_OUT, 4),),
    MIX_0: ((AG, B_GU_2, 3),),
    N2_0: ((AG, B_GU, 4), (AG, B_DOWN, 2), (AG, B_DOWN, 3),),
    FF: ((AG, B_GU_2, 4),),
    ACT: ((WG, DOWN), (RS, DOWN, 0), (RS, DOWN, 1), (AG, B_DOWN, 4),),
    DN2_1: ((RS, DOWN, 2), (WG, GU),),
    DN2_2: ((RS, GU, 0), (RS, GU_2, 0), (FFN, 0), (RS, GU_2, 1),),
    DH_1: ((RS, GU, 1),),
    BACKS_Y: ((RS, GU_2, 2), (WG, OUT), (RS, OUT, 0), (FFN, 1), (SHORT_1,), (WG, IN),),
    BACKS_Z: ((RS, IN, 0), (RS, GU, 2), (RS, GU_2, 3), (RS, IN, 1), (FFN, 2),),
    DQ: ((RS, OUT, 1), (RS, OUT, 2), (RS, IN, 2), (RS, GU, 3), (RS, S_GU, 0),),
    DN1_0: ((WG, IN_2), (RS, IN_2, 0),),
    DN1_1: ((RS, IN_2, 1), (SMALL, 0),),
    DN1_2: ((FFN, 3), (RS, IN, 3), (RS, OUT, 3), (RS, S_IN, 0), (RS, IN_2, 2),),
    GT_0: ((RS, DOWN, 3), (RS, S_DOWN, 0), (FFN, 4), (SMALL, 1), (RS, S_OUT, 0),),
    GT_1: ((RS, IN_2, 3), (RS, S_IN_2, 0), (RS, S_IN, 1),),
    GT_2: ((RS, S_DOWN, 1), (RS, S_GU, 1), (SMALL, 2), (RS, S_IN_2, 1),),
    GT_3: ((RS, S_OUT, 1), (RS, S_IN, 2), (RS, S_DOWN, 2), (FFN, 5),),
    GT_4: ((RS, S_GU, 2), (RS, S_IN_2, 2), (RS, S_OUT, 2),),
}


class Rings:
    def __init__(self):
        self.z, self.y, self.c, self.x = where()
        self.chip = self.z * 4 + self.y
        self.sib = device(self.z, self.y, 1 - self.c, self.x)

    def near(self, axis, d, other=False):
        c = 1 - self.c if other else self.c
        if axis == 0:
            return device(rem4(self.z + d), self.y, c, self.x)
        if axis == 1:
            return device(self.z, rem4(self.y + d), c, self.x)
        return device(self.z, self.y, c, rem4(self.x + d))

    def along(self, d):
        return (lax.rem(self.chip + d + 16, 16) * 2 + self.c, self.x)


class Gather:
    def __init__(self, r, ref, lanes, rows, phase, axis, split, send, recv, own=None):
        self.r, self.ref, self.lanes, self.rows, self.own = r, ref, lanes, rows, own
        self.phase, self.axis, self.split = phase, axis, split
        self.send, self.recv, self.sent = send, recv, []

    def copy(self, d, part, to, i):
        r, axis = self.r, self.axis
        z, y = (rem4(r.z + d), r.y) if axis == 0 else (r.z, rem4(r.y + d))
        if self.phase == 0:
            o, n = self.rows
            rows = (pl.ds(o, n), pl.ds(o, n // 2), pl.ds(o + n // 2, n // 2))[part]
            ref = self.ref.at[z, y, rows, self.lanes]
        else:
            many, rows = (pl.ds(0, 4), pl.ds(0, 2), pl.ds(2, 2))[part], pl.ds(*self.rows)
            ref = self.ref.at[z, many, rows, self.lanes] if axis == 0 else self.ref.at[many, y, rows, self.lanes]
        return remote(ref, ref, self.send, self.recv.at[i], r.near(axis, to))

    def start(self, *a):
        copy = self.copy(*a)
        copy.start()
        self.sent.append(copy)

    def step(self, i):
        if i == 1 and self.own:
            there = self.ref.at[self.r.z, self.r.y, self.own[1], self.lanes]
            for j, d in enumerate((1, -1)):
                for other, src in enumerate((there, self.own[0])):
                    to = self.r.near(self.axis, d, bool(other))
                    self.sent.append(remote(src, there, self.send, self.recv.at[j], to))
                    self.sent[-1].start()
        elif i == 1 and not self.split:
            self.start(0, 0, 1, 0)
            self.start(0, 0, -1, 1)
        elif i == 1:
            self.start(0, 1, 1, 0)
            self.start(0, 2, -1, 1)
        elif i == 2 and not self.split:
            pass
        elif i == 2:
            self.start(0, 2, 1, 2)
            self.start(0, 1, -1, 2)
        elif i == 3:
            self.copy(-1, 1 if self.split else 0, 1, 0).wait_recv()
            self.start(-1, 1, 1, 2)
            self.copy(1, 2 if self.split else 0, -1, 1).wait_recv()
            self.start(1, 2, -1, 2)
        else:
            waiting(self.units(2 if self.split else 1), self.recv.at[2]).wait_recv()

    def units(self, count):
        rows = pl.ds(*self.rows)
        if self.phase == 0:
            return self.ref.at[0, pl.ds(0, count), rows, self.lanes]
        return self.ref.at[pl.ds(0, count), :, rows, self.lanes]

    def drain(self):
        if self.sent:
            waiting(self.units(3), self.send).wait_send()
        self.sent = []


class Trade:
    def __init__(self, r, axis, src, land, send, recv):
        self.r, self.axis, self.src, self.land, self.send, self.recv = r, axis, src, land, send, recv
        self.me, self.sent = (r.z, r.y, r.x)[axis], []

    def copy(self, d):
        return remote(
            self.src(rem4(self.me + d)), self.land.at[self.me], self.send, self.recv,
            self.r.near(self.axis, d),
        )

    def begin(self):
        for d in (2, 1, 3):
            copy = self.copy(d)
            copy.start()
            self.sent.append(copy)

    def end(self):
        waiting(self.land.at[0:3], self.recv).wait_recv()

    def drain(self):
        if self.sent:
            waiting(self.land.at[0:3], self.send).wait_send()


class Scatter:
    def __init__(self, r, ref, lanes, rows, at, phase, axis, buf, send, recv):
        self.r, self.ref, self.lanes, self.rows, self.at = r, ref, lanes, rows, at
        self.phase, self.axis, self.buf, self.send, self.recv, self.sent = phase, axis, buf, send, recv, []

    def unit(self, d, part):
        r, axis = self.r, self.axis
        z, y = (rem4(r.z + d), r.y) if axis == 0 else (r.z, rem4(r.y + d))
        if self.phase == 1:
            o, n = self.rows
            return self.ref.at[z, y, pl.ds(o + n // 2 * part, n // 2), self.lanes]
        many, rows = pl.ds(2 * part, 2), pl.ds(*self.rows)
        return self.ref.at[z, many, rows, self.lanes] if axis == 0 else self.ref.at[many, y, rows, self.lanes]

    def landing(self, i):
        o, n = self.rows
        if self.phase == 0:
            return self.buf.at[i, :, pl.ds(o, n), self.at]
        return self.buf.at[i, pl.ds(o // 2, n // 2), self.at]

    def copy(self, d, part, to, i):
        return remote(
            self.unit(d, part), self.landing(i), self.send, self.recv.at[min(i, 2)],
            self.r.near(self.axis, to),
        )

    def start(self, *a):
        copy = self.copy(*a)
        copy.start()
        self.sent.append(copy)

    def arrived(self, i):
        self.copy(0, 0, 1, i).wait_recv()

    def add(self, d, part, many):
        unit = self.unit(d, part)
        lands, many = [self.landing(i) for i in many], self.rows[1] // 32
        if self.phase == 0:
            def body(i):
                k, rows = i // many, span(lax.rem(i, many) * 32, 32)
                total = unit[k, rows, :].astype(F32)
                for l in lands:
                    total = total + l[k, rows, :].astype(F32)
                unit[k, rows, :] = total.astype(BF16)
            loop(2 * many, body)
        else:
            def body(i):
                rows = span(i * 32, 32)
                total = unit[rows, :].astype(F32)
                for l in lands:
                    total = total + l[rows, :].astype(F32)
                unit[rows, :] = total.astype(BF16)
            loop(many // 2, body)

    def far(self):
        self.start(2, 0, 1, 0)
        self.start(2, 1, -1, 1)

    def early(self):
        self.start(1, 1, 1, 3)
        self.start(-1, 0, -1, 4)

    def forward(self):
        self.arrived(0)
        self.add(1, 0, (0,))
        self.start(1, 0, 1, 2)
        self.arrived(1)
        self.add(-1, 1, (1,))
        self.start(-1, 1, -1, 5)

    def units(self, count):
        o, n = self.rows
        if self.phase == 0:
            return self.buf.at[pl.ds(0, 2 * count), :, pl.ds(o, n), self.at]
        return self.buf.at[pl.ds(0, 2 * count), pl.ds(o // 2, n // 2), self.at]

    def finish(self):
        waiting(self.units(2), self.recv.at[2]).wait_recv()
        self.add(0, 0, (2, 4))
        self.add(0, 1, (3, 5))

    def drain(self):
        if self.sent:
            waiting(self.units(3), self.send).wait_send()
        self.sent = []


class CrossSum:
    def __init__(self, r, part, got, mid, one, two, send, recv):
        self.r, self.part, self.got, self.mid, self.one, self.two = r, part, got, mid, one, two
        self.send, self.recv, self.sent = send, recv, []

    def start(self, copy):
        copy.start()
        self.sent.append(copy)

    def rows(self, c, x):
        return span((c * 4 + x) * 32, 32)

    def pair(self, d):
        x = rem4(self.r.x + d)
        return remote(
            self.part.at[self.rows(1 - self.r.c, x)], self.got.at[x],
            self.send, self.recv.at[(4, 1, 0, 1)[d]], self.r.sib,
        )

    def begin(self):
        for d in (2, 1, 3, 0):
            self.start(self.pair(d))

    def pairsum(self, d):
        x = rem4(self.r.x + d)
        rows = self.rows(self.r.c, x)
        self.mid[x] = (self.part[rows].astype(F32) + self.got[x].astype(F32)).astype(BF16)

    def far(self, side):
        x = rem4(self.r.x + 2)
        return remote(
            self.mid.at[x, pl.ds(16 * side, 16)], self.one.at[side],
            self.send, self.recv.at[2 + side], self.r.near(2, 1 - 2 * side),
        )

    def late(self, side, summed):
        d = 1 - 2 * side
        x = rem4(self.r.x + d)
        half = side if summed else 1 - side
        return remote(
            self.mid.at[x, pl.ds(16 * half, 16)], self.two.at[side, pl.ds(16 * half, 16)],
            self.send, self.recv.at[4], self.r.near(2, d),
        )

    def middle(self):
        self.near_half()
        self.far_half()

    def near_half(self):
        self.pair(2).wait_recv()
        self.pairsum(2)
        self.start(self.far(0))
        self.start(self.far(1))
        waiting(self.part.at[0:64], self.recv.at[1]).wait_recv()
        self.pairsum(1)
        self.start(self.late(0, 0))
        self.pairsum(3)
        self.start(self.late(1, 0))

    def far_half(self):
        for side in range(2):
            self.far(side).wait_recv()
            x = rem4(self.r.x + 1 - 2 * side)
            rows = pl.ds(16 * side, 16)
            self.mid[x, rows] = (self.mid[x, rows].astype(F32) + self.one[side].astype(F32)).astype(BF16)
            self.start(self.late(side, 1))

    def end(self):
        waiting(self.part.at[0:96], self.recv.at[4]).wait_recv()

    def result(self, rows):
        base = (self.r.c * 4 + self.r.x) * 32
        own = self.part[pl.ds(pl.multiple_of(base + rows.start, rows.size), rows.size)].astype(F32)
        own = own + self.got[self.r.x, rows].astype(F32)
        return own + self.two[0, rows].astype(F32) + self.two[1, rows].astype(F32)

    def drain(self):
        if self.sent:
            waiting(self.part.at[0:224], self.send).wait_send()
        self.sent = []


class CrossGather:
    def __init__(self, r, ref, both, send, recv):
        self.r, self.ref, self.both, self.send, self.recv, self.sent = r, ref, both, send, recv, []

    def start(self, copy):
        copy.start()
        self.sent.append(copy)

    def rows(self, d, part):
        base = rem4(self.r.x + d) * 32
        if self.both:
            base = base + self.r.c * 128
        if part is None:
            return self.ref.at[pl.ds(pl.multiple_of(base, 32), 32)]
        return self.ref.at[pl.ds(pl.multiple_of(base + 16 * part, 16), 16)]

    def ring(self, d, part, to, i):
        ref = self.rows(d, part)
        return remote(ref, ref, self.send, self.recv.at[i], self.r.near(2, to))

    def pair(self, d):
        ref = self.rows(d, None)
        return remote(ref, ref, self.send, self.recv.at[4], self.r.sib)

    def begin(self):
        self.start(self.ring(0, 0, 1, 0))
        self.start(self.ring(0, 1, -1, 1))
        self.start(self.ring(0, 1, 1, 2))
        self.start(self.ring(0, 0, -1, 2))
        if self.both:
            self.start(self.pair(0))

    def middle(self):
        self.ring(-1, 0, 1, 0).wait_recv()
        self.start(self.ring(-1, 0, 1, 3))
        self.ring(1, 1, -1, 1).wait_recv()
        self.start(self.ring(1, 1, -1, 3))
        waiting(self.ref.at[0:32], self.recv.at[2]).wait_recv()
        if self.both:
            self.start(self.pair(-1))
            self.start(self.pair(1))

    def end(self):
        waiting(self.ref.at[0:32], self.recv.at[3]).wait_recv()
        if self.both:
            self.start(self.pair(2))
            waiting(self.ref.at[0:128], self.recv.at[4]).wait_recv()

    def drain(self):
        waiting(self.ref.at[0:224 if self.both else 96], self.send).wait_send()


class Refs:
    pass


class Inputs:
    in_w = out_w = gate_w = up_w = down_w = gain_1 = gain_2 = resets = tok = cot = conv_w = 0
    decay = angle = res_re = res_im = 0


class Outputs:
    block_out = grad_tok = grad_w = grad_small = grad_gain = 0


class Scratch:
    other = ((64, LANES_A + LANES_B), BF16)
    tab = ((8, 16, 256), F32)
    ga = ((4, 4, 128, LANES_A), BF16)
    gb = ((4, 4, 128, LANES_B), BF16)
    s0a = ((6, 2, 128, LANES_A), BF16)
    s0b = ((6, 2, 128, LANES_B), BF16)
    s1a = ((6, 64, LANES_A), BF16)
    s1b = ((6, 64, LANES_B), BF16)
    da = ((4, 4, 128, 384), BF16)
    ia = ((4, 4, 128, 128), BF16)
    ib = ((4, 4, 128, 128), BF16)
    db = ((4, 4, 128, 384), BF16)
    sib_a = ((64, LANES_A), BF16)
    sib_b = ((64, LANES_B), BF16)
    gain_pair = ((2, 8, 128), F32)
    gains_y = ((4, 8, 128), F32)
    gains_all = ((4, 4, 8, 128), F32)
    gains = ((8, 2048), F32)
    gain_in = ((8, 128), F32)
    taps = ((8, 768), F32)
    keep = ((256, 256), F32)
    gy = ((256, 2048), BF16)
    n1 = ((272, 2048), BF16)
    n2 = ((256, 2048), BF16)
    dh = ((256, 2048), BF16)
    part = ((256, 2048), BF16)
    mid = ((4, 32, 2048), BF16)
    part_f = ((256, 2048), BF16)
    mid_f = ((4, 32, 2048), BF16)
    got = ((4, 4, 32, 2048), BF16)
    one = ((4, 2, 16, 2048), BF16)
    two = ((4, 2, 32, 2048), BF16)
    bo = ((128, 2048), BF16)
    gt = ((128, 2048), BF16)
    h = ((32, 2048), F32)
    dhf = ((32, 2048), F32)
    p = ((272, 768), F32)
    q0 = ((256, 256), F32)
    q1 = ((256, 256), F32)
    q2 = ((256, 256), F32)
    u = ((256, 256), F32)
    v = ((256, 256), F32)
    z = ((256, 256), BF16)
    st_re = ((257, 16, 256), F32)
    st_im = ((257, 16, 256), F32)
    ends_y = ((4, 32, 256), BF16)
    ends_z = ((4, 32, 256), BF16)
    backs_y = ((4, 32, 256), BF16)
    backs_z = ((4, 32, 256), BF16)
    gu = ((256, 1408), F32)
    act = ((256, 768), BF16)
    dgu = ((256, 1408), BF16)
    dv = ((256, 256), F32)
    dq = ((264, 768), F32)
    dp = ((256, 768), BF16)
    small_y = ((4, 80, 256), BF16)
    small_z = ((4, 80, 256), BF16)
    small_sum = ((80, 256), F32)
    small_sib = ((80, 256), F32)
    ggain = ((8, 2048), F32)
    gg_z = ((4, 8, 512), F32)
    gg_1 = ((8, 512), F32)
    gg_y = ((4, 8, 128), F32)
    gg_2 = ((8, 128), F32)
    gg_s = ((8, 128), F32)
    gg_x = ((4, 8, 128), F32)
    gg_out = ((8, 128), F32)


def fields(group):
    return [(name, value) for name, value in vars(group).items() if name[0] != "_"]


class Sems:
    w = (18,), (18, 3)
    w_sib = (2,), (2,)
    gain_sib = keep_s = gy_s = n1_s = edge = dq_s = dq_1 = small_x = gg_s = (), ()
    trade = (11,), (11,)
    sum = (4,), (4, 5)
    cg = (4,), (4, 5)
    rs = (26,), (26, 3)
    rs_sib = (5,), (5,)


def kernel(*refs):
    names = [name for group in (Inputs, Outputs, Scratch) for name, _ in fields(group)]
    k, S, R = Refs(), Refs(), Refs()
    for name, ref in zip(names, refs):
        setattr(k, name, ref)
    rest = refs[len(names):]
    for i, (name, _) in enumerate(fields(Sems)):
        setattr(S, name, rest[2 * i])
        setattr(R, name, rest[2 * i + 1])
    local = rest[-1]
    r = Rings()
    g = (k.ga, k.gb)
    z, y, c, x = r.z, r.y, r.c, r.x

    barrier = pltpu.get_barrier_semaphore()
    peers = [r.sib] + [r.near(a, d) for a in range(3) for d in (1, 2, 3)] + [r.along(1), r.along(-1)]
    peers += [r.near(a, d, True) for a in range(2) for d in (1, -1)]
    for peer in peers:
        pl.semaphore_signal(barrier, inc=1, device_id=peer, device_id_type=MESH)

    def lanes(n, h):
        o, w = CHUNKS[n][h]
        return pl.ds(o, w)

    def columns(n, start, stop):
        (oa, wa), (ob, _) = WHOLE[n]
        parts = []
        if start < wa:
            parts.append(g[0][:, :, :, oa + start:oa + min(stop, wa)])
        if stop > wa:
            parts.append(g[1][:, :, :, ob + max(start - wa, 0):ob + stop - wa])
        return jnp.concatenate([p.reshape(2048, p.shape[-1]) for p in parts], 1)

    def weight(n, h, i):
        o, w = WHOLE[n][h]
        return g[h][i, :, :, o:o + w].reshape(512, w)

    trades = []

    def trade(axis, src, land):
        i = len(trades)
        trades.append(Trade(r, axis, src if callable(src) else lambda _: src, land, S.trade.at[i], R.trade.at[i]))
        return trades[-1]

    my64 = span(c * 64, 64)
    my128 = span(c * 128, 128)
    gather = []
    for n, (phase, split, parts) in enumerate(GATHERS):
        first = sum(len(group) for group in gather)
        gather.append([
            Gather(r, g[b], pl.ds(o, w), rows, phase, 1 - way if phase == 0 else way, split and rows[1] == 128,
                   S.w.at[first + i], R.w.at[first + i],
                   (k.other.at[:, pl.ds(o + (LANES_A if b else 0), w)], my64) if n == A_IN else None)
            for i, (way, b, o, w, *rows) in enumerate(parts)
        ])

    def put(cc, n, sink):
        wa = WHOLE[n][0][1]

        def store(start, value):
            stop = start + value.shape[1]
            if start < wa:
                sink(0, WHOLE[n][0][0] + start, value[:, :min(stop, wa) - start])
            if stop > wa:
                sink(1, WHOLE[n][1][0] + max(start - wa, 0), value[:, max(wa - start, 0):])

        def main(ref):
            return ref[:, pl.ds(pl.multiple_of(cc * 640, 128), 640)]

        def tail(ref):
            a = ref[:, 1280:1408].astype(F32)
            return jnp.where(cc == 0, a[:, 0:64], a[:, 64:128])

        channels = pl.ds(pl.multiple_of(cc * 256, 256), 256)
        if n == IN:
            store(0, k.in_w[0, :, channels])
        elif n == IN_2:
            store(0, k.in_w[1, :, channels])
            store(256, k.in_w[2, :, channels])
        elif n == OUT:
            store(0, k.out_w[:, channels])
        elif n == GU:
            store(0, main(k.gate_w))
            store(640, main(k.up_w))
            store(1280, jnp.concatenate([tail(k.gate_w), tail(k.up_w)], 1).astype(BF16))
        else:
            store(0, main(k.down_w))
            store(640, jnp.concatenate([tail(k.down_w), jnp.zeros((64, 64), F32)], 1).astype(BF16))

    def to_other(h, at, value):
        at = at + (LANES_A if h else 0)
        k.other[:, at:at + value.shape[1]] = value

    def to_own(h, at, value):
        g[h][z, y, my64, at:at + value.shape[1]] = value

    def weight_sib(n, h):
        o, w = ((0, 384), (384, (1280, 1152)[h]))[n]
        return remote(
            k.other.at[:, pl.ds(o + (LANES_A if h else 0), w)], g[h].at[z, y, my64, pl.ds(o, w)],
            S.w_sib.at[n], R.w_sib.at[n], r.sib,
        )

    side = lax.broadcasted_iota(jnp.int32, (1, 128), 1) // 64 == c
    for i, ref in enumerate((k.gain_1, k.gain_2)):
        a = ref[...].astype(F32)
        k.gain_in[i:i + 1, :] = jnp.where(side, jnp.concatenate([a, a], 1), 0.0)
    k.gain_in[2:8, :] = jnp.zeros((6, 128), F32)
    for n in (IN, IN_2):
        put(1 - c, n, to_other)
        put(c, n, to_own)
    keep = 1.0 - k.resets[...].astype(F32)
    keep = jnp.broadcast_to(keep, (128, 128)).T
    k.keep[my128] = jnp.concatenate([keep, keep], 1)
    pl.semaphore_wait(barrier, len(peers))

    gain_sib = remote(k.gain_in, k.gain_pair.at[c], S.gain_sib, R.gain_sib, r.sib)
    keep_sib = remote(k.keep.at[my128], k.keep.at[my128], S.keep_s, R.keep_s, r.sib)
    gy_sib = remote(k.cot, k.gy.at[my128], S.gy_s, R.gy_s, r.sib)
    def share(n):
        for h in range(2):
            weight_sib(n, h).start()

    share(A_IN)
    gain_sib.start()

    def ag(n, i):
        if (n, i) in ((A_IN, 4), (A_REST, 1)):
            waiting(k.other.at[:, 0:(768, 2432)[n]], R.w_sib.at[n]).wait_recv()
        for piece in gather[n]:
            piece.step(i)

    tasks = {}

    def at(point):
        for name, *rest in PLAN.get(point, ()):
            tasks[name](*rest)

    tasks[AG] = ag
    at(START)
    gain_y = trade(1, k.gains_y.at[y], k.gains_y)
    gain_z = trade(0, k.gains_y, k.gains_all)
    gain_sib.wait_recv()
    k.gains_y[y] = k.gain_in[...] + k.gain_pair[1 - c]
    gain_y.begin()

    for n in (OUT, GU, DOWN):
        put(1 - c, n, to_other)
        put(c, n, to_own)
    share(A_REST)
    keep_sib.start()
    at(GAIN_Y)
    gain_y.end()
    gain_z.begin()
    k.gains_all[z] = k.gains_y[...]
    at(GAIN_Z)
    k.gy[my128] = k.cot[...]

    channels = pl.ds(pl.multiple_of(c * 256, 256), 256)
    decay, angle = k.decay[:, channels], k.angle[:, channels]
    size = jnp.exp(-decay)
    gin = jnp.sqrt(-expm1(-2.0 * decay))
    power = (size * jnp.cos(angle), size * jnp.sin(angle))
    k.tab[0], k.tab[1] = power
    k.tab[2] = gin * k.res_re[:, channels]
    k.tab[3] = gin * k.res_im[:, channels]
    for _ in range(8):
        power = (power[0] * power[0] - power[1] * power[1], 2.0 * power[0] * power[1])
    k.tab[4], k.tab[5] = power
    k.tab[6] = gin
    k.tab[7] = size * size / gin
    for i in range(3):
        for b in range(3):
            k.taps[i:i + 1, b * 256:b * 256 + 256] = k.conv_w[i, b:b + 1, channels]

    gain_z.end()
    for i in range(16):
        k.gains[:, i * 128:(i + 1) * 128] = k.gains_all[i // 4, i % 4]

    def norm_one(i):
        rows = span(i * 16, 16)
        a = k.tok[rows, :].astype(F32)
        s = lax.rsqrt(jnp.mean(a * a, axis=-1, keepdims=True) + EPSILON)
        k.n1[pl.ds(pl.multiple_of(16 + c * 128 + i * 16, 16), 16), :] = (a * s * k.gains[0:1, :]).astype(BF16)
    loop(8, norm_one)

    def n1_rows(c):
        return k.n1.at[pl.ds(pl.multiple_of(16 + c * 128, 16), 128)]

    n1_sib = remote(n1_rows(c), n1_rows(c), S.n1_s, R.n1_s, r.sib)
    n1_sib.start()
    at(NORM_1)
    k_other = span((1 - c) * 128, 128)
    remote(n1_rows(1 - c), n1_rows(1 - c), S.n1_s, R.n1_s, r.sib).wait_recv()
    edge = remote(k.n1.at[256:272], k.n1.at[0:16], S.edge, R.edge, r.along(1))
    edge.start()
    gy_sib.start()
    at(EDGE)

    edge.wait_recv()
    at(PROJECT)

    def project(_):
        for o in range(0, 512, 256):
            k.p[:, 256 + o:512 + o] = nn(k.n1[...], columns(IN_2, o, o + 256))
        k.p[:, 0:256] = nn(k.n1[...], columns(IN, 0, 256))
    loop(1, project)

    def round_p(i):
        rows = span(i * 16, 16)
        k.p[rows, :] = k.p[rows, :].astype(BF16).astype(F32)
    loop(17, round_p)
    remote(k.keep.at[k_other], k.keep.at[k_other], S.keep_s, R.keep_s, r.sib).wait_recv()
    at(SHORT)

    def masks(i):
        rows = span(i * 16, 16)
        near = k.keep[rows, :]
        before = k.keep[span(jnp.maximum(i * 16 - 8, 0), 8), :]
        first = jnp.where(i == 0, 1.0, before[7:8, :])
        shifted = jnp.concatenate([first, near[0:15, :]], 0)
        return near, near * shifted

    def short(i):
        near, far = masks(i)
        ext = k.p[pl.ds(pl.multiple_of(i * 16 + 8, 8), 24), :]
        q = []
        for b in range(3):
            l = slice(b * 256, b * 256 + 256)
            e = ext[:, l]
            q.append(
                k.taps[0:1, l] * e[8:24] + near * k.taps[1:2, l] * e[7:23] + far * k.taps[2:3, l] * e[6:22]
            )
        rows = span(i * 16, 16)
        k.q0[rows, :] = q[0]
        k.q1[rows, :] = q[1]
        k.q2[rows, :] = q[2]
        k.u[rows, :] = q[1] * q[2]
    loop(16, short)

    zero = jnp.zeros((16, 256), F32)
    lr, li, cr, ci, pr, pi = (k.tab[i] for i in range(6))

    def advance(re, im, u, keep):
        kr, ki = keep * re, keep * im
        return lr * kr - li * ki + u, lr * ki + li * kr

    def end_state(i, state):
        rows = span(i * 8, 8)
        u, keep = k.u[rows, :], k.keep[rows, :]
        for j in range(8):
            state = advance(*state, u[j:j + 1, :], keep[j:j + 1, :])
        return state

    def times(a, b, g, h):
        return a * g - b * h, a * h + b * g

    def chain(own, ref_y, ref_z, sign, between):
        order = range(4) if sign > 0 else range(3, -1, -1)
        qr, qi = pr, sign * pi

        def put(ref, at, state):
            ref[at, 0:16] = state[0].astype(BF16)
            ref[at, 16:32] = state[1].astype(BF16)

        def horner(ref, wr, wi, state, here, every):
            for i in order:
                nr, ni = times(wr, wi, *state)
                nr, ni = nr + ref[i, 0:16].astype(F32), ni + ref[i, 16:32].astype(F32)
                use = (i < here) if sign > 0 else (i > here)
                state = (nr, ni) if every else (jnp.where(use, nr, state[0]), jnp.where(use, ni, state[1]))
            return state

        put(ref_y, y, own)
        t = trade(1, ref_y.at[y], ref_y)
        t.begin()
        at(between[0])
        t.end()
        put(ref_z, z, horner(ref_y, qr, qi, (zero, zero), y, True))
        t = trade(0, ref_z.at[z], ref_z)
        t.begin()
        at(between[1])
        t.end()
        w = times(*times(qr, qi, qr, qi), *times(qr, qi, qr, qi))
        return horner(ref_y, qr, qi, horner(ref_z, *w, (zero, zero), z, False), y, False)

    end = fold(32, end_state, (zero, zero))
    enter = chain(end, k.ends_y, k.ends_z, 1, (ENDS_Y, ENDS_Z))
    k.st_re[0] = enter[0]
    k.st_im[0] = enter[1]
    at(SCAN)

    def scan(i, state):
        rows = span(i * 8, 8)
        u, keep = k.u[rows, :], k.keep[rows, :]
        for j in range(8):
            state = advance(*state, u[j:j + 1, :], keep[j:j + 1, :])
            k.st_re[i * 8 + j + 1] = state[0]
            k.st_im[i * 8 + j + 1] = state[1]
            k.v[pl.ds(i * 8 + j, 1), :] = jnp.sum(cr * state[0] - ci * state[1], axis=0, keepdims=True)
        return state
    fold(32, scan, enter)

    def gated(i):
        rows = span(i * 32, 32)
        k.z[rows, :] = (k.q0[rows, :] * k.v[rows, :]).astype(BF16)
    loop(8, gated)

    at(MIX)
    def out_weight(i):
        return jnp.concatenate([weight(OUT, 0, i), weight(OUT, 1, i)], 1)

    def mix(i):
        k.part[:, span(i * 512, 512)] = nt(k.z[...], out_weight(i)).astype(BF16)
    loop(4, mix)

    def cross(i):
        part, mid = (k.part_f, k.mid_f) if i == 1 else (k.part, k.mid)
        return CrossSum(r, part, k.got.at[i], mid, k.one.at[i], k.two.at[i], S.sum.at[i], R.sum.at[i])

    s_mix = cross(0)
    s_mix.begin()
    at(MIX_0)
    s_mix.near_half()
    at(MIX_1)
    s_mix.far_half()
    at(MIX_2)
    s_mix.end()

    own = (c * 4 + x) * 32

    def norm_two(i):
        rows = pl.ds(pl.multiple_of(i * 16, 16), 16)
        a = k.tok[pl.ds(pl.multiple_of(x * 32 + i * 16, 16), 16), :].astype(F32) + s_mix.result(rows)
        k.h[rows, :] = a
        s = lax.rsqrt(jnp.mean(a * a, axis=-1, keepdims=True) + EPSILON)
        k.n2[pl.ds(pl.multiple_of(own + i * 16, 16), 16), :] = (a * s * k.gains[1:2, :]).astype(BF16)
    loop(2, norm_two)
    g_n2 = CrossGather(r, k.n2, True, S.cg.at[0], R.cg.at[0])
    g_n2.begin()
    at(N2_0)
    g_n2.middle()
    at(N2_1)
    g_n2.end()
    s_mix.drain()
    at(FF)

    def gate_up(_):
        for o in range(0, 1408, 256):
            e = min(o + 256, 1408)
            k.gu[:, o:e] = nn(k.n2[...], columns(GU, o, e))
    loop(1, gate_up)
    def halves(t):
        last = t[:, 1280:1408]
        turned = jnp.concatenate([last[:, 64:128], last[:, 0:64]], 1)
        return jnp.concatenate([t[:, 0:640], last], 1), jnp.concatenate([t[:, 640:1280], turned], 1)

    used = lax.broadcasted_iota(jnp.int32, (1, 768), 1) < 704

    def activate(i):
        rows = span(i * 16, 16)
        gate, up = halves(k.gu[rows, :])
        k.act[rows, :] = jnp.where(used, gate * jax.nn.sigmoid(gate) * up, 0.0).astype(BF16)
    loop(16, activate)

    def down_weight(i):
        return jnp.concatenate([weight(DOWN, 0, i), weight(DOWN, 1, i)], 1)

    s_ffn = cross(1)
    g_bo = CrossGather(r, k.bo, False, S.cg.at[1], R.cg.at[1])
    out_bo = pltpu.make_async_copy(k.bo, k.block_out, local.at[0])

    def ffn_step(i):
        if i == 0:
            def ffn(i):
                k.part_f[:, span(i * 512, 512)] = nt(k.act[...], down_weight(i)).astype(BF16)
            loop(4, ffn)
            s_ffn.begin()
        elif i == 1:
            s_ffn.near_half()
        elif i == 2:
            s_ffn.far_half()
        elif i == 3:
            s_ffn.end()

            def top(i):
                rows = pl.ds(pl.multiple_of(i * 16, 16), 16)
                here = pl.ds(pl.multiple_of(x * 32 + i * 16, 16), 16)
                k.bo[here, :] = (k.h[rows, :] + s_ffn.result(rows)).astype(BF16)
            loop(2, top)
            s_ffn.drain()
            g_bo.begin()
        elif i == 4:
            g_bo.middle()
        else:
            g_bo.end()
            out_bo.start()

    tasks[FFN] = ffn_step

    apart = {DOWN: (k.da, k.db), IN: (k.ia, k.ib)}
    scatter = []
    for n, parts in enumerate(SCATTERS):
        phase = 0 if n < S_IN else 1
        m = {S_IN: IN, S_DOWN: DOWN}.get(n, n if phase == 0 else None)
        first = sum(len(group) for group in scatter)
        scatter.append([])
        for i, (way, b, o, w, *rows) in enumerate(parts):
            ref, here = g[b], pl.ds(o, w)
            if m in apart:
                ref, here = apart[m][b], pl.ds(o - CHUNKS[m][b][0], w)
            buf = ((k.s0a, k.s0b), (k.s1a, k.s1b))[phase][b]
            axis = 1 - way if phase == 0 else way
            scatter[n].append(
                Scatter(r, ref, here, rows, pl.ds(o, w), phase, axis, buf, S.rs.at[first + i], R.rs.at[first + i])
            )

    def finished(n, h):
        o, w = SECOND[n - S_IN][h]
        m = {S_IN: IN, S_DOWN: DOWN}.get(n)
        return (apart[m][h], pl.ds(0, w), pl.ds(o, w)) if m in apart else (g[h], pl.ds(o, w), pl.ds(o, w))

    sib_bufs = (k.sib_a, k.sib_b)

    def rs_sib(n, h):
        ref, here, at = finished(n, h)
        return remote(
            ref.at[z, y, span((1 - c) * 64, 64), here], sib_bufs[h].at[:, at],
            S.rs_sib.at[n - S_IN], R.rs_sib.at[n - S_IN], r.sib,
        )

    def rs(n, i):
        for s in scatter[n]:
            if n < S_IN:
                (s.far, s.early, s.forward, s.finish)[i]()
            elif i == 0:
                s.far()
                s.early()
            elif i == 1:
                s.forward()
            else:
                s.finish()
        if n >= S_IN and i == 2:
            for h in range(2):
                rs_sib(n, h).start()

    tasks[RS] = rs

    def wg(n):
        a, b, first = {
            IN: (k.n1, k.dp.at[:, 0:256], 16), IN_2: (k.n1, k.dp.at[:, 256:768], 16), OUT: (k.dh, k.z, 0),
            GU: (k.n2, k.dgu, 0), DOWN: (k.gy, k.act, 0),
        }[n]
        for m in {GU: (B_GU, B_GU_2), OUT: (B_OUT,), IN_2: (B_IN,)}.get(n, ()) + ((A_IN, A_REST) if n == GU else ()):
            for piece in gather[m]:
                piece.drain()
        (oa, wa), (ob, wb) = [(0, CHUNKS[n][h][1]) for h in range(2)] if n in apart else WHOLE[n]
        into = apart.get(n, g)

        def weight_grad(i):
            t = tn(a[pl.ds(first, 256), pl.ds(pl.multiple_of(i * 512, 512), 512)], b[...]).astype(BF16)
            into[0][i, :, :, oa:oa + wa] = t[:, 0:wa].reshape(4, 128, wa)
            into[1][i, :, :, ob:ob + wb] = t[:, wa:wa + wb].reshape(4, 128, wb)
        weight_grad.width = wa + wb
        loop(4, weight_grad)

    tasks[WG] = wg

    remote(k.gy.at[k_other], k.gy.at[k_other], S.gy_s, R.gy_s, r.sib).wait_recv()
    at(ACT)

    def d_act(_):
        for o in range(0, 768, 256):
            k.dq[0:256, o:o + 256] = nn(k.gy[...], columns(DOWN, o, o + 256))
    loop(1, d_act)
    at(DA)

    def d_gates(i):
        rows = span(i * 16, 16)
        gate, up = halves(k.gu[rows, :])
        da = k.dq[rows, :]
        sg = jax.nn.sigmoid(gate)
        dgate = da * up * sg * (1.0 + gate * (1.0 - sg))
        dup = da * (gate * sg)
        last = jnp.concatenate([dgate[:, 640:704], dup[:, 640:704]], 1)
        k.dgu[rows, :] = jnp.concatenate([dgate[:, 0:640], dup[:, 0:640], last], 1).astype(BF16)
    loop(16, d_gates)

    def d_n2(i):
        w = jnp.concatenate([weight(GU, 0, i), weight(GU, 1, i)], 1)
        k.part[:, span(i * 512, 512)] = nt(k.dgu[...], w).astype(BF16)
    loop(4, d_n2)
    s_dn2 = cross(2)
    s_dn2.begin()
    at(DN2_0)
    s_dn2.near_half()
    at(DN2_1)
    s_dn2.far_half()
    at(DN2_2)
    s_dn2.end()

    def d_norm_two(i):
        rows = pl.ds(pl.multiple_of(i * 16, 16), 16)
        a = k.h[rows, :]
        s = lax.rsqrt(jnp.mean(a * a, axis=-1, keepdims=True) + EPSILON)
        hat = a * s
        dn = s_dn2.result(rows)
        dng = dn * k.gains[1:2, :]
        gy = k.gy[pl.ds(pl.multiple_of(own + i * 16, 16), 16), :].astype(F32)
        dh = gy + s * (dng - hat * jnp.mean(dng * hat, axis=-1, keepdims=True))
        k.dhf[rows, :] = dh
        k.dh[pl.ds(pl.multiple_of(own + i * 16, 16), 16), :] = dh.astype(BF16)
        t = jnp.sum(dn * hat, axis=0, keepdims=True)

        @pl.when(i == 0)
        def _():
            k.ggain[...] = jnp.zeros((8, 2048), F32)
            k.ggain[1:2, :] = t

        @pl.when(i > 0)
        def _():
            k.ggain[1:2, :] += t
    loop(2, d_norm_two)
    s_dn2.drain()
    g_dh = CrossGather(r, k.dh, True, S.cg.at[2], R.cg.at[2])
    g_dh.begin()
    at(DH_0)
    g_dh.middle()
    at(DH_1)
    g_dh.end()
    at(DZ)

    def d_z(_):
        k.dv[...] = nn(k.dh[...], columns(OUT, 0, 256))
    loop(1, d_z)

    def d_gated(i):
        rows = span(i * 32, 32)
        dz = k.dv[rows, :]
        k.dq[rows, 0:256] = dz * k.v[rows, :]
        k.dv[rows, :] = dz * k.q0[rows, :]
    loop(8, d_gated)

    first = slice(0, 256)
    others = slice(256, 768)

    def dq_edge(at, send, recv):
        return remote(k.dq.at[0:8, at], k.dq.at[256:264, at], send, recv, r.along(-1))

    dq_first = dq_edge(first, S.dq_1, R.dq_1)
    dq_first.start()

    last = jnp.where(r.chip < 15, 1.0, 0.0)

    def d_short(i, taps, branches):
        near, far = masks(i)
        j = jnp.minimum(i * 16 + 16, 248)
        after = k.keep[span(j, 8), :]
        inside = i < 15
        tail_near = jnp.where(inside, after, last)
        tail_far = jnp.where(
            inside, after * jnp.concatenate([near[15:16, :], after[0:7, :]], 0), last
        )
        near = jnp.concatenate([near, tail_near], 0)
        far = jnp.concatenate([far, tail_far], 0)
        ext = k.p[pl.ds(pl.multiple_of(i * 16 + 8, 8), 24), :]
        rows = span(i * 16, 16)
        new = []
        for n, b in enumerate(branches):
            l = slice(b * 256, b * 256 + 256)
            e, db = ext[:, l], k.dq[pl.ds(pl.multiple_of(i * 16, 16), 24), l]
            dn, df = near * db, far * db
            k.dp[rows, l] = (
                k.taps[0:1, l] * db[0:16] + k.taps[1:2, l] * dn[1:17] + k.taps[2:3, l] * df[2:18]
            ).astype(BF16)
            new.append(taps[3 * n + 0] + jnp.sum(e[8:24] * db[0:16], axis=0, keepdims=True))
            new.append(taps[3 * n + 1] + jnp.sum(e[7:23] * dn[0:16], axis=0, keepdims=True))
            new.append(taps[3 * n + 2] + jnp.sum(e[6:22] * df[0:16], axis=0, keepdims=True))
        return tuple(new)

    line = jnp.zeros((1, 256), F32)
    def d_short_1(i, taps):
        return d_short(i, taps, (0,))

    def d_short_2(i, taps):
        return d_short(i, taps, (1, 2))

    d_taps = []

    def short_1():
        dq_first.wait()
        d_taps.extend(fold(16, d_short_1, (line,) * 3))

    tasks[SHORT_1] = short_1

    def retreat(a, b, keep):
        ka, kb = keep * a, keep * b
        return ka, kb, lr * ka + li * kb, lr * kb - li * ka

    def start_state(i, state):
        rows = span((31 - i) * 8, 8)
        dv, keep = k.dv[rows, :], k.keep[rows, :]
        for j in reversed(range(8)):
            a = cr * dv[j:j + 1, :] + state[0]
            b = state[1] - ci * dv[j:j + 1, :]
            _, _, pa, pb = retreat(a, b, keep[j:j + 1, :])
            state = (pa, pb)
        return state

    begin = fold(32, start_state, (zero, zero))
    arrive = chain(begin, k.backs_y, k.backs_z, -1, (BACKS_Y, BACKS_Z))
    at(ADJOINT)

    def adjoint(i, carry):
        rows = span((31 - i) * 8, 8)
        dv, keep = k.dv[rows, :], k.keep[rows, :]
        for j in reversed(range(8)):
            t = (31 - i) * 8 + j
            d = dv[j:j + 1, :]
            a = cr * d + carry[0]
            b = carry[1] - ci * d
            k.u[pl.ds(t, 1), :] = jnp.sum(a, axis=0, keepdims=True)
            _, _, pa, pb = retreat(a, b, keep[j:j + 1, :])
            carry = (pa, pb)
        return carry

    fold(32, adjoint, arrive)

    def d_poles(i, carry):
        pa, pb, dcr, dci, dlr, dli = carry
        rows = span((31 - i) * 8, 8)
        dv, keep = k.dv[rows, :], k.keep[rows, :]
        for j in reversed(range(8)):
            t = (31 - i) * 8 + j
            d = dv[j:j + 1, :]
            a = cr * d + pa
            b = pb - ci * d
            dcr = dcr + d * k.st_re[t + 1]
            dci = dci - d * k.st_im[t + 1]
            ka, kb, pa, pb = retreat(a, b, keep[j:j + 1, :])
            sr, si = k.st_re[t], k.st_im[t]
            dlr = dlr + ka * sr + kb * si
            dli = dli + kb * sr - ka * si
        return pa, pb, dcr, dci, dlr, dli

    def d_branches(i):
        rows = span(i * 32, 32)
        du = k.u[rows, :]
        k.dq[rows, 256:512] = du * k.q2[rows, :]
        k.dq[rows, 512:768] = du * k.q1[rows, :]
    loop(8, d_branches)
    dq_next = dq_edge(others, S.dq_s, R.dq_s)
    dq_next.start()
    at(DQ)
    dq_next.wait()
    d_taps.extend(fold(16, d_short_2, (line,) * 6))

    def d_n1(i):
        w = jnp.concatenate([weight(n, h, i) for n in (IN, IN_2) for h in range(2)], 1)
        k.part[:, span(i * 512, 512)] = nt(k.dp[...], w).astype(BF16)
    loop(4, d_n1)
    s_dn1 = cross(3)
    s_dn1.begin()
    at(DN1_0)

    small_1 = trade(1, k.small_y.at[y], k.small_y)
    small_2 = trade(0, k.small_z.at[z], k.small_z)

    def small_total(ref):
        return sum(ref[j].astype(F32) for j in range(4))

    small_x = remote(k.small_sum, k.small_sib, S.small_x, R.small_x, r.sib)

    def small(i):
        if i == 0:
            _, _, *dpoles = fold(32, d_poles, (*arrive, zero, zero, zero, zero))
            for j in range(4):
                k.small_y[y, 16 * j:16 * j + 16] = dpoles[j].astype(BF16)
            k.small_y[y, 64:80] = jnp.concatenate([d_taps[3 * b + t] for t in range(3) for b in range(3)] + [jnp.zeros((7, 256), F32)], 0).astype(BF16)
            small_1.begin()
        elif i == 1:
            small_1.end()
            k.small_z[z] = small_total(k.small_y).astype(BF16)
            small_2.begin()
        else:
            small_2.end()
            k.small_sum[...] = small_total(k.small_z)
            dcr, dci, dlr, dli = (k.small_sum[16 * j:16 * j + 16, :] for j in range(4))
            dgin = k.res_re[:, channels] * dcr + k.res_im[:, channels] * dci
            k.small_sum[0:16, :] = dgin * k.tab[7] - (lr * dlr + li * dli)
            k.small_sum[16:32, :] = lr * dli - li * dlr
            k.small_sum[32:48, :] = k.tab[6] * dcr
            k.small_sum[48:64, :] = k.tab[6] * dci
            small_x.start()

    tasks[SMALL] = small
    at(DN1_X)
    s_dn1.near_half()
    at(DN1_1)
    s_dn1.far_half()
    at(DN1_2)
    s_dn1.end()

    def d_norm_one(i):
        rows = pl.ds(pl.multiple_of(i * 16, 16), 16)
        here = pl.ds(pl.multiple_of(x * 32 + i * 16, 16), 16)
        a = k.tok[here, :].astype(F32)
        s = lax.rsqrt(jnp.mean(a * a, axis=-1, keepdims=True) + EPSILON)
        hat = a * s
        dn = s_dn1.result(rows)
        dng = dn * k.gains[0:1, :]
        k.gt[here, :] = (
            k.dhf[rows, :] + s * (dng - hat * jnp.mean(dng * hat, axis=-1, keepdims=True))
        ).astype(BF16)
        t = jnp.sum(dn * hat, axis=0, keepdims=True)

        @pl.when(i == 0)
        def _():
            k.ggain[0:1, :] = t

        @pl.when(i > 0)
        def _():
            k.ggain[0:1, :] += t
    loop(2, d_norm_one)
    g_gt = CrossGather(r, k.gt, False, S.cg.at[3], R.cg.at[3])
    g_gt.begin()

    def piece(ref, width):
        return lambda i: ref.at[:, pl.ds(pl.multiple_of(i * width, width), width)]

    gg_1 = trade(0, piece(k.ggain, 512), k.gg_z)
    gg_2 = trade(1, piece(k.gg_1, 128), k.gg_y)
    gg_3 = trade(2, k.gg_s, k.gg_x)
    gg_sib = remote(k.gg_2, k.gg_s, S.gg_s, R.gg_s, r.sib)
    gg_1.begin()
    k.gg_z[z] = k.ggain[:, span(z * 512, 512)]
    at(GT_0)
    gg_1.end()
    k.gg_1[...] = sum(k.gg_z[j] for j in range(4))
    gg_2.begin()
    k.gg_y[y] = k.gg_1[:, span(y * 128, 128)]
    at(GT_1)
    g_gt.middle()
    at(GT_2)
    gg_2.end()
    k.gg_2[...] = sum(k.gg_y[j] for j in range(4))
    gg_sib.start()
    at(GT_3)
    gg_sib.wait()
    k.gg_s[...] = k.gg_s[...] + k.gg_2[...]
    gg_3.begin()
    k.gg_x[x] = k.gg_s[...]
    g_gt.end()
    out_gt = pltpu.make_async_copy(k.gt, k.grad_tok, local.at[1])
    out_gt.start()
    at(GT_4)
    small_x.wait()
    gg_3.end()
    k.gg_out[...] = sum(k.gg_x[j] for j in range(4))

    for n in range(S_IN, 11):
        both = k.other.at[:, 0:SECOND[n - S_IN][0][1] + SECOND[n - S_IN][1][1]]
        waiting(both, S.rs_sib.at[n - S_IN]).wait_send()
        waiting(both, R.rs_sib.at[n - S_IN]).wait_recv()
        for h in range(2):
            (ref, here, at), (o, w) = finished(n, h), SECOND[n - S_IN][h]
            there = pl.ds(o + (LANES_A if h else 0), w)
            pltpu.make_async_copy(ref.at[z, y, my64, here], k.grad_w.at[0, :, there], local.at[2]).start()
            pltpu.make_async_copy(sib_bufs[h].at[:, at], k.grad_w.at[1, :, there], local.at[2]).start()
    for j, src in enumerate((k.small_sum, k.small_sib)):
        pltpu.make_async_copy(src, k.grad_small.at[j], local.at[3]).start()
    out_gain = pltpu.make_async_copy(k.gg_out, k.grad_gain, local.at[4])
    out_gain.start()
    out_bo.wait()
    out_gt.wait()
    pltpu.make_async_copy(k.grad_w, k.grad_w, local.at[2]).wait()
    pltpu.make_async_copy(k.grad_small, k.grad_small, local.at[3]).wait()
    out_gain.wait()
    for n in (A_IN, A_REST):
        waiting(k.other.at[:, 0:(768, 2432)[n]], S.w_sib.at[n]).wait_send()
    for piece in sum(gather + scatter, []):
        piece.drain()
    for copy in [gain_sib, keep_sib, gy_sib, n1_sib, edge]:
        copy.wait_send()
    for group in trades + [s_dn1, g_n2, g_bo, g_dh, g_gt]:
        group.drain()


def block(*arrays):
    sems = []
    for _, shape in fields(Sems):
        sems += [pltpu.SemaphoreType.DMA(a) for a in shape]
    vmem = pl.BlockSpec(memory_space=pltpu.VMEM)
    return pl.pallas_call(
        kernel,
        out_shape=(
            jax.ShapeDtypeStruct((128, 2048), BF16),
            jax.ShapeDtypeStruct((128, 2048), BF16),
            jax.ShapeDtypeStruct((2, 64, LANES_A + LANES_B), BF16),
            jax.ShapeDtypeStruct((2, 80, 256), F32),
            jax.ShapeDtypeStruct((8, 128), F32),
        ),
        in_specs=[vmem] * len(arrays),
        out_specs=[pl.BlockSpec(memory_space=pl.ANY)] * 5,
        scratch_shapes=[pltpu.VMEM(*value) for _, value in fields(Scratch)] + sems + [pltpu.SemaphoreType.DMA((5,))],
        compiler_params=pltpu.CompilerParams(
            collective_id=0, has_side_effects=True, vmem_limit_bytes=63 * 2**20
        ),
        name="block",
    )(*arrays)


def results(*refs):
    sources, refs = refs[:5], refs[5:]
    outs, refs = refs[:14], refs[14:]
    (bo, gt, g_gain_1, g_in, g_taps, g_decay, g_angle, g_re, g_im, g_out, g_gain_2, g_gate, g_up, g_down) = refs[:14]
    grad_w, small, gain, sems = refs[14:]
    c = lax.rem(lax.axis_index("seq"), 2)
    copies = [
        pltpu.make_async_copy(source, ref, sems.at[i])
        for i, (source, ref) in enumerate(zip(sources, (bo, gt, grad_w, small, gain)))
    ]
    leaving = [pltpu.make_async_copy(ref, out, sems.at[5 + i]) for i, (ref, out) in enumerate(zip(refs, outs))]
    for copy in copies[::-1]:
        copy.start()
    for copy in copies[2:]:
        copy.wait()

    def cols(core, n, start, stop):
        wa = WHOLE[n][0][1]
        parts = []
        if start < wa:
            parts.append(grad_w[core, :, WHOLE[n][0][0] + start:WHOLE[n][0][0] + min(stop, wa)])
        if stop > wa:
            o = LANES_A + WHOLE[n][1][0]
            parts.append(grad_w[core, :, o + max(start - wa, 0):o + stop - wa])
        return jnp.concatenate(parts, 1).astype(F32)

    cores = ((0, c), (1, 1 - c))
    for at, core in cores:
        g_in[0, :, at * 256:at * 256 + 256] = cols(core, IN, 0, 256)
        for b in (1, 2):
            g_in[b, :, at * 256:at * 256 + 256] = cols(core, IN_2, b * 256 - 256, b * 256)
    leaving[3].start()
    for at, core in cores:
        g_gate[:, at * 640:at * 640 + 640] = cols(core, GU, 0, 640)
        g_up[:, at * 640:at * 640 + 640] = cols(core, GU, 640, 1280)
    first, second = cols(c, GU, 1280, 1408), cols(1 - c, GU, 1280, 1408)
    g_gate[:, 1280:1408] = jnp.concatenate([first[:, 0:64], second[:, 0:64]], 1)
    g_up[:, 1280:1408] = jnp.concatenate([first[:, 64:128], second[:, 64:128]], 1)
    leaving[11].start()
    leaving[12].start()
    for copy in copies[:2]:
        copy.wait()
    leaving[0].start()
    leaving[1].start()
    for at, core in cores:
        g_down[:, at * 640:at * 640 + 640] = cols(core, DOWN, 0, 640)
    first, second = cols(c, DOWN, 640, 768), cols(1 - c, DOWN, 640, 768)
    g_down[:, 1280:1408] = jnp.concatenate([first[:, 0:64], second[:, 0:64]], 1)
    leaving[13].start()
    for at, core in cores:
        here = slice(at * 256, at * 256 + 256)
        g_out[:, here] = cols(core, OUT, 0, 256)
        for i, ref in enumerate((g_decay, g_angle, g_re, g_im)):
            ref[:, here] = small[core, 16 * i:16 * i + 16, :]
        for i in range(3):
            g_taps[i, :, here] = small[core, 64 + 3 * i:67 + 3 * i, :]
    for i, ref in enumerate((g_gain_1, g_gain_2)):
        a = gain[i:i + 1, :]
        ref[...] = jnp.where(c == 0, a[:, 0:64], a[:, 64:128])
    for i in (9, 4, 5, 6, 7, 8, 2, 10):
        leaving[i].start()
    for copy in leaving:
        copy.wait()


def on_device(
    tokens, cotangent, resets, norm1_gain, in_weight, conv_weight, pole_decay, pole_angle, residue_re, residue_im,
    out_weight, norm2_gain, gate_weight, up_weight, down_weight,
):
    raw = block(
        in_weight.transpose(1, 0, 2), out_weight, gate_weight, up_weight, down_weight, norm1_gain.reshape(1, 64),
        norm2_gain.reshape(1, 64), resets.reshape(1, 128), tokens, cotangent, conv_weight, pole_decay, pole_angle,
        residue_re, residue_im,
    )
    shapes = [
        ((128, 2048), BF16), ((128, 2048), BF16), ((1, 64), F32), ((3, 64, 512), F32), ((3, 3, 512), F32),
        ((16, 512), F32), ((16, 512), F32), ((16, 512), F32), ((16, 512), F32), ((64, 512), F32), ((1, 64), F32),
        ((64, 1408), F32), ((64, 1408), F32), ((64, 1408), F32),
    ]
    outs = list(pl.pallas_call(
        results,
        out_shape=[jax.ShapeDtypeStruct(s, t) for s, t in shapes],
        in_specs=[pl.BlockSpec(memory_space=pl.ANY)] * len(raw),
        out_specs=[pl.BlockSpec(memory_space=pl.ANY)] * len(shapes),
        scratch_shapes=[pltpu.VMEM(*a) for a in shapes] + [pltpu.VMEM(a.shape, a.dtype) for a in raw[2:]]
        + [pltpu.SemaphoreType.DMA((19,))],
        compiler_params=pltpu.CompilerParams(vmem_limit_bytes=60 * 2**20),
        name="results",
    )(*raw))
    outs[2], outs[10] = outs[2].reshape(64), outs[10].reshape(64)
    outs[3] = outs[3].transpose(1, 0, 2)
    return tuple(outs)


def solution(mesh):
    row, cols = P("seq", "mp"), P(None, "mp")
    return jax.shard_map(
        on_device,
        mesh=mesh,
        in_specs=(
            P("seq", None), P("seq", None), P("seq"), P("seq"), P("seq", None, "mp"), P(None, None, "mp"),
            cols, cols, cols, cols, row, P("seq"), row, row, row,
        ),
        out_specs=(
            P("seq", None), P("seq", None), P("seq"), P("seq", None, "mp"), P(None, None, "mp"),
            cols, cols, cols, cols, row, P("seq"), row, row, row,
        ),
        check_vma=False,
    )
```

```python
import functools

import jax
import jax.numpy as jnp
from jax import lax
from jax.experimental import pallas as pl
from jax.experimental.pallas import tpu as pltpu
from jax.sharding import PartitionSpec as P

EPSILON = 1e-05
BF16, F32 = jnp.bfloat16, jnp.float32
MESH = pl.DeviceIdType.MESH
LANES_A, LANES_B = 1664, 1536
CHUNKS = (
    ((0, 128), (0, 128)),
    ((128, 256), (128, 256)),
    ((384, 128), (384, 128)),
    ((512, 384), (512, 384)),
    ((896, 384), (896, 256)),
    ((1280, 384), (1152, 384)),
)
IN, IN_2, OUT, GU, GU_2, DOWN = range(6)
def pieces(a, b, last=False):
    both = [(0, 0, *a, 0, 128), (1, 1, *b, 0, 128)]
    return both + [(0, 0, 1536, 128, 0, 64), (1, 0, 1536, 128, 64, 64)] * last


GATHERS = (
    (0, False, pieces((0, 384), (0, 384))),
    (0, False, pieces((384, 1152), (384, 1152), True)),
    (1, True, pieces((0, 384), (0, 384))),
    (1, False, pieces((384, 128), (384, 128))),
    (1, True, pieces((512, 384), (512, 384))),
    (1, True, pieces((896, 384), (896, 256))),
    (1, True, pieces((1280, 256), (1152, 384), True)),
)
A_IN, A_REST, B_IN, B_OUT, B_GU, B_GU_2, B_DOWN = range(7)
SECOND = (CHUNKS[0], CHUNKS[1], CHUNKS[2], ((512, 768), (512, 640)), CHUNKS[5])
SCATTERS = [pieces(*parts) for parts in CHUNKS[:5] + SECOND[:4]]
SCATTERS = SCATTERS[:5] + [pieces((1280, 256), (1152, 384), True)] + SCATTERS[5:] + [pieces((1280, 256), (1152, 384), True)]
S_IN, S_IN_2, S_OUT, S_GU, S_DOWN = range(6, 11)
WHOLE = {n: CHUNKS[n] for n in (IN, IN_2, OUT, DOWN)} | {GU: ((512, 768), (512, 640))}


def where():
    place = lax.axis_index("seq")
    chip = place // 2
    return chip // 4, lax.rem(chip, 4), lax.rem(place, 2), lax.axis_index("mp")


def device(z, y, c, x):
    return ((z * 4 + y) * 2 + c, x)


def rem4(a):
    return lax.rem(a + 4, 4)


def remote(src, dst, send, recv, to):
    return pltpu.make_async_remote_copy(
        src_ref=src, dst_ref=dst, send_sem=send, recv_sem=recv, device_id=to, device_id_type=MESH
    )


def waiting(ref, sem):
    return remote(ref, ref, sem, sem, device(0, 0, 0, 0))


def nn(a, b):
    return jnp.dot(a, b, preferred_element_type=F32)


def nt(a, b):
    return lax.dot_general(a, b, (((1,), (1,)), ((), ())), preferred_element_type=F32)


def tn(a, b):
    return lax.dot_general(a, b, (((0,), (0,)), ((), ())), preferred_element_type=F32)


def expm1(x):
    series = x / 8.0 + 1.0
    for n in range(7, 1, -1):
        series = series * (x / n) + 1.0
    return jnp.where(jnp.abs(x) < 0.25, x * series, jnp.exp(x) - 1.0)


def fold(count, body, state):
    return lax.fori_loop(0, count, body, state)


def loop(count, body):
    lax.fori_loop(0, count, lambda i, _: (body(i), 0)[1], 0)


def span(start, size):
    return pl.ds(pl.multiple_of(start, size), size)


(
    START, GAIN_Y, GAIN_Z, NORM_1, EDGE, PROJECT, SHORT, ENDS_Y,
    ENDS_Z, SCAN, MIX, MIX_0, MIX_1, MIX_2, N2_0, N2_1,
    FF, ACT, DA, DN2_0, DN2_1, DN2_2, DH_0, DH_1,
    DZ, BACKS_Y, BACKS_Z, ADJOINT, DQ, DN1_0, DN1_X, DN1_1,
    DN1_2, GT_0, GT_1, GT_2, GT_3, GT_4,
) = range(38)
AG, RS, WG, FFN, SMALL, SHORT_1 = range(6)
PLAN = {
    START: ((AG, A_IN, 1),),
    GAIN_Y: ((AG, A_REST, 1), (AG, A_IN, 3),),
    GAIN_Z: ((AG, A_REST, 3), (AG, A_IN, 4), (AG, B_IN, 1),),
    NORM_1: ((AG, B_IN, 2),),
    EDGE: ((AG, B_IN, 3), (AG, A_REST, 4), (AG, B_GU_2, 1), (AG, B_OUT, 1),),
    PROJECT: ((AG, B_IN, 4),),
    ENDS_Y: ((AG, B_GU, 1),),
    ENDS_Z: ((AG, B_OUT, 3), (AG, B_DOWN, 1), (AG, B_GU, 2), (AG, B_GU, 3), (AG, B_GU_2, 2),),
    MIX: ((AG, B_OUT, 4),),
    MIX_0: ((AG, B_GU_2, 3),),
    N2_0: ((AG, B_GU, 4), (AG, B_DOWN, 2), (AG, B_DOWN, 3),),
    FF: ((AG, B_GU_2, 4),),
    ACT: ((WG, DOWN), (RS, DOWN, 0), (RS, DOWN, 1), (AG, B_DOWN, 4),),
    DN2_1: ((RS, DOWN, 2), (WG, GU),),
    DN2_2: ((RS, GU, 0), (RS, GU_2, 0), (FFN, 0), (RS, GU_2, 1),),
    DH_1: ((RS, GU, 1),),
    BACKS_Y: ((RS, GU_2, 2), (WG, OUT), (RS, OUT, 0), (FFN, 1), (SHORT_1,), (WG, IN),),
    BACKS_Z: ((RS, IN, 0), (RS, GU, 2), (RS, GU_2, 3), (RS, IN, 1), (FFN, 2),),
    DQ: ((RS, OUT, 1), (RS, OUT, 2), (RS, IN, 2), (RS, GU, 3), (RS, S_GU, 0),),
    DN1_0: ((WG, IN_2), (RS, IN_2, 0),),
    DN1_1: ((RS, IN_2, 1), (SMALL, 0),),
    DN1_2: ((FFN, 3), (RS, IN, 3), (RS, OUT, 3), (RS, S_IN, 0), (RS, IN_2, 2),),
    GT_0: ((RS, DOWN, 3), (RS, S_DOWN, 0), (FFN, 4), (SMALL, 1), (RS, S_OUT, 0),),
    GT_1: ((RS, IN_2, 3), (RS, S_IN_2, 0), (RS, S_IN, 1),),
    GT_2: ((RS, S_DOWN, 1), (RS, S_GU, 1), (SMALL, 2), (RS, S_IN_2, 1),),
    GT_3: ((RS, S_OUT, 1), (RS, S_IN, 2), (RS, S_DOWN, 2), (FFN, 5),),
    GT_4: ((RS, S_GU, 2), (RS, S_IN_2, 2), (RS, S_OUT, 2),),
}


class Rings:
    def __init__(self):
        self.z, self.y, self.c, self.x = where()
        self.chip = self.z * 4 + self.y
        self.sib = device(self.z, self.y, 1 - self.c, self.x)

    def near(self, axis, d, other=False):
        c = 1 - self.c if other else self.c
        if axis == 0:
            return device(rem4(self.z + d), self.y, c, self.x)
        if axis == 1:
            return device(self.z, rem4(self.y + d), c, self.x)
        return device(self.z, self.y, c, rem4(self.x + d))

    def along(self, d):
        return (lax.rem(self.chip + d + 16, 16) * 2 + self.c, self.x)


class Gather:
    def __init__(self, r, ref, lanes, rows, phase, axis, split, send, recv, own=None):
        self.r, self.ref, self.lanes, self.rows, self.own = r, ref, lanes, rows, own
        self.phase, self.axis, self.split = phase, axis, split
        self.send, self.recv, self.sent = send, recv, []

    def copy(self, d, part, to, i):
        r, axis = self.r, self.axis
        z, y = (rem4(r.z + d), r.y) if axis == 0 else (r.z, rem4(r.y + d))
        if self.phase == 0:
            o, n = self.rows
            rows = (pl.ds(o, n), pl.ds(o, n // 2), pl.ds(o + n // 2, n // 2))[part]
            ref = self.ref.at[z, y, rows, self.lanes]
        else:
            many, rows = (pl.ds(0, 4), pl.ds(0, 2), pl.ds(2, 2))[part], pl.ds(*self.rows)
            ref = self.ref.at[z, many, rows, self.lanes] if axis == 0 else self.ref.at[many, y, rows, self.lanes]
        return remote(ref, ref, self.send, self.recv.at[i], r.near(axis, to))

    def start(self, *a):
        copy = self.copy(*a)
        copy.start()
        self.sent.append(copy)

    def step(self, i):
        if i == 1 and self.own:
            there = self.ref.at[self.r.z, self.r.y, self.own[1], self.lanes]
            for j, d in enumerate((1, -1)):
                for other, src in enumerate((there, self.own[0])):
                    to = self.r.near(self.axis, d, bool(other))
                    self.sent.append(remote(src, there, self.send, self.recv.at[j], to))
                    self.sent[-1].start()
        elif i == 1 and not self.split:
            self.start(0, 0, 1, 0)
            self.start(0, 0, -1, 1)
        elif i == 1:
            self.start(0, 1, 1, 0)
            self.start(0, 2, -1, 1)
        elif i == 2 and not self.split:
            pass
        elif i == 2:
            self.start(0, 2, 1, 2)
            self.start(0, 1, -1, 2)
        elif i == 3:
            self.copy(-1, 1 if self.split else 0, 1, 0).wait_recv()
            self.start(-1, 1, 1, 2)
            self.copy(1, 2 if self.split else 0, -1, 1).wait_recv()
            self.start(1, 2, -1, 2)
        else:
            waiting(self.units(2 if self.split else 1), self.recv.at[2]).wait_recv()

    def units(self, count):
        rows = pl.ds(*self.rows)
        if self.phase == 0:
            return self.ref.at[0, pl.ds(0, count), rows, self.lanes]
        return self.ref.at[pl.ds(0, count), :, rows, self.lanes]

    def drain(self):
        if self.sent:
            waiting(self.units(3), self.send).wait_send()
        self.sent = []


class Trade:
    def __init__(self, r, axis, src, land, send, recv):
        self.r, self.axis, self.src, self.land, self.send, self.recv = r, axis, src, land, send, recv
        self.me, self.sent = (r.z, r.y, r.x)[axis], []

    def copy(self, d):
        return remote(
            self.src(rem4(self.me + d)), self.land.at[self.me], self.send, self.recv,
            self.r.near(self.axis, d),
        )

    def begin(self):
        for d in (2, 1, 3):
            copy = self.copy(d)
            copy.start()
            self.sent.append(copy)

    def end(self):
        waiting(self.land.at[0:3], self.recv).wait_recv()

    def drain(self):
        if self.sent:
            waiting(self.land.at[0:3], self.send).wait_send()


class Scatter:
    def __init__(self, r, ref, lanes, rows, at, phase, axis, buf, send, recv):
        self.r, self.ref, self.lanes, self.rows, self.at = r, ref, lanes, rows, at
        self.phase, self.axis, self.buf, self.send, self.recv, self.sent = phase, axis, buf, send, recv, []

    def unit(self, d, part):
        r, axis = self.r, self.axis
        z, y = (rem4(r.z + d), r.y) if axis == 0 else (r.z, rem4(r.y + d))
        if self.phase == 1:
            o, n = self.rows
            return self.ref.at[z, y, pl.ds(o + n // 2 * part, n // 2), self.lanes]
        many, rows = pl.ds(2 * part, 2), pl.ds(*self.rows)
        return self.ref.at[z, many, rows, self.lanes] if axis == 0 else self.ref.at[many, y, rows, self.lanes]

    def landing(self, i):
        o, n = self.rows
        if self.phase == 0:
            return self.buf.at[i, :, pl.ds(o, n), self.at]
        return self.buf.at[i, pl.ds(o // 2, n // 2), self.at]

    def copy(self, d, part, to, i):
        return remote(
            self.unit(d, part), self.landing(i), self.send, self.recv.at[min(i, 2)],
            self.r.near(self.axis, to),
        )

    def start(self, *a):
        copy = self.copy(*a)
        copy.start()
        self.sent.append(copy)

    def arrived(self, i):
        self.copy(0, 0, 1, i).wait_recv()

    def add(self, d, part, many):
        unit = self.unit(d, part)
        lands, many = [self.landing(i) for i in many], self.rows[1] // 32
        if self.phase == 0:
            def body(i):
                k, rows = i // many, span(lax.rem(i, many) * 32, 32)
                total = unit[k, rows, :].astype(F32)
                for l in lands:
                    total = total + l[k, rows, :].astype(F32)
                unit[k, rows, :] = total.astype(BF16)
            loop(2 * many, body)
        else:
            def body(i):
                rows = span(i * 32, 32)
                total = unit[rows, :].astype(F32)
                for l in lands:
                    total = total + l[rows, :].astype(F32)
                unit[rows, :] = total.astype(BF16)
            loop(many // 2, body)

    def far(self):
        self.start(2, 0, 1, 0)
        self.start(2, 1, -1, 1)

    def early(self):
        self.start(1, 1, 1, 3)
        self.start(-1, 0, -1, 4)

    def forward(self):
        self.arrived(0)
        self.add(1, 0, (0,))
        self.start(1, 0, 1, 2)
        self.arrived(1)
        self.add(-1, 1, (1,))
        self.start(-1, 1, -1, 5)

    def units(self, count):
        o, n = self.rows
        if self.phase == 0:
            return self.buf.at[pl.ds(0, 2 * count), :, pl.ds(o, n), self.at]
        return self.buf.at[pl.ds(0, 2 * count), pl.ds(o // 2, n // 2), self.at]

    def finish(self):
        waiting(self.units(2), self.recv.at[2]).wait_recv()
        self.add(0, 0, (2, 4))
        self.add(0, 1, (3, 5))

    def drain(self):
        if self.sent:
            waiting(self.units(3), self.send).wait_send()
        self.sent = []


class CrossSum:
    def __init__(self, r, part, got, mid, one, two, send, recv):
        self.r, self.part, self.got, self.mid, self.one, self.two = r, part, got, mid, one, two
        self.send, self.recv, self.sent = send, recv, []

    def start(self, copy):
        copy.start()
        self.sent.append(copy)

    def rows(self, c, x):
        return span((c * 4 + x) * 32, 32)

    def pair(self, d):
        x = rem4(self.r.x + d)
        return remote(
            self.part.at[self.rows(1 - self.r.c, x)], self.got.at[x],
            self.send, self.recv.at[(4, 1, 0, 1)[d]], self.r.sib,
        )

    def begin(self):
        for d in (2, 1, 3, 0):
            self.start(self.pair(d))

    def pairsum(self, d):
        x = rem4(self.r.x + d)
        rows = self.rows(self.r.c, x)
        self.mid[x] = (self.part[rows].astype(F32) + self.got[x].astype(F32)).astype(BF16)

    def far(self, side):
        x = rem4(self.r.x + 2)
        return remote(
            self.mid.at[x, pl.ds(16 * side, 16)], self.one.at[side],
            self.send, self.recv.at[2 + side], self.r.near(2, 1 - 2 * side),
        )

    def late(self, side, summed):
        d = 1 - 2 * side
        x = rem4(self.r.x + d)
        half = side if summed else 1 - side
        return remote(
            self.mid.at[x, pl.ds(16 * half, 16)], self.two.at[side, pl.ds(16 * half, 16)],
            self.send, self.recv.at[4], self.r.near(2, d),
        )

    def middle(self):
        self.near_half()
        self.far_half()

    def near_half(self):
        self.pair(2).wait_recv()
        self.pairsum(2)
        self.start(self.far(0))
        self.start(self.far(1))
        waiting(self.part.at[0:64], self.recv.at[1]).wait_recv()
        self.pairsum(1)
        self.start(self.late(0, 0))
        self.pairsum(3)
        self.start(self.late(1, 0))

    def far_half(self):
        for side in range(2):
            self.far(side).wait_recv()
            x = rem4(self.r.x + 1 - 2 * side)
            rows = pl.ds(16 * side, 16)
            self.mid[x, rows] = (self.mid[x, rows].astype(F32) + self.one[side].astype(F32)).astype(BF16)
            self.start(self.late(side, 1))

    def end(self):
        waiting(self.part.at[0:96], self.recv.at[4]).wait_recv()

    def result(self, rows):
        base = (self.r.c * 4 + self.r.x) * 32
        own = self.part[pl.ds(pl.multiple_of(base + rows.start, rows.size), rows.size)].astype(F32)
        own = own + self.got[self.r.x, rows].astype(F32)
        return own + self.two[0, rows].astype(F32) + self.two[1, rows].astype(F32)

    def drain(self):
        if self.sent:
            waiting(self.part.at[0:224], self.send).wait_send()
        self.sent = []


class CrossGather:
    def __init__(self, r, ref, both, send, recv):
        self.r, self.ref, self.both, self.send, self.recv, self.sent = r, ref, both, send, recv, []

    def start(self, copy):
        copy.start()
        self.sent.append(copy)

    def rows(self, d, part):
        base = rem4(self.r.x + d) * 32
        if self.both:
            base = base + self.r.c * 128
        if part is None:
            return self.ref.at[pl.ds(pl.multiple_of(base, 32), 32)]
        return self.ref.at[pl.ds(pl.multiple_of(base + 16 * part, 16), 16)]

    def ring(self, d, part, to, i):
        ref = self.rows(d, part)
        return remote(ref, ref, self.send, self.recv.at[i], self.r.near(2, to))

    def pair(self, d):
        ref = self.rows(d, None)
        return remote(ref, ref, self.send, self.recv.at[4], self.r.sib)

    def begin(self):
        self.start(self.ring(0, 0, 1, 0))
        self.start(self.ring(0, 1, -1, 1))
        self.start(self.ring(0, 1, 1, 2))
        self.start(self.ring(0, 0, -1, 2))
        if self.both:
            self.start(self.pair(0))

    def middle(self):
        self.ring(-1, 0, 1, 0).wait_recv()
        self.start(self.ring(-1, 0, 1, 3))
        self.ring(1, 1, -1, 1).wait_recv()
        self.start(self.ring(1, 1, -1, 3))
        waiting(self.ref.at[0:32], self.recv.at[2]).wait_recv()
        if self.both:
            self.start(self.pair(-1))
            self.start(self.pair(1))

    def end(self):
        waiting(self.ref.at[0:32], self.recv.at[3]).wait_recv()
        if self.both:
            self.start(self.pair(2))
            waiting(self.ref.at[0:128], self.recv.at[4]).wait_recv()

    def drain(self):
        waiting(self.ref.at[0:224 if self.both else 96], self.send).wait_send()


class Refs:
    pass


class Inputs:
    in_w = out_w = gate_w = up_w = down_w = gain_1 = gain_2 = resets = tok = cot = conv_w = 0
    decay = angle = res_re = res_im = 0


class Outputs:
    block_out = grad_tok = grad_w = grad_small = grad_gain = 0


class Scratch:
    other = ((64, LANES_A + LANES_B), BF16)
    tab = ((8, 16, 256), F32)
    ga = ((4, 4, 128, LANES_A), BF16)
    gb = ((4, 4, 128, LANES_B), BF16)
    s0a = ((6, 2, 128, LANES_A), BF16)
    s0b = ((6, 2, 128, LANES_B), BF16)
    s1a = ((6, 64, LANES_A), BF16)
    s1b = ((6, 64, LANES_B), BF16)
    da = ((4, 4, 128, 384), BF16)
    ia = ((4, 4, 128, 128), BF16)
    ib = ((4, 4, 128, 128), BF16)
    db = ((4, 4, 128, 384), BF16)
    sib_a = ((64, LANES_A), BF16)
    sib_b = ((64, LANES_B), BF16)
    gain_pair = ((2, 8, 128), F32)
    gains_y = ((4, 8, 128), F32)
    gains_all = ((4, 4, 8, 128), F32)
    gains = ((8, 2048), F32)
    gain_in = ((8, 128), F32)
    taps = ((8, 768), F32)
    keep = ((256, 256), F32)
    tok_here = ((128, 2048), BF16)
    gy = ((256, 2048), BF16)
    n1 = ((272, 2048), BF16)
    n2 = ((256, 2048), BF16)
    dh = ((256, 2048), BF16)
    part = ((256, 2048), BF16)
    mid = ((4, 32, 2048), BF16)
    part_f = ((256, 2048), BF16)
    mid_f = ((4, 32, 2048), BF16)
    got = ((4, 4, 32, 2048), BF16)
    one = ((4, 2, 16, 2048), BF16)
    two = ((4, 2, 32, 2048), BF16)
    bo = ((128, 2048), BF16)
    gt = ((128, 2048), BF16)
    h = ((32, 2048), F32)
    dhf = ((32, 2048), F32)
    p = ((272, 768), F32)
    q0 = ((256, 256), F32)
    q1 = ((256, 256), F32)
    q2 = ((256, 256), F32)
    u = ((256, 256), F32)
    v = ((256, 256), F32)
    z = ((256, 256), BF16)
    st_re = ((257, 16, 256), F32)
    st_im = ((257, 16, 256), F32)
    ends_y = ((4, 32, 256), BF16)
    ends_z = ((4, 32, 256), BF16)
    backs_y = ((4, 32, 256), BF16)
    backs_z = ((4, 32, 256), BF16)
    gu = ((256, 1408), F32)
    act = ((256, 768), BF16)
    dgu = ((256, 1408), BF16)
    dv = ((256, 256), F32)
    dq = ((264, 768), F32)
    dp = ((256, 768), BF16)
    small_y = ((4, 80, 256), BF16)
    small_z = ((4, 80, 256), BF16)
    small_sum = ((80, 256), F32)
    small_sib = ((80, 256), F32)
    ggain = ((8, 2048), F32)
    gg_z = ((4, 8, 512), F32)
    gg_1 = ((8, 512), F32)
    gg_y = ((4, 8, 128), F32)
    gg_2 = ((8, 128), F32)
    gg_s = ((8, 128), F32)
    gg_x = ((4, 8, 128), F32)
    gg_out = ((8, 128), F32)


def fields(group):
    return [(name, value) for name, value in vars(group).items() if name[0] != "_"]


class Sems:
    w = (18,), (18, 3)
    w_sib = (2,), (2,)
    gain_sib = keep_s = gy_s = n1_s = edge = dq_s = dq_1 = small_x = gg_s = (), ()
    trade = (11,), (11,)
    sum = (4,), (4, 5)
    cg = (4,), (4, 5)
    rs = (26,), (26, 3)
    rs_sib = (5,), (5,)


def kernel(*refs):
    names = [name for group in (Inputs, Outputs, Scratch) for name, _ in fields(group)]
    k, S, R = Refs(), Refs(), Refs()
    for name, ref in zip(names, refs):
        setattr(k, name, ref)
    rest = refs[len(names):]
    for i, (name, _) in enumerate(fields(Sems)):
        setattr(S, name, rest[2 * i])
        setattr(R, name, rest[2 * i + 1])
    local = rest[-1]
    r = Rings()
    g = (k.ga, k.gb)
    z, y, c, x = r.z, r.y, r.c, r.x

    barrier = pltpu.get_barrier_semaphore()
    peers = [r.sib] + [r.near(a, d) for a in range(3) for d in (1, 2, 3)] + [r.along(1), r.along(-1)]
    peers += [r.near(a, d, True) for a in range(2) for d in (1, -1)]
    for peer in peers:
        pl.semaphore_signal(barrier, inc=1, device_id=peer, device_id_type=MESH)

    def lanes(n, h):
        o, w = CHUNKS[n][h]
        return pl.ds(o, w)

    def columns(n, start, stop):
        (oa, wa), (ob, _) = WHOLE[n]
        parts = []
        if start < wa:
            parts.append(g[0][:, :, :, oa + start:oa + min(stop, wa)])
        if stop > wa:
            parts.append(g[1][:, :, :, ob + max(start - wa, 0):ob + stop - wa])
        return jnp.concatenate([p.reshape(2048, p.shape[-1]) for p in parts], 1)

    def weight(n, h, i):
        o, w = WHOLE[n][h]
        return g[h][i, :, :, o:o + w].reshape(512, w)

    trades = []

    def trade(axis, src, land):
        i = len(trades)
        trades.append(Trade(r, axis, src if callable(src) else lambda _: src, land, S.trade.at[i], R.trade.at[i]))
        return trades[-1]

    my64 = span(c * 64, 64)
    my128 = span(c * 128, 128)
    tok_copy = pltpu.make_async_copy(k.tok, k.tok_here, local.at[5])
    cot_copy = pltpu.make_async_copy(k.cot, k.gy.at[my128], local.at[6])
    tok_copy.start()
    cot_copy.start()
    gather = []
    for n, (phase, split, parts) in enumerate(GATHERS):
        first = sum(len(group) for group in gather)
        gather.append([
            Gather(r, g[b], pl.ds(o, w), rows, phase, 1 - way if phase == 0 else way, split and rows[1] == 128,
                   S.w.at[first + i], R.w.at[first + i],
                   (k.other.at[:, pl.ds(o + (LANES_A if b else 0), w)], my64) if n == A_IN else None)
            for i, (way, b, o, w, *rows) in enumerate(parts)
        ])

    def put(cc, n, sink):
        wa = WHOLE[n][0][1]

        def store(start, value):
            stop = start + value.shape[1]
            if start < wa:
                sink(0, WHOLE[n][0][0] + start, value[:, :min(stop, wa) - start])
            if stop > wa:
                sink(1, WHOLE[n][1][0] + max(start - wa, 0), value[:, max(wa - start, 0):])

        def main(ref):
            return ref[:, pl.ds(pl.multiple_of(cc * 640, 128), 640)]

        def tail(ref):
            a = ref[:, 1280:1408].astype(F32)
            return jnp.where(cc == 0, a[:, 0:64], a[:, 64:128])

        channels = pl.ds(pl.multiple_of(cc * 256, 256), 256)
        if n == IN:
            store(0, k.in_w[0, :, channels])
        elif n == IN_2:
            store(0, k.in_w[1, :, channels])
            store(256, k.in_w[2, :, channels])
        elif n == OUT:
            store(0, k.out_w[:, channels])
        elif n == GU:
            store(0, main(k.gate_w))
            store(640, main(k.up_w))
            store(1280, jnp.concatenate([tail(k.gate_w), tail(k.up_w)], 1).astype(BF16))
        else:
            store(0, main(k.down_w))
            store(640, jnp.concatenate([tail(k.down_w), jnp.zeros((64, 64), F32)], 1).astype(BF16))

    def to_other(h, at, value):
        at = at + (LANES_A if h else 0)
        k.other[:, at:at + value.shape[1]] = value

    def to_own(h, at, value):
        g[h][z, y, my64, at:at + value.shape[1]] = value

    def weight_sib(n, h):
        o, w = ((0, 384), (384, (1280, 1152)[h]))[n]
        return remote(
            k.other.at[:, pl.ds(o + (LANES_A if h else 0), w)], g[h].at[z, y, my64, pl.ds(o, w)],
            S.w_sib.at[n], R.w_sib.at[n], r.sib,
        )

    side = lax.broadcasted_iota(jnp.int32, (1, 128), 1) // 64 == c
    for i, ref in enumerate((k.gain_1, k.gain_2)):
        a = ref[...].astype(F32)
        k.gain_in[i:i + 1, :] = jnp.where(side, jnp.concatenate([a, a], 1), 0.0)
    k.gain_in[2:8, :] = jnp.zeros((6, 128), F32)
    for n in (IN, IN_2):
        put(1 - c, n, to_other)
        put(c, n, to_own)
    keep = 1.0 - k.resets[...].astype(F32)
    keep = jnp.broadcast_to(keep, (128, 128)).T
    k.keep[my128] = jnp.concatenate([keep, keep], 1)
    pl.semaphore_wait(barrier, len(peers))

    gain_sib = remote(k.gain_in, k.gain_pair.at[c], S.gain_sib, R.gain_sib, r.sib)
    keep_sib = remote(k.keep.at[my128], k.keep.at[my128], S.keep_s, R.keep_s, r.sib)
    gy_sib = remote(k.gy.at[my128], k.gy.at[my128], S.gy_s, R.gy_s, r.sib)
    def share(n):
        for h in range(2):
            weight_sib(n, h).start()

    share(A_IN)
    gain_sib.start()

    def ag(n, i):
        if (n, i) in ((A_IN, 4), (A_REST, 1)):
            waiting(k.other.at[:, 0:(768, 2432)[n]], R.w_sib.at[n]).wait_recv()
        for piece in gather[n]:
            piece.step(i)

    tasks = {}

    def at(point):
        for name, *rest in PLAN.get(point, ()):
            tasks[name](*rest)

    tasks[AG] = ag
    at(START)
    gain_y = trade(1, k.gains_y.at[y], k.gains_y)
    gain_z = trade(0, k.gains_y, k.gains_all)
    gain_sib.wait_recv()
    k.gains_y[y] = k.gain_in[...] + k.gain_pair[1 - c]
    gain_y.begin()

    for n in (OUT, GU, DOWN):
        put(1 - c, n, to_other)
        put(c, n, to_own)
    share(A_REST)
    keep_sib.start()
    at(GAIN_Y)
    gain_y.end()
    gain_z.begin()
    k.gains_all[z] = k.gains_y[...]
    at(GAIN_Z)
    cot_copy.wait()

    channels = pl.ds(pl.multiple_of(c * 256, 256), 256)
    decay, angle = k.decay[:, channels], k.angle[:, channels]
    size = jnp.exp(-decay)
    gin = jnp.sqrt(-expm1(-2.0 * decay))
    power = (size * jnp.cos(angle), size * jnp.sin(angle))
    k.tab[0], k.tab[1] = power
    k.tab[2] = gin * k.res_re[:, channels]
    k.tab[3] = gin * k.res_im[:, channels]
    for _ in range(8):
        power = (power[0] * power[0] - power[1] * power[1], 2.0 * power[0] * power[1])
    k.tab[4], k.tab[5] = power
    k.tab[6] = gin
    k.tab[7] = size * size / gin
    for i in range(3):
        for b in range(3):
            k.taps[i:i + 1, b * 256:b * 256 + 256] = k.conv_w[i, b:b + 1, channels]

    gain_z.end()
    for i in range(16):
        k.gains[:, i * 128:(i + 1) * 128] = k.gains_all[i // 4, i % 4]

    def norm_one(i):
        rows = span(i * 16, 16)
        a = k.tok_here[rows, :].astype(F32)
        s = lax.rsqrt(jnp.mean(a * a, axis=-1, keepdims=True) + EPSILON)
        k.n1[pl.ds(pl.multiple_of(16 + c * 128 + i * 16, 16), 16), :] = (a * s * k.gains[0:1, :]).astype(BF16)
    tok_copy.wait()
    loop(8, norm_one)

    def n1_rows(c):
        return k.n1.at[pl.ds(pl.multiple_of(16 + c * 128, 16), 128)]

    n1_sib = remote(n1_rows(c), n1_rows(c), S.n1_s, R.n1_s, r.sib)
    n1_sib.start()
    at(NORM_1)
    k_other = span((1 - c) * 128, 128)
    remote(n1_rows(1 - c), n1_rows(1 - c), S.n1_s, R.n1_s, r.sib).wait_recv()
    edge = remote(k.n1.at[256:272], k.n1.at[0:16], S.edge, R.edge, r.along(1))
    edge.start()
    gy_sib.start()
    at(EDGE)

    edge.wait_recv()
    at(PROJECT)

    def project(_):
        for o in range(0, 512, 256):
            k.p[:, 256 + o:512 + o] = nn(k.n1[...], columns(IN_2, o, o + 256))
        k.p[:, 0:256] = nn(k.n1[...], columns(IN, 0, 256))
    loop(1, project)

    def round_p(i):
        rows = span(i * 16, 16)
        k.p[rows, :] = k.p[rows, :].astype(BF16).astype(F32)
    loop(17, round_p)
    remote(k.keep.at[k_other], k.keep.at[k_other], S.keep_s, R.keep_s, r.sib).wait_recv()
    at(SHORT)

    def masks(i):
        rows = span(i * 16, 16)
        near = k.keep[rows, :]
        before = k.keep[span(jnp.maximum(i * 16 - 8, 0), 8), :]
        first = jnp.where(i == 0, 1.0, before[7:8, :])
        shifted = jnp.concatenate([first, near[0:15, :]], 0)
        return near, near * shifted

    def short(i):
        near, far = masks(i)
        ext = k.p[pl.ds(pl.multiple_of(i * 16 + 8, 8), 24), :]
        q = []
        for b in range(3):
            l = slice(b * 256, b * 256 + 256)
            e = ext[:, l]
            q.append(
                k.taps[0:1, l] * e[8:24] + near * k.taps[1:2, l] * e[7:23] + far * k.taps[2:3, l] * e[6:22]
            )
        rows = span(i * 16, 16)
        k.q0[rows, :] = q[0]
        k.q1[rows, :] = q[1]
        k.q2[rows, :] = q[2]
        k.u[rows, :] = q[1] * q[2]
    loop(16, short)

    zero = jnp.zeros((16, 256), F32)
    lr, li, cr, ci, pr, pi = (k.tab[i] for i in range(6))

    def advance(re, im, u, keep):
        kr, ki = keep * re, keep * im
        return lr * kr - li * ki + u, lr * ki + li * kr

    def end_state(i, state):
        rows = span(i * 8, 8)
        u, keep = k.u[rows, :], k.keep[rows, :]
        for j in range(8):
            state = advance(*state, u[j:j + 1, :], keep[j:j + 1, :])
        return state

    def times(a, b, g, h):
        return a * g - b * h, a * h + b * g

    def chain(own, ref_y, ref_z, sign, between):
        order = range(4) if sign > 0 else range(3, -1, -1)
        qr, qi = pr, sign * pi

        def put(ref, at, state):
            ref[at, 0:16] = state[0].astype(BF16)
            ref[at, 16:32] = state[1].astype(BF16)

        def horner(ref, wr, wi, state, here, every):
            for i in order:
                nr, ni = times(wr, wi, *state)
                nr, ni = nr + ref[i, 0:16].astype(F32), ni + ref[i, 16:32].astype(F32)
                use = (i < here) if sign > 0 else (i > here)
                state = (nr, ni) if every else (jnp.where(use, nr, state[0]), jnp.where(use, ni, state[1]))
            return state

        put(ref_y, y, own)
        t = trade(1, ref_y.at[y], ref_y)
        t.begin()
        at(between[0])
        t.end()
        put(ref_z, z, horner(ref_y, qr, qi, (zero, zero), y, True))
        t = trade(0, ref_z.at[z], ref_z)
        t.begin()
        at(between[1])
        t.end()
        w = times(*times(qr, qi, qr, qi), *times(qr, qi, qr, qi))
        return horner(ref_y, qr, qi, horner(ref_z, *w, (zero, zero), z, False), y, False)

    end = fold(32, end_state, (zero, zero))
    enter = chain(end, k.ends_y, k.ends_z, 1, (ENDS_Y, ENDS_Z))
    k.st_re[0] = enter[0]
    k.st_im[0] = enter[1]
    at(SCAN)

    def scan(i, state):
        rows = span(i * 8, 8)
        u, keep = k.u[rows, :], k.keep[rows, :]
        for j in range(8):
            state = advance(*state, u[j:j + 1, :], keep[j:j + 1, :])
            k.st_re[i * 8 + j + 1] = state[0]
            k.st_im[i * 8 + j + 1] = state[1]
            k.v[pl.ds(i * 8 + j, 1), :] = jnp.sum(cr * state[0] - ci * state[1], axis=0, keepdims=True)
        return state
    fold(32, scan, enter)

    def gated(i):
        rows = span(i * 32, 32)
        k.z[rows, :] = (k.q0[rows, :] * k.v[rows, :]).astype(BF16)
    loop(8, gated)

    at(MIX)
    def out_weight(i):
        return jnp.concatenate([weight(OUT, 0, i), weight(OUT, 1, i)], 1)

    def mix(i):
        k.part[:, span(i * 512, 512)] = nt(k.z[...], out_weight(i)).astype(BF16)
    loop(4, mix)

    def cross(i):
        part, mid = (k.part_f, k.mid_f) if i == 1 else (k.part, k.mid)
        return CrossSum(r, part, k.got.at[i], mid, k.one.at[i], k.two.at[i], S.sum.at[i], R.sum.at[i])

    s_mix = cross(0)
    s_mix.begin()
    at(MIX_0)
    s_mix.near_half()
    at(MIX_1)
    s_mix.far_half()
    at(MIX_2)
    s_mix.end()

    own = (c * 4 + x) * 32

    def norm_two(i):
        rows = pl.ds(pl.multiple_of(i * 16, 16), 16)
        a = k.tok_here[pl.ds(pl.multiple_of(x * 32 + i * 16, 16), 16), :].astype(F32) + s_mix.result(rows)
        k.h[rows, :] = a
        s = lax.rsqrt(jnp.mean(a * a, axis=-1, keepdims=True) + EPSILON)
        k.n2[pl.ds(pl.multiple_of(own + i * 16, 16), 16), :] = (a * s * k.gains[1:2, :]).astype(BF16)
    loop(2, norm_two)
    g_n2 = CrossGather(r, k.n2, True, S.cg.at[0], R.cg.at[0])
    g_n2.begin()
    at(N2_0)
    g_n2.middle()
    at(N2_1)
    g_n2.end()
    s_mix.drain()
    at(FF)

    def gate_up(_):
        for o in range(0, 1408, 256):
            e = min(o + 256, 1408)
            k.gu[:, o:e] = nn(k.n2[...], columns(GU, o, e))
    loop(1, gate_up)
    def halves(t):
        last = t[:, 1280:1408]
        turned = jnp.concatenate([last[:, 64:128], last[:, 0:64]], 1)
        return jnp.concatenate([t[:, 0:640], last], 1), jnp.concatenate([t[:, 640:1280], turned], 1)

    used = lax.broadcasted_iota(jnp.int32, (1, 768), 1) < 704

    def activate(i):
        rows = span(i * 16, 16)
        gate, up = halves(k.gu[rows, :])
        k.act[rows, :] = jnp.where(used, gate * jax.nn.sigmoid(gate) * up, 0.0).astype(BF16)
    loop(16, activate)

    def down_weight(i):
        return jnp.concatenate([weight(DOWN, 0, i), weight(DOWN, 1, i)], 1)

    s_ffn = cross(1)
    g_bo = CrossGather(r, k.bo, False, S.cg.at[1], R.cg.at[1])
    out_bo = pltpu.make_async_copy(k.bo, k.block_out, local.at[0])

    def ffn_step(i):
        if i == 0:
            def ffn(i):
                k.part_f[:, span(i * 512, 512)] = nt(k.act[...], down_weight(i)).astype(BF16)
            loop(4, ffn)
            s_ffn.begin()
        elif i == 1:
            s_ffn.near_half()
        elif i == 2:
            s_ffn.far_half()
        elif i == 3:
            s_ffn.end()

            def top(i):
                rows = pl.ds(pl.multiple_of(i * 16, 16), 16)
                here = pl.ds(pl.multiple_of(x * 32 + i * 16, 16), 16)
                k.bo[here, :] = (k.h[rows, :] + s_ffn.result(rows)).astype(BF16)
            loop(2, top)
            s_ffn.drain()
            g_bo.begin()
        elif i == 4:
            g_bo.middle()
        else:
            g_bo.end()
            out_bo.start()

    tasks[FFN] = ffn_step

    apart = {DOWN: (k.da, k.db), IN: (k.ia, k.ib)}
    scatter = []
    for n, parts in enumerate(SCATTERS):
        phase = 0 if n < S_IN else 1
        m = {S_IN: IN, S_DOWN: DOWN}.get(n, n if phase == 0 else None)
        first = sum(len(group) for group in scatter)
        scatter.append([])
        for i, (way, b, o, w, *rows) in enumerate(parts):
            ref, here = g[b], pl.ds(o, w)
            if m in apart:
                ref, here = apart[m][b], pl.ds(o - CHUNKS[m][b][0], w)
            buf = ((k.s0a, k.s0b), (k.s1a, k.s1b))[phase][b]
            axis = 1 - way if phase == 0 else way
            scatter[n].append(
                Scatter(r, ref, here, rows, pl.ds(o, w), phase, axis, buf, S.rs.at[first + i], R.rs.at[first + i])
            )

    def finished(n, h):
        o, w = SECOND[n - S_IN][h]
        m = {S_IN: IN, S_DOWN: DOWN}.get(n)
        return (apart[m][h], pl.ds(0, w), pl.ds(o, w)) if m in apart else (g[h], pl.ds(o, w), pl.ds(o, w))

    sib_bufs = (k.sib_a, k.sib_b)

    def rs_sib(n, h):
        ref, here, at = finished(n, h)
        return remote(
            ref.at[z, y, span((1 - c) * 64, 64), here], sib_bufs[h].at[:, at],
            S.rs_sib.at[n - S_IN], R.rs_sib.at[n - S_IN], r.sib,
        )

    def rs(n, i):
        for s in scatter[n]:
            if n < S_IN:
                (s.far, s.early, s.forward, s.finish)[i]()
            elif i == 0:
                s.far()
                s.early()
            elif i == 1:
                s.forward()
            else:
                s.finish()
        if n >= S_IN and i == 2:
            for h in range(2):
                rs_sib(n, h).start()

    tasks[RS] = rs

    def wg(n):
        a, b, first = {
            IN: (k.n1, k.dp.at[:, 0:256], 16), IN_2: (k.n1, k.dp.at[:, 256:768], 16), OUT: (k.dh, k.z, 0),
            GU: (k.n2, k.dgu, 0), DOWN: (k.gy, k.act, 0),
        }[n]
        for m in {GU: (B_GU, B_GU_2), OUT: (B_OUT,), IN_2: (B_IN,)}.get(n, ()) + ((A_IN, A_REST) if n == GU else ()):
            for piece in gather[m]:
                piece.drain()
        (oa, wa), (ob, wb) = [(0, CHUNKS[n][h][1]) for h in range(2)] if n in apart else WHOLE[n]
        into = apart.get(n, g)

        def weight_grad(i):
            t = tn(a[pl.ds(first, 256), pl.ds(pl.multiple_of(i * 512, 512), 512)], b[...]).astype(BF16)
            into[0][i, :, :, oa:oa + wa] = t[:, 0:wa].reshape(4, 128, wa)
            into[1][i, :, :, ob:ob + wb] = t[:, wa:wa + wb].reshape(4, 128, wb)
        weight_grad.width = wa + wb
        loop(4, weight_grad)

    tasks[WG] = wg

    remote(k.gy.at[k_other], k.gy.at[k_other], S.gy_s, R.gy_s, r.sib).wait_recv()
    at(ACT)

    def d_act(_):
        for o in range(0, 768, 256):
            k.dq[0:256, o:o + 256] = nn(k.gy[...], columns(DOWN, o, o + 256))
    loop(1, d_act)
    at(DA)

    def d_gates(i):
        rows = span(i * 16, 16)
        gate, up = halves(k.gu[rows, :])
        da = k.dq[rows, :]
        sg = jax.nn.sigmoid(gate)
        dgate = da * up * sg * (1.0 + gate * (1.0 - sg))
        dup = da * (gate * sg)
        last = jnp.concatenate([dgate[:, 640:704], dup[:, 640:704]], 1)
        k.dgu[rows, :] = jnp.concatenate([dgate[:, 0:640], dup[:, 0:640], last], 1).astype(BF16)
    loop(16, d_gates)

    def d_n2(i):
        w = jnp.concatenate([weight(GU, 0, i), weight(GU, 1, i)], 1)
        k.part[:, span(i * 512, 512)] = nt(k.dgu[...], w).astype(BF16)
    loop(4, d_n2)
    s_dn2 = cross(2)
    s_dn2.begin()
    at(DN2_0)
    s_dn2.near_half()
    at(DN2_1)
    s_dn2.far_half()
    at(DN2_2)
    s_dn2.end()

    def d_norm_two(i):
        rows = pl.ds(pl.multiple_of(i * 16, 16), 16)
        a = k.h[rows, :]
        s = lax.rsqrt(jnp.mean(a * a, axis=-1, keepdims=True) + EPSILON)
        hat = a * s
        dn = s_dn2.result(rows)
        dng = dn * k.gains[1:2, :]
        gy = k.gy[pl.ds(pl.multiple_of(own + i * 16, 16), 16), :].astype(F32)
        dh = gy + s * (dng - hat * jnp.mean(dng * hat, axis=-1, keepdims=True))
        k.dhf[rows, :] = dh
        k.dh[pl.ds(pl.multiple_of(own + i * 16, 16), 16), :] = dh.astype(BF16)
        t = jnp.sum(dn * hat, axis=0, keepdims=True)

        @pl.when(i == 0)
        def _():
            k.ggain[...] = jnp.zeros((8, 2048), F32)
            k.ggain[1:2, :] = t

        @pl.when(i > 0)
        def _():
            k.ggain[1:2, :] += t
    loop(2, d_norm_two)
    s_dn2.drain()
    g_dh = CrossGather(r, k.dh, True, S.cg.at[2], R.cg.at[2])
    g_dh.begin()
    at(DH_0)
    g_dh.middle()
    at(DH_1)
    g_dh.end()
    at(DZ)

    def d_z(_):
        k.dv[...] = nn(k.dh[...], columns(OUT, 0, 256))
    loop(1, d_z)

    def d_gated(i):
        rows = span(i * 32, 32)
        dz = k.dv[rows, :]
        k.dq[rows, 0:256] = dz * k.v[rows, :]
        k.dv[rows, :] = dz * k.q0[rows, :]
    loop(8, d_gated)

    first = slice(0, 256)
    others = slice(256, 768)

    def dq_edge(at, send, recv):
        return remote(k.dq.at[0:8, at], k.dq.at[256:264, at], send, recv, r.along(-1))

    dq_first = dq_edge(first, S.dq_1, R.dq_1)
    dq_first.start()

    last = jnp.where(r.chip < 15, 1.0, 0.0)

    def d_short(i, taps, branches):
        near, far = masks(i)
        j = jnp.minimum(i * 16 + 16, 248)
        after = k.keep[span(j, 8), :]
        inside = i < 15
        tail_near = jnp.where(inside, after, last)
        tail_far = jnp.where(
            inside, after * jnp.concatenate([near[15:16, :], after[0:7, :]], 0), last
        )
        near = jnp.concatenate([near, tail_near], 0)
        far = jnp.concatenate([far, tail_far], 0)
        ext = k.p[pl.ds(pl.multiple_of(i * 16 + 8, 8), 24), :]
        rows = span(i * 16, 16)
        new = []
        for n, b in enumerate(branches):
            l = slice(b * 256, b * 256 + 256)
            e, db = ext[:, l], k.dq[pl.ds(pl.multiple_of(i * 16, 16), 24), l]
            dn, df = near * db, far * db
            k.dp[rows, l] = (
                k.taps[0:1, l] * db[0:16] + k.taps[1:2, l] * dn[1:17] + k.taps[2:3, l] * df[2:18]
            ).astype(BF16)
            new.append(taps[3 * n + 0] + jnp.sum(e[8:24] * db[0:16], axis=0, keepdims=True))
            new.append(taps[3 * n + 1] + jnp.sum(e[7:23] * dn[0:16], axis=0, keepdims=True))
            new.append(taps[3 * n + 2] + jnp.sum(e[6:22] * df[0:16], axis=0, keepdims=True))
        return tuple(new)

    line = jnp.zeros((1, 256), F32)
    def d_short_1(i, taps):
        return d_short(i, taps, (0,))

    def d_short_2(i, taps):
        return d_short(i, taps, (1, 2))

    d_taps = []

    def short_1():
        dq_first.wait()
        d_taps.extend(fold(16, d_short_1, (line,) * 3))

    tasks[SHORT_1] = short_1

    def retreat(a, b, keep):
        ka, kb = keep * a, keep * b
        return ka, kb, lr * ka + li * kb, lr * kb - li * ka

    def start_state(i, state):
        rows = span((31 - i) * 8, 8)
        dv, keep = k.dv[rows, :], k.keep[rows, :]
        for j in reversed(range(8)):
            a = cr * dv[j:j + 1, :] + state[0]
            b = state[1] - ci * dv[j:j + 1, :]
            _, _, pa, pb = retreat(a, b, keep[j:j + 1, :])
            state = (pa, pb)
        return state

    begin = fold(32, start_state, (zero, zero))
    arrive = chain(begin, k.backs_y, k.backs_z, -1, (BACKS_Y, BACKS_Z))
    at(ADJOINT)

    def adjoint(i, carry):
        rows = span((31 - i) * 8, 8)
        dv, keep = k.dv[rows, :], k.keep[rows, :]
        for j in reversed(range(8)):
            t = (31 - i) * 8 + j
            d = dv[j:j + 1, :]
            a = cr * d + carry[0]
            b = carry[1] - ci * d
            k.u[pl.ds(t, 1), :] = jnp.sum(a, axis=0, keepdims=True)
            _, _, pa, pb = retreat(a, b, keep[j:j + 1, :])
            carry = (pa, pb)
        return carry

    fold(32, adjoint, arrive)

    def d_poles(i, carry):
        pa, pb, dcr, dci, dlr, dli = carry
        rows = span((31 - i) * 8, 8)
        dv, keep = k.dv[rows, :], k.keep[rows, :]
        for j in reversed(range(8)):
            t = (31 - i) * 8 + j
            d = dv[j:j + 1, :]
            a = cr * d + pa
            b = pb - ci * d
            dcr = dcr + d * k.st_re[t + 1]
            dci = dci - d * k.st_im[t + 1]
            ka, kb, pa, pb = retreat(a, b, keep[j:j + 1, :])
            sr, si = k.st_re[t], k.st_im[t]
            dlr = dlr + ka * sr + kb * si
            dli = dli + kb * sr - ka * si
        return pa, pb, dcr, dci, dlr, dli

    def d_branches(i):
        rows = span(i * 32, 32)
        du = k.u[rows, :]
        k.dq[rows, 256:512] = du * k.q2[rows, :]
        k.dq[rows, 512:768] = du * k.q1[rows, :]
    loop(8, d_branches)
    dq_next = dq_edge(others, S.dq_s, R.dq_s)
    dq_next.start()
    at(DQ)
    dq_next.wait()
    d_taps.extend(fold(16, d_short_2, (line,) * 6))

    def d_n1(i):
        w = jnp.concatenate([weight(n, h, i) for n in (IN, IN_2) for h in range(2)], 1)
        k.part[:, span(i * 512, 512)] = nt(k.dp[...], w).astype(BF16)
    loop(4, d_n1)
    s_dn1 = cross(3)
    s_dn1.begin()
    at(DN1_0)

    small_1 = trade(1, k.small_y.at[y], k.small_y)
    small_2 = trade(0, k.small_z.at[z], k.small_z)

    def small_total(ref):
        return sum(ref[j].astype(F32) for j in range(4))

    small_x = remote(k.small_sum, k.small_sib, S.small_x, R.small_x, r.sib)

    def small(i):
        if i == 0:
            _, _, *dpoles = fold(32, d_poles, (*arrive, zero, zero, zero, zero))
            for j in range(4):
                k.small_y[y, 16 * j:16 * j + 16] = dpoles[j].astype(BF16)
            k.small_y[y, 64:80] = jnp.concatenate([d_taps[3 * b + t] for t in range(3) for b in range(3)] + [jnp.zeros((7, 256), F32)], 0).astype(BF16)
            small_1.begin()
        elif i == 1:
            small_1.end()
            k.small_z[z] = small_total(k.small_y).astype(BF16)
            small_2.begin()
        else:
            small_2.end()
            k.small_sum[...] = small_total(k.small_z)
            dcr, dci, dlr, dli = (k.small_sum[16 * j:16 * j + 16, :] for j in range(4))
            dgin = k.res_re[:, channels] * dcr + k.res_im[:, channels] * dci
            k.small_sum[0:16, :] = dgin * k.tab[7] - (lr * dlr + li * dli)
            k.small_sum[16:32, :] = lr * dli - li * dlr
            k.small_sum[32:48, :] = k.tab[6] * dcr
            k.small_sum[48:64, :] = k.tab[6] * dci
            small_x.start()

    tasks[SMALL] = small
    at(DN1_X)
    s_dn1.near_half()
    at(DN1_1)
    s_dn1.far_half()
    at(DN1_2)
    s_dn1.end()

    def d_norm_one(i):
        rows = pl.ds(pl.multiple_of(i * 16, 16), 16)
        here = pl.ds(pl.multiple_of(x * 32 + i * 16, 16), 16)
        a = k.tok_here[here, :].astype(F32)
        s = lax.rsqrt(jnp.mean(a * a, axis=-1, keepdims=True) + EPSILON)
        hat = a * s
        dn = s_dn1.result(rows)
        dng = dn * k.gains[0:1, :]
        k.gt[here, :] = (
            k.dhf[rows, :] + s * (dng - hat * jnp.mean(dng * hat, axis=-1, keepdims=True))
        ).astype(BF16)
        t = jnp.sum(dn * hat, axis=0, keepdims=True)

        @pl.when(i == 0)
        def _():
            k.ggain[0:1, :] = t

        @pl.when(i > 0)
        def _():
            k.ggain[0:1, :] += t
    loop(2, d_norm_one)
    g_gt = CrossGather(r, k.gt, False, S.cg.at[3], R.cg.at[3])
    g_gt.begin()

    def piece(ref, width):
        return lambda i: ref.at[:, pl.ds(pl.multiple_of(i * width, width), width)]

    gg_1 = trade(0, piece(k.ggain, 512), k.gg_z)
    gg_2 = trade(1, piece(k.gg_1, 128), k.gg_y)
    gg_3 = trade(2, k.gg_s, k.gg_x)
    gg_sib = remote(k.gg_2, k.gg_s, S.gg_s, R.gg_s, r.sib)
    gg_1.begin()
    k.gg_z[z] = k.ggain[:, span(z * 512, 512)]
    at(GT_0)
    gg_1.end()
    k.gg_1[...] = sum(k.gg_z[j] for j in range(4))
    gg_2.begin()
    k.gg_y[y] = k.gg_1[:, span(y * 128, 128)]
    at(GT_1)
    g_gt.middle()
    at(GT_2)
    gg_2.end()
    k.gg_2[...] = sum(k.gg_y[j] for j in range(4))
    gg_sib.start()
    at(GT_3)
    gg_sib.wait()
    k.gg_s[...] = k.gg_s[...] + k.gg_2[...]
    gg_3.begin()
    k.gg_x[x] = k.gg_s[...]
    g_gt.end()
    out_gt = pltpu.make_async_copy(k.gt, k.grad_tok, local.at[1])
    out_gt.start()
    at(GT_4)
    small_x.wait()
    gg_3.end()
    k.gg_out[...] = sum(k.gg_x[j] for j in range(4))

    for n in range(S_IN, 11):
        both = k.other.at[:, 0:SECOND[n - S_IN][0][1] + SECOND[n - S_IN][1][1]]
        waiting(both, S.rs_sib.at[n - S_IN]).wait_send()
        waiting(both, R.rs_sib.at[n - S_IN]).wait_recv()
        for h in range(2):
            (ref, here, at), (o, w) = finished(n, h), SECOND[n - S_IN][h]
            there = pl.ds(o + (LANES_A if h else 0), w)
            pltpu.make_async_copy(ref.at[z, y, my64, here], k.grad_w.at[0, :, there], local.at[2]).start()
            pltpu.make_async_copy(sib_bufs[h].at[:, at], k.grad_w.at[1, :, there], local.at[2]).start()
    for j, src in enumerate((k.small_sum, k.small_sib)):
        pltpu.make_async_copy(src, k.grad_small.at[j], local.at[3]).start()
    out_gain = pltpu.make_async_copy(k.gg_out, k.grad_gain, local.at[4])
    out_gain.start()
    out_bo.wait()
    out_gt.wait()
    pltpu.make_async_copy(k.grad_w, k.grad_w, local.at[2]).wait()
    pltpu.make_async_copy(k.grad_small, k.grad_small, local.at[3]).wait()
    out_gain.wait()
    for n in (A_IN, A_REST):
        waiting(k.other.at[:, 0:(768, 2432)[n]], S.w_sib.at[n]).wait_send()
    for piece in sum(gather + scatter, []):
        piece.drain()
    for copy in [gain_sib, keep_sib, gy_sib, n1_sib, edge]:
        copy.wait_send()
    for group in trades + [s_dn1, g_n2, g_bo, g_dh, g_gt]:
        group.drain()


def block(*arrays):
    sems = []
    for _, shape in fields(Sems):
        sems += [pltpu.SemaphoreType.DMA(a) for a in shape]
    vmem = pl.BlockSpec(memory_space=pltpu.VMEM)
    return pl.pallas_call(
        kernel,
        out_shape=(
            jax.ShapeDtypeStruct((128, 2048), BF16),
            jax.ShapeDtypeStruct((128, 2048), BF16),
            jax.ShapeDtypeStruct((2, 64, LANES_A + LANES_B), BF16),
            jax.ShapeDtypeStruct((2, 80, 256), F32),
            jax.ShapeDtypeStruct((8, 128), F32),
        ),
        in_specs=[vmem] * 8 + [pl.BlockSpec(memory_space=pl.ANY)] * 2 + [vmem] * 5,
        out_specs=[pl.BlockSpec(memory_space=pl.ANY)] * 5,
        scratch_shapes=[pltpu.VMEM(*value) for _, value in fields(Scratch)] + sems + [pltpu.SemaphoreType.DMA((7,))],
        compiler_params=pltpu.CompilerParams(
            collective_id=0, has_side_effects=True, vmem_limit_bytes=63 * 2**20
        ),
        name="block",
    )(*arrays)


def results(*refs):
    sources, refs = refs[:5], refs[5:]
    outs, refs = refs[:14], refs[14:]
    (bo, gt, g_gain_1, g_in, g_taps, g_decay, g_angle, g_re, g_im, g_out, g_gain_2, g_gate, g_up, g_down) = refs[:14]
    grad_w, small, gain, sems = refs[14:]
    c = lax.rem(lax.axis_index("seq"), 2)
    copies = [
        pltpu.make_async_copy(source, ref, sems.at[i])
        for i, (source, ref) in enumerate(zip(sources, (bo, gt, grad_w, small, gain)))
    ]
    leaving = [pltpu.make_async_copy(ref, out, sems.at[5 + i]) for i, (ref, out) in enumerate(zip(refs, outs))]
    for copy in copies[::-1]:
        copy.start()
    for copy in copies[2:]:
        copy.wait()

    def cols(core, n, start, stop):
        wa = WHOLE[n][0][1]
        parts = []
        if start < wa:
            parts.append(grad_w[core, :, WHOLE[n][0][0] + start:WHOLE[n][0][0] + min(stop, wa)])
        if stop > wa:
            o = LANES_A + WHOLE[n][1][0]
            parts.append(grad_w[core, :, o + max(start - wa, 0):o + stop - wa])
        return jnp.concatenate(parts, 1).astype(F32)

    cores = ((0, c), (1, 1 - c))
    for at, core in cores:
        g_in[0, :, at * 256:at * 256 + 256] = cols(core, IN, 0, 256)
        for b in (1, 2):
            g_in[b, :, at * 256:at * 256 + 256] = cols(core, IN_2, b * 256 - 256, b * 256)
    leaving[3].start()
    for at, core in cores:
        g_gate[:, at * 640:at * 640 + 640] = cols(core, GU, 0, 640)
        g_up[:, at * 640:at * 640 + 640] = cols(core, GU, 640, 1280)
    first, second = cols(c, GU, 1280, 1408), cols(1 - c, GU, 1280, 1408)
    g_gate[:, 1280:1408] = jnp.concatenate([first[:, 0:64], second[:, 0:64]], 1)
    g_up[:, 1280:1408] = jnp.concatenate([first[:, 64:128], second[:, 64:128]], 1)
    leaving[11].start()
    leaving[12].start()
    for copy in copies[:2]:
        copy.wait()
    leaving[0].start()
    leaving[1].start()
    for at, core in cores:
        g_down[:, at * 640:at * 640 + 640] = cols(core, DOWN, 0, 640)
    first, second = cols(c, DOWN, 640, 768), cols(1 - c, DOWN, 640, 768)
    g_down[:, 1280:1408] = jnp.concatenate([first[:, 0:64], second[:, 0:64]], 1)
    leaving[13].start()
    for at, core in cores:
        here = slice(at * 256, at * 256 + 256)
        g_out[:, here] = cols(core, OUT, 0, 256)
        for i, ref in enumerate((g_decay, g_angle, g_re, g_im)):
            ref[:, here] = small[core, 16 * i:16 * i + 16, :]
        for i in range(3):
            g_taps[i, :, here] = small[core, 64 + 3 * i:67 + 3 * i, :]
    for i, ref in enumerate((g_gain_1, g_gain_2)):
        a = gain[i:i + 1, :]
        ref[...] = jnp.where(c == 0, a[:, 0:64], a[:, 64:128])
    for i in (9, 4, 5, 6, 7, 8, 2, 10):
        leaving[i].start()
    for copy in leaving:
        copy.wait()


def on_device(
    tokens, cotangent, resets, norm1_gain, in_weight, conv_weight, pole_decay, pole_angle, residue_re, residue_im,
    out_weight, norm2_gain, gate_weight, up_weight, down_weight,
):
    raw = block(
        in_weight.transpose(1, 0, 2), out_weight, gate_weight, up_weight, down_weight, norm1_gain.reshape(1, 64),
        norm2_gain.reshape(1, 64), resets.reshape(1, 128), tokens, cotangent, conv_weight, pole_decay, pole_angle,
        residue_re, residue_im,
    )
    shapes = [
        ((128, 2048), BF16), ((128, 2048), BF16), ((1, 64), F32), ((3, 64, 512), F32), ((3, 3, 512), F32),
        ((16, 512), F32), ((16, 512), F32), ((16, 512), F32), ((16, 512), F32), ((64, 512), F32), ((1, 64), F32),
        ((64, 1408), F32), ((64, 1408), F32), ((64, 1408), F32),
    ]
    outs = list(pl.pallas_call(
        results,
        out_shape=[jax.ShapeDtypeStruct(s, t) for s, t in shapes],
        in_specs=[pl.BlockSpec(memory_space=pl.ANY)] * len(raw),
        out_specs=[pl.BlockSpec(memory_space=pl.ANY)] * len(shapes),
        scratch_shapes=[pltpu.VMEM(*a) for a in shapes] + [pltpu.VMEM(a.shape, a.dtype) for a in raw[2:]]
        + [pltpu.SemaphoreType.DMA((19,))],
        compiler_params=pltpu.CompilerParams(vmem_limit_bytes=60 * 2**20),
        name="results",
    )(*raw))
    outs[2], outs[10] = outs[2].reshape(64), outs[10].reshape(64)
    outs[3] = outs[3].transpose(1, 0, 2)
    return tuple(outs)


def solution(mesh):
    row, cols = P("seq", "mp"), P(None, "mp")
    return jax.shard_map(
        on_device,
        mesh=mesh,
        in_specs=(
            P("seq", None), P("seq", None), P("seq"), P("seq"), P("seq", None, "mp"), P(None, None, "mp"),
            cols, cols, cols, cols, row, P("seq"), row, row, row,
        ),
        out_specs=(
            P("seq", None), P("seq", None), P("seq"), P("seq", None, "mp"), P(None, None, "mp"),
            cols, cols, cols, cols, row, P("seq"), row, row, row,
        ),
        check_vma=False,
    )
```
